32 devices in a mesh: dom: 32 (over z, y, x, core).
Axes of the slice: x: 2, y: 2, z: 4, core: 2. Of those that a mesh axis runs over, the one named last changes fastest.
Arguments:
- ham_core: float32 [20480, 1280], P('dom')
- halo_rows: float32 [32, 8, 80, 1280], P('dom'), as said below
- halo_request: int32 [32, 160], P('dom'), may hold values from -1 to 159, as said below
- deriv: float32 [3, 5120, 4, 1280], P(None, 'dom'), may hold values from -15 to 15
- e_low: float32 [1], replicated, may hold values from -8 to -5
- e_high: float32 [1], replicated, may hold values from 4.5 to 7.5
- branches: int32 [5], replicated, may hold values from 0 to 1
Outputs:
- density: float32 [20480, 1280], P('dom')
- forces: float32 [3, 5120], P(None, 'dom')
The draws below stay inside these ranges and needn't reach their ends.
Inputs may be any that keep to these rules, and one draw needn't show every extreme that they name: Entry halo_request[d, k * 20 + s] is an atom index of the owner of block k of d, or -1 for an empty slot; in each block of 20 the live entries come first and are distinct; in every draw some partition asks 20 atoms of each of its 8 neighbours and is asked 20 atoms by each of them. For c < 640: halo_rows[p, k, r, c] equals ham_core[d * 640 + c, 640 + 4 * 20 * k + r] with d = (p - off_k) mod 32.
All inputs are finite; a program needn't handle non-finite values.
Results may differ from the reference program's by a relative error of at most 0.0003.
Values sent between devices are 32-bit elements; how exact they have to be, the bound alone decides.
No kernel may reach another device: no remote copies, remote signals or barrier semaphores. Data moves between devices by JAX's collectives and lax.ppermute only.
A program may use at most 128 MiB of HBM per device.

```python
import jax
import jax.numpy as jnp
from jax import lax

ORB = 4
ATOM_DEV = 160
NB = 4
CAP = 20
ITERS = 5
ROWS = 640
HALO_SLOTS = 160
ATOM_S = 320
M = 1280
ATOMS = 5120
NORB = 20480
N_DOM = 32


def neighbour_offsets_drawn():
    blocks = jnp.arange(2 * NB, dtype=jnp.int32)
    return jnp.where(blocks < NB, blocks + 1, NB - 1 - blocks).astype(jnp.int32)


def onsite_values(key, orbital):
    low_key, high_key = jax.random.split(key)
    s_level = jax.random.uniform(low_key, orbital.shape, jnp.float32, -2.5, -1.5)
    p_level = jax.random.uniform(high_key, orbital.shape, jnp.float32, 0.5, 1.5)
    return jnp.where(orbital % ORB == 0, s_level, p_level)


def coupling(key, block_shape):
    spread = 1.2 * M ** (-0.5)
    return jax.random.normal(key, block_shape, jnp.float32) * spread


def core_hamiltonian(key):
    base_key = jax.random.fold_in(key, 11)
    values = coupling(jax.random.fold_in(base_key, 1), (NORB, M))
    row_ids = lax.broadcasted_iota(jnp.int32, (NORB, M), 0)
    col_ids = lax.broadcasted_iota(jnp.int32, (NORB, M), 1)
    levels = onsite_values(jax.random.fold_in(base_key, 2), row_ids[:, :1])
    return jnp.where(col_ids == row_ids % ROWS, levels, values)


def draw_ham_core(key, part):
    return core_hamiltonian(key)


def draw_halo_rows(key, part):
    devices = NORB // ROWS
    blocks = 2 * NB
    slot_rows = ORB * CAP
    core_values = core_hamiltonian(key).reshape(devices, ROWS, M)
    halo_cols = core_values[:, :, ROWS:].reshape(devices, ROWS, blocks, slot_rows)
    halo_cols = jnp.transpose(halo_cols, (0, 2, 3, 1))
    sender_ids = jnp.arange(devices, dtype=jnp.int32)[:, None]
    block_ids = jnp.arange(blocks, dtype=jnp.int32)[None, :]
    holder_ids = ((sender_ids - neighbour_offsets_drawn()[None, :]) % devices).astype(jnp.int32)
    mirrored = halo_cols[holder_ids, block_ids]
    block_shape = (devices, blocks, slot_rows, M - ROWS)
    base_key = jax.random.fold_in(key, 23)
    fresh_part = coupling(jax.random.fold_in(base_key, 1), block_shape)
    block_iota = lax.broadcasted_iota(jnp.int32, block_shape, 1)
    row_ids = lax.broadcasted_iota(jnp.int32, block_shape, 2)
    col_ids = lax.broadcasted_iota(jnp.int32, block_shape, 3)
    levels = onsite_values(jax.random.fold_in(base_key, 2), row_ids[:, :, :, :1])
    fresh_part = jnp.where(col_ids == block_iota * slot_rows + row_ids, levels, fresh_part)
    return jnp.concatenate([mirrored, fresh_part], axis=3)


def draw_halo_request(key, part):
    devices = NORB // ROWS
    blocks = 2 * NB
    base_key = jax.random.fold_in(key, 37)
    hot_owner = jax.random.randint(jax.random.fold_in(base_key, 1), (), 0, devices)
    heavy_rows = jax.random.randint(jax.random.fold_in(base_key, 2), (devices, 1), 0, 4) == 0
    counts = jax.random.randint(jax.random.fold_in(base_key, 3), (devices, blocks), 0, CAP + 1)
    requester = lax.broadcasted_iota(jnp.int32, (devices, blocks), 0)
    owner_ids = (requester + neighbour_offsets_drawn()[None, :]) % devices
    full = heavy_rows | (owner_ids == hot_owner) | (requester == hot_owner)
    counts = jnp.where(full, CAP, counts)
    starts = jax.random.randint(jax.random.fold_in(base_key, 4), (devices, blocks, 1), 0, ATOM_DEV)
    slot_ids = lax.broadcasted_iota(jnp.int32, (devices, blocks, CAP), 2)
    atom_ids = (starts + slot_ids * (ATOM_DEV // CAP)) % ATOM_DEV
    chosen = jnp.where(slot_ids < counts[:, :, None], atom_ids, -1)
    return chosen.reshape(devices, blocks * CAP).astype(jnp.int32)


def set_ends(result, own_key, least, high):
    shape = result.shape
    index_at = [jax.random.randint(jax.random.fold_in(own_key, axis), (), 0, shape[axis]) for axis in range(len(shape))]
    result = result.at[tuple(index_at)].set(least)
    longest = shape.index(max(shape))
    index_at[longest] = (index_at[longest] + 1) % shape[longest]
    return result.at[tuple(index_at)].set(high)


def steps_of(stream_key, dims, cuts, least, high):
    def one(position, parts):
        steps = jax.random.uniform(jax.random.fold_in(jax.random.fold_in(stream_key, 6), position), (parts,), jnp.float32, least / len(cuts), high / len(cuts))
        return jnp.repeat(jnp.exp(steps), dims[position] // parts).reshape((-1,) + (1,) * (len(dims) - position - 1))

    loudness = one(*cuts[0])
    for cut in cuts[1:]:
        loudness = loudness * one(*cut)
    return loudness


def normal_values(own_key, shape, width, limit, cuts=(), held_as=jnp.bfloat16):
    entries = jax.random.normal(own_key, shape, jnp.float32) * width
    if len(cuts) > 0:
        entries = steps_of(own_key, shape, cuts, -0.22, 0.18) * entries
    return jnp.clip(entries, min=-limit, max=limit).astype(held_as)


def setup_inputs(seed: int = 0) -> dict:
    seeds = jax.random.split(jax.random.key(seed), 8)
    ham_core = draw_ham_core(jax.random.fold_in(seeds[7], 71), 0)
    halo_rows = draw_halo_rows(jax.random.fold_in(seeds[7], 71), 0)
    halo_request = draw_halo_request(jax.random.fold_in(seeds[7], 71), 0)
    deriv = normal_values(seeds[3], (3, ATOMS, ORB, M), 2.5, 15.0, ((1, 32),), jnp.float32)
    e_low = jnp.clip(jax.random.uniform(seeds[4], (1,), jnp.float32, -8.0, -5.0), -8.0, -5.0)
    e_high = jnp.clip(jax.random.uniform(seeds[5], (1,), jnp.float32, 4.5, 7.5), 4.5, 7.5)
    branches = set_ends(jax.random.randint(seeds[6], (ITERS,), 0, 2), jax.random.fold_in(seeds[6], 1), 0, 1).astype(jnp.int32)
    return {"ham_core": ham_core, "halo_rows": halo_rows, "halo_request": halo_request, "deriv": deriv, "e_low": e_low, "e_high": e_high, "branches": branches}


def product(left, right):
    return jnp.dot(left, right, precision=lax.Precision.HIGHEST, preferred_element_type=jnp.float32)


def neighbour_offsets():
    blocks = jnp.arange(2 * NB, dtype=jnp.int32)
    return jnp.where(blocks < NB, blocks + 1, NB - 1 - blocks).astype(jnp.int32)


def partition(part_index, ham_core, halo_rows, halo_request, deriv, e_low, e_high, branches):
    core_rows = lax.dynamic_slice_in_dim(ham_core, part_index * ROWS, ROWS, 0)
    owners = ((part_index + neighbour_offsets()) % N_DOM).astype(jnp.int32)
    halo_block = halo_rows[owners, jnp.arange(2 * NB, dtype=jnp.int32)]
    halo_block = halo_block.reshape(ORB * HALO_SLOTS, M)
    request = lax.dynamic_index_in_dim(halo_request, part_index, 0, keepdims=False)
    live_halo = jnp.repeat((request >= 0).astype(jnp.float32), ORB)
    live_mask = jnp.concatenate([jnp.ones((ROWS,), jnp.float32), live_halo])
    whole_ham = jnp.concatenate([core_rows, halo_block], axis=0) * live_mask[:, None] * live_mask[None, :]
    symmetric = 0.5 * (whole_ham + whole_ham.T)
    spread = e_high[0] - e_low[0]
    projector = (jnp.diag(e_high[0] * live_mask) - symmetric) / spread
    for number in range(ITERS):
        square = product(projector, projector)
        projector = jnp.where(branches[number] == 1, 2.0 * projector - square, square)
    core_density = projector[:ROWS]
    blocks = lax.dynamic_slice_in_dim(deriv, part_index * ATOM_DEV, ATOM_DEV, 1)
    weighted = jnp.sum(core_density.reshape(ATOM_DEV, ORB, M)[None] * blocks, axis=2)
    pair_force = 2.0 * jnp.sum(weighted.reshape(3, ATOM_DEV, ATOM_S, ORB), axis=3)
    own_force = jnp.sum(pair_force, axis=2)
    reaction = -jnp.sum(pair_force, axis=1)
    core_ids = part_index * ATOM_DEV + jnp.arange(ATOM_DEV, dtype=jnp.int32)
    slot_owner = jnp.repeat(owners, CAP).astype(jnp.int32)
    halo_ids = jnp.where(request >= 0, slot_owner * ATOM_DEV + request, ATOMS).astype(jnp.int32)
    all_ids = jnp.concatenate([core_ids, halo_ids])
    return core_density, own_force, reaction, core_ids, all_ids


def reference(ham_core, halo_rows, halo_request, deriv, e_low, e_high, branches):
    def visit(totals, part_index):
        core_density, own_force, reaction, core_ids, all_ids = partition(part_index, ham_core, halo_rows, halo_request, deriv, e_low, e_high, branches)
        totals = totals.at[:, all_ids].add(reaction, mode="drop")
        totals = totals.at[:, core_ids].add(own_force)
        return totals, core_density

    forces, stacked = lax.scan(visit, jnp.zeros((3, ATOMS), jnp.float32), jnp.arange(N_DOM, dtype=jnp.int32))
    return stacked.reshape(NORB, M), forces
```

```python
import functools

import jax
import jax.numpy as jnp
from jax import lax
from jax.experimental import pallas as pl
from jax.experimental.pallas import tpu as pltpu
from jax.sharding import PartitionSpec as P

ORB = 4
NB = 4
ITERS = 5
PANEL = 256
SUB = 128
VMEM_BYTES = 56 * 1024 * 1024


def passed_along(value, axis, steps):
    count = lax.axis_size(axis)
    pairs = [(source, (source + steps) % count) for source in range(count)]
    return lax.ppermute(value, axis, pairs)


def block_offset(block):
    if block < NB:
        return block + 1
    return NB - 1 - block


def halves(value):
    high = value.astype(jnp.bfloat16)
    low = (value - high.astype(jnp.float32)).astype(jnp.bfloat16)
    return high, low


def thirds(value):
    high = value.astype(jnp.bfloat16)
    rest = value - high.astype(jnp.float32)
    middle, low = halves(rest)
    return high, middle, low


def dot(left, right):
    return jnp.dot(left, right, preferred_element_type=jnp.float32)


def dot_one_hot(value, one_hot):
    return sum(dot(part, one_hot) for part in thirds(value))


def kernel(
    ends, branches, core, request_row, request_col, deriv, *refs
):
    block_count = 2 * NB
    pieces = refs[:block_count]
    density_out, own_out = refs[block_count : block_count + 2]
    halo_outs = refs[block_count + 2 : 2 * block_count + 2]
    (x, high_a, low_a, high_b, low_b, halo, density, deriv_held, row_part, deriv_sems, out_sem) = refs[
        2 * block_count + 2 :
    ]
    rows, order = core.shape
    atoms = rows // ORB
    slot_rows = (order - rows) // block_count

    deriv_copies = [
        pltpu.make_async_copy(deriv.at[c], deriv_held.at[c], deriv_sems.at[c]) for c in range(3)
    ]
    for copy in deriv_copies:
        copy.start()

    top = ends[0]
    scale = 1.0 / (ends[0] - ends[1])
    for block in range(block_count):
        halo[block * slot_rows : (block + 1) * slot_rows, :] = pieces[block][...]
    live_row = (request_row[...] >= 0).astype(jnp.float32)
    live_col = (request_col[...] >= 0).astype(jnp.float32)
    eye = (
        lax.broadcasted_iota(jnp.int32, (SUB, SUB), 0) == lax.broadcasted_iota(jnp.int32, (SUB, SUB), 1)
    ).astype(jnp.float32)

    def put(value, row, col):
        x[row : row + SUB, col : col + SUB] = value
        high, low = halves(value)
        high_a[row : row + SUB, col : col + SUB] = high
        low_a[row : row + SUB, col : col + SUB] = low
        if row != col:
            if row // PANEL == col // PANEL:
                x[col : col + SUB, row : row + SUB] = value.T
            high_a[col : col + SUB, row : row + SUB] = high.T
            low_a[col : col + SUB, row : row + SUB] = low.T

    for row in range(0, rows, SUB):
        for col in range(row, rows, SUB):
            value = 0.5 * (
                core[row : row + SUB, col : col + SUB] + core[col : col + SUB, row : row + SUB].T
            )
            if row == col:
                value = value - top * eye
            put(-scale * value, row, col)
    for row in range(0, rows, SUB):
        for col in range(rows, order, SUB):
            value = core[row : row + SUB, col : col + SUB] * live_row[:, col - rows : col - rows + SUB]
            put(-scale * value, row, col)
    for row in range(0, order - rows, SUB):
        for col in range(row, order - rows, SUB):
            value = 0.5 * (
                halo[row : row + SUB, col : col + SUB] + halo[col : col + SUB, row : row + SUB].T
            )
            if row == col:
                value = value - top * eye
            value = value * live_col[row : row + SUB, :] * live_row[:, col : col + SUB]
            put(-scale * value, row + rows, col + rows)

    def product(high, low, upto, cols):
        right_high, right_low = high[:, cols], low[:, cols]
        left_high, left_low = high[0:upto, :], low[0:upto, :]
        return dot(left_high, right_high) + (dot(left_high, right_low) + dot(left_low, right_high))

    def factors(number):
        taken = (branches[number] == 1).astype(jnp.float32)
        return 2.0 * taken, 1.0 - 2.0 * taken

    def squaring(number, high, low, next_high, next_low):
        keep, add = factors(number)
        for start in range(0, order, PANEL):
            end = start + PANEL
            cols = slice(start, end)
            value = keep * x[0:end, cols] + add * product(high, low, end, cols)
            x[0:end, cols] = value
            new_high, new_low = halves(value)
            next_high[0:end, cols] = new_high
            next_low[0:end, cols] = new_low
            if start > 0:
                next_high[cols, 0:start] = new_high[0:start].T
                next_low[cols, 0:start] = new_low[0:start].T

    def two(pair, carry):
        squaring(2 * pair, high_a, low_a, high_b, low_b)
        squaring(2 * pair + 1, high_b, low_b, high_a, low_a)
        return carry

    lax.fori_loop(0, (ITERS - 1) // 2, two, 0)
    keep, add = factors(ITERS - 1)
    for start in range(0, order, PANEL):
        upto = min(start + PANEL, rows)
        cols = slice(start, start + PANEL)
        value = keep * x[0:upto, cols] + add * product(high_a, low_a, upto, cols)
        density[0:upto, cols] = value
        if 0 < start < rows:
            end = min(start + PANEL, rows)
            density[start:end, 0:start] = value[0:start, 0 : end - start].T

    out_copy = pltpu.make_async_copy(density, density_out, out_sem)
    out_copy.start()

    chunk = 64
    line = lax.broadcasted_iota(jnp.int32, (8, order), 0)
    columns = jnp.zeros((8, order), jnp.float32)
    own_rows = jnp.zeros((8, rows), jnp.float32)
    ones = jnp.ones((8, SUB), jnp.bfloat16)
    for c in range(3):
        deriv_copies[c].wait()

        def strip(number, total, c=c):
            at = pl.ds(pl.multiple_of(number * chunk, chunk), chunk)
            weighted = density[at, :] * deriv_held[c, at, :]
            row_part[at, :] = sum(weighted[:, lane : lane + SUB] for lane in range(0, order, SUB))
            return total + jnp.sum(weighted.reshape(chunk // 8, 8, order), axis=0)

        total = lax.fori_loop(0, rows // chunk, strip, jnp.zeros((8, order), jnp.float32))
        columns = jnp.where(line == c, jnp.sum(total, axis=0, keepdims=True), columns)
        row_sums = sum(
            lax.dot_general(ones, part, (((1,), (1,)), ((), ())), preferred_element_type=jnp.float32)
            for part in thirds(row_part[...])
        )
        own_rows = jnp.where(line[:, :rows] == c, row_sums, own_rows)
    atom_ids = lax.broadcasted_iota(jnp.int32, (rows, atoms), 1)
    own_hot = (lax.broadcasted_iota(jnp.int32, (rows, atoms), 0) // ORB == atom_ids).astype(jnp.float32)
    own_out[...] = dot_one_hot(2.0 * (own_rows - columns[:, :rows]), own_hot.astype(jnp.bfloat16))
    asked_hot = (request_col[...] == atom_ids).astype(jnp.float32).astype(jnp.bfloat16)
    lane_block = lax.broadcasted_iota(jnp.int32, (8, order - rows), 1) // slot_rows
    halo_columns = -2.0 * columns[:, rows:]
    spread = jnp.concatenate(
        [jnp.where(lane_block == block, halo_columns, 0.0) for block in range(block_count)], axis=0
    )
    terms = dot_one_hot(spread, asked_hot)
    for block in range(block_count):
        halo_outs[block][...] = terms[8 * block : 8 * block + 8, :]
    out_copy.wait()


def density_and_terms(ends, branches, core, request_row, request_col, deriv, pieces):
    rows, order = core.shape
    atoms = rows // ORB
    block_count = len(pieces)
    vmem = pl.BlockSpec(memory_space=pltpu.VMEM)
    smem = pl.BlockSpec(memory_space=pltpu.SMEM)
    anywhere = pl.BlockSpec(memory_space=pl.ANY)
    square = (order, order)
    small = jax.ShapeDtypeStruct((8, atoms), jnp.float32)
    return pl.pallas_call(
        kernel,
        out_shape=[jax.ShapeDtypeStruct((rows, order), jnp.float32)] + [small] * (block_count + 1),
        in_specs=[smem, smem, vmem, vmem, vmem, anywhere] + [vmem] * block_count,
        out_specs=[anywhere] + [vmem] * (block_count + 1),
        scratch_shapes=[
            pltpu.VMEM(square, jnp.float32),
            pltpu.VMEM(square, jnp.bfloat16),
            pltpu.VMEM(square, jnp.bfloat16),
            pltpu.VMEM(square, jnp.bfloat16),
            pltpu.VMEM(square, jnp.bfloat16),
            pltpu.VMEM((order - rows, order - rows), jnp.float32),
            pltpu.VMEM((rows, order), jnp.float32),
            pltpu.VMEM((3, rows, order), jnp.float32),
            pltpu.VMEM((rows, SUB), jnp.float32),
            pltpu.SemaphoreType.DMA((3,)),
            pltpu.SemaphoreType.DMA,
        ],
        compiler_params=pltpu.CompilerParams(vmem_limit_bytes=VMEM_BYTES),
        cost_estimate=pl.CostEstimate(
            flops=2 * 3 * 3 * order**3, bytes_accessed=24_000_000, transcendentals=0
        ),
    )(ends, branches, core, request_row, request_col, deriv, *pieces)


def per_device(ham_core, halo_rows, halo_request, deriv, e_low, e_high, branches):
    row_count, order_all = ham_core.shape
    block_count = 2 * NB
    pieces = [
        passed_along(halo_rows[0, block, :, row_count:], "dom", -block_offset(block))
        for block in range(block_count)
    ]
    request = jnp.repeat(halo_request[0], ORB)
    outs = density_and_terms(
        jnp.concatenate([e_high, e_low]),
        branches,
        ham_core,
        request[None, :],
        request[:, None],
        deriv.reshape(3, row_count, order_all),
        pieces,
    )
    density, forces = outs[:2]
    for block in range(block_count):
        forces = forces + passed_along(outs[2 + block], "dom", block_offset(block))
    return (density, forces[:3])


def solution(mesh):
    in_specs = (
        P("dom", None),
        P("dom", None, None, None),
        P("dom", None),
        P(None, "dom", None, None),
        P(),
        P(),
        P(),
    )
    out_specs = (P("dom", None), P(None, "dom"))
    return jax.shard_map(
        per_device, mesh=mesh, in_specs=in_specs, out_specs=out_specs, check_vma=False
    )
```

```python
import functools

import jax
import jax.numpy as jnp
from jax import lax
from jax.experimental import pallas as pl
from jax.experimental.pallas import tpu as pltpu
from jax.sharding import PartitionSpec as P

ORB = 4
NB = 4
ITERS = 5
PANEL = 256
SUB = 128
VMEM_BYTES = 56 * 1024 * 1024


def passed_along(value, axis, steps):
    count = lax.axis_size(axis)
    pairs = [(source, (source + steps) % count) for source in range(count)]
    return lax.ppermute(value, axis, pairs)


def block_offset(block):
    if block < NB:
        return block + 1
    return NB - 1 - block


def halves(value):
    high = value.astype(jnp.bfloat16)
    low = (value - high.astype(jnp.float32)).astype(jnp.bfloat16)
    return high, low


def thirds(value):
    high = value.astype(jnp.bfloat16)
    rest = value - high.astype(jnp.float32)
    middle, low = halves(rest)
    return high, middle, low


def dot(left, right):
    return jnp.dot(left, right, preferred_element_type=jnp.float32)


def dot_one_hot(value, one_hot):
    return sum(dot(part, one_hot) for part in thirds(value))


def kernel(
    ends, branches, core, request_row, request_col, deriv, *refs
):
    block_count = 2 * NB
    pieces = refs[:block_count]
    density_out, own_out, near_up, near_down, far_up, far_down = refs[block_count : block_count + 6]
    (x, high_a, low_a, high_b, low_b, diag_row_a, diag_row_b, diag_col_a, diag_col_b, halo, density, deriv_held, row_part, deriv_sems, out_sem) = refs[
        block_count + 6 :
    ]
    rows, order = core.shape
    atoms = rows // ORB
    slot_rows = (order - rows) // block_count

    deriv_copies = [
        pltpu.make_async_copy(deriv.at[c], deriv_held.at[c], deriv_sems.at[c]) for c in range(3)
    ]
    for copy in deriv_copies:
        copy.start()

    top = ends[0]
    scale = 1.0 / (ends[0] - ends[1])
    for block in range(block_count):
        halo[block * slot_rows : (block + 1) * slot_rows, :] = pieces[block][...]
    live_row = (request_row[...] >= 0).astype(jnp.float32)
    live_col = (request_col[...] >= 0).astype(jnp.float32)
    eye = lax.broadcasted_iota(jnp.int32, (SUB, SUB), 0) == lax.broadcasted_iota(jnp.int32, (SUB, SUB), 1)

    def put(value, row, col):
        x[row : row + SUB, col : col + SUB] = value
        if row == col:
            line = jnp.where(eye, value, 0.0)
            diag_row_a[:, col : col + SUB] = jnp.broadcast_to(
                jnp.sum(line, axis=0, keepdims=True), (8, SUB)
            )
            diag_col_a[row : row + SUB, :] = jnp.broadcast_to(
                jnp.sum(line, axis=1, keepdims=True), (SUB, SUB)
            )
            value = value - line
        high, low = halves(value)
        high_a[row : row + SUB, col : col + SUB] = high
        low_a[row : row + SUB, col : col + SUB] = low
        if row != col:
            if row // PANEL == col // PANEL:
                x[col : col + SUB, row : row + SUB] = value.T
            high_a[col : col + SUB, row : row + SUB] = high.T
            low_a[col : col + SUB, row : row + SUB] = low.T

    for row in range(0, rows, SUB):
        for col in range(row, rows, SUB):
            value = 0.5 * (
                core[row : row + SUB, col : col + SUB] + core[col : col + SUB, row : row + SUB].T
            )
            if row == col:
                value = value - jnp.where(eye, top, 0.0)
            put(-scale * value, row, col)
    for row in range(0, rows, SUB):
        for col in range(rows, order, SUB):
            value = core[row : row + SUB, col : col + SUB] * live_row[:, col - rows : col - rows + SUB]
            put(-scale * value, row, col)
    for row in range(0, order - rows, SUB):
        for col in range(row, order - rows, SUB):
            value = 0.5 * (
                halo[row : row + SUB, col : col + SUB] + halo[col : col + SUB, row : row + SUB].T
            )
            if row == col:
                value = value - jnp.where(eye, top, 0.0)
            value = value * live_col[row : row + SUB, :] * live_row[:, col : col + SUB]
            put(-scale * value, row + rows, col + rows)

    def stepped(number, now, rows_at, cols_at):
        high, low, diag_row, diag_col = now
        taken = (branches[number] == 1).astype(jnp.float32)
        keep, add = 2.0 * taken, 1.0 - 2.0 * taken
        left_high, left_low = high[rows_at, :], low[rows_at, :]
        right_high, right_low = high[:, cols_at], low[:, cols_at]
        if rows_at == cols_at:
            cross = dot(left_high, right_low)
            off = dot(left_high, right_high) + (cross + cross.T)
        else:
            off = dot(
                jnp.concatenate([left_high, left_high, left_low], axis=1),
                jnp.concatenate([right_high, right_low, right_high], axis=0),
            )
        old = x[rows_at, cols_at]
        factor_col = keep + add * diag_col[rows_at, :]
        factor = jnp.concatenate([factor_col, factor_col], axis=1) + add * diag_row[0:1, cols_at]
        value = old * factor + add * off
        if rows_at.start == cols_at.start:
            on = lax.broadcasted_iota(jnp.int32, value.shape, 0) == lax.broadcasted_iota(
                jnp.int32, value.shape, 1
            )
            value = value - jnp.where(on, add * (old * old), 0.0)
        return value

    def squaring(number, now, later):
        next_high, next_low, next_row, next_col = later
        for start in range(0, order, PANEL):
            cols = slice(start, start + PANEL)
            for at in range(0, start + PANEL, PANEL):
                lines = slice(at, at + PANEL)
                value = stepped(number, now, lines, cols)
                x[lines, cols] = value
                if at == start:
                    on = lax.broadcasted_iota(jnp.int32, value.shape, 0) == lax.broadcasted_iota(
                        jnp.int32, value.shape, 1
                    )
                    line = jnp.where(on, value, 0.0)
                    next_row[:, cols] = jnp.broadcast_to(
                        jnp.sum(line, axis=0, keepdims=True), (8, PANEL)
                    )
                    next_col[cols, :] = jnp.broadcast_to(
                        jnp.sum(line, axis=1, keepdims=True), (PANEL, SUB)
                    )
                    value = value - line
                new_high, new_low = halves(value)
                next_high[lines, cols] = new_high
                next_low[lines, cols] = new_low
                if at < start:
                    next_high[cols, lines] = new_high.T
                    next_low[cols, lines] = new_low.T

    state_a = (high_a, low_a, diag_row_a, diag_col_a)
    state_b = (high_b, low_b, diag_row_b, diag_col_b)

    def two(pair, carry):
        squaring(2 * pair, state_a, state_b)
        squaring(2 * pair + 1, state_b, state_a)
        return carry

    lax.fori_loop(0, (ITERS - 1) // 2, two, 0)
    for start in range(0, order, PANEL):
        cols = slice(start, start + PANEL)
        for at in range(0, min(start + PANEL, rows), PANEL):
            lines = slice(at, min(at + PANEL, rows))
            value = stepped(ITERS - 1, state_a, lines, cols)
            density[lines, cols] = value
            if at < start < rows:
                end = min(start + PANEL, rows)
                density[start:end, lines] = value[:, 0 : end - start].T

    out_copy = pltpu.make_async_copy(density, density_out, out_sem)
    out_copy.start()

    chunk = 64
    line = lax.broadcasted_iota(jnp.int32, (8, order), 0)
    columns = jnp.zeros((8, order), jnp.float32)
    own_rows = jnp.zeros((8, rows), jnp.float32)
    ones = jnp.ones((8, SUB), jnp.bfloat16)
    for c in range(3):
        deriv_copies[c].wait()

        def strip(number, total, c=c):
            at = pl.ds(pl.multiple_of(number * chunk, chunk), chunk)
            weighted = density[at, :] * deriv_held[c, at, :]
            row_part[at, :] = sum(weighted[:, lane : lane + SUB] for lane in range(0, order, SUB))
            return total + jnp.sum(weighted.reshape(chunk // 8, 8, order), axis=0)

        total = lax.fori_loop(0, rows // chunk, strip, jnp.zeros((8, order), jnp.float32))
        columns = jnp.where(line == c, jnp.sum(total, axis=0, keepdims=True), columns)
        row_sums = sum(
            lax.dot_general(ones, part, (((1,), (1,)), ((), ())), preferred_element_type=jnp.float32)
            for part in thirds(row_part[...])
        )
        own_rows = jnp.where(line[:, :rows] == c, row_sums, own_rows)
    atom_ids = lax.broadcasted_iota(jnp.int32, (rows, atoms), 1)
    own_hot = (lax.broadcasted_iota(jnp.int32, (rows, atoms), 0) // ORB == atom_ids).astype(jnp.float32)
    own_out[...] = dot_one_hot(2.0 * (own_rows - columns[:, :rows]), own_hot.astype(jnp.bfloat16))
    asked_hot = (request_col[...] == atom_ids).astype(jnp.float32).astype(jnp.bfloat16)
    lane_block = lax.broadcasted_iota(jnp.int32, (8, order - rows), 1) // slot_rows
    halo_columns = -2.0 * columns[:, rows:]
    spread = jnp.concatenate(
        [jnp.where(lane_block == block, halo_columns, 0.0) for block in range(block_count)], axis=0
    )
    terms = dot_one_hot(spread, asked_hot)
    places = {
        block_offset(block): terms[8 * block : 8 * block + 8, :] for block in range(block_count)
    }
    near_up[...] = jnp.concatenate([places[1], places[4], places[-2]], axis=0)
    near_down[...] = jnp.concatenate([places[-1], places[-4], places[2]], axis=0)
    far_up[...] = places[3]
    far_down[...] = places[-3]
    out_copy.wait()


def density_and_terms(ends, branches, core, request_row, request_col, deriv, pieces):
    rows, order = core.shape
    atoms = rows // ORB
    block_count = len(pieces)
    vmem = pl.BlockSpec(memory_space=pltpu.VMEM)
    smem = pl.BlockSpec(memory_space=pltpu.SMEM)
    anywhere = pl.BlockSpec(memory_space=pl.ANY)
    square = (order, order)
    one = jax.ShapeDtypeStruct((8, atoms), jnp.float32)
    three = jax.ShapeDtypeStruct((24, atoms), jnp.float32)
    return pl.pallas_call(
        kernel,
        out_shape=[jax.ShapeDtypeStruct((rows, order), jnp.float32), one, three, three, one, one],
        in_specs=[smem, smem, vmem, vmem, vmem, anywhere] + [vmem] * block_count,
        out_specs=[anywhere] + [vmem] * 5,
        scratch_shapes=[
            pltpu.VMEM(square, jnp.float32),
            pltpu.VMEM(square, jnp.bfloat16),
            pltpu.VMEM(square, jnp.bfloat16),
            pltpu.VMEM(square, jnp.bfloat16),
            pltpu.VMEM(square, jnp.bfloat16),
            pltpu.VMEM((8, order), jnp.float32),
            pltpu.VMEM((8, order), jnp.float32),
            pltpu.VMEM((order, SUB), jnp.float32),
            pltpu.VMEM((order, SUB), jnp.float32),
            pltpu.VMEM((order - rows, order - rows), jnp.float32),
            pltpu.VMEM((rows, order), jnp.float32),
            pltpu.VMEM((3, rows, order), jnp.float32),
            pltpu.VMEM((rows, SUB), jnp.float32),
            pltpu.SemaphoreType.DMA((3,)),
            pltpu.SemaphoreType.DMA,
        ],
        compiler_params=pltpu.CompilerParams(vmem_limit_bytes=VMEM_BYTES),
        cost_estimate=pl.CostEstimate(
            flops=2 * 3 * 3 * order**3, bytes_accessed=24_000_000, transcendentals=0
        ),
    )(ends, branches, core, request_row, request_col, deriv, *pieces)


def per_device(ham_core, halo_rows, halo_request, deriv, e_low, e_high, branches):
    row_count, order_all = ham_core.shape
    block_count = 2 * NB
    halo = halo_rows[0, :, :, row_count:]
    flat_deriv = deriv.reshape(3, row_count, order_all)
    early = (1, 2, 3, 5, 6)
    late = (0, 4, 7)
    pieces = {block: passed_along(halo[block], "dom", -block_offset(block)) for block in early}
    waiting, flat_deriv = lax.optimization_barrier(([halo[block] for block in late], flat_deriv))
    for block, piece in zip(late, waiting):
        pieces[block] = passed_along(piece, "dom", -block_offset(block))
    request = jnp.repeat(halo_request[0], ORB)
    density, forces, near_up, near_down, far_up, far_down = density_and_terms(
        jnp.concatenate([e_high, e_low]),
        branches,
        ham_core,
        request[None, :],
        request[:, None],
        flat_deriv,
        [pieces[block] for block in range(block_count)],
    )
    from_below = passed_along(near_up, "dom", 1)
    from_above = passed_along(near_down, "dom", -1)
    far_up = far_up + (from_below[8:16] + from_above[16:24])
    far_down = far_down + (from_above[8:16] + from_below[16:24])
    forces = forces + (from_below[:8] + from_above[:8])
    forces = forces + (passed_along(far_up, "dom", 3) + passed_along(far_down, "dom", -3))
    return (density, forces[:3])


def solution(mesh):
    in_specs = (
        P("dom", None),
        P("dom", None, None, None),
        P("dom", None),
        P(None, "dom", None, None),
        P(),
        P(),
        P(),
    )
    out_specs = (P("dom", None), P(None, "dom"))
    return jax.shard_map(
        per_device, mesh=mesh, in_specs=in_specs, out_specs=out_specs, check_vma=False
    )
```

```python
import functools

import jax
import jax.numpy as jnp
from jax import lax
from jax.experimental import pallas as pl
from jax.experimental.pallas import tpu as pltpu
from jax.sharding import PartitionSpec as P

ORB = 4
NB = 4
ITERS = 5
PANEL = 256
SUB = 128
VMEM_BYTES = 56 * 1024 * 1024


def passed_along(value, axis, steps):
    count = lax.axis_size(axis)
    pairs = [(source, (source + steps) % count) for source in range(count)]
    return lax.ppermute(value, axis, pairs)


def block_offset(block):
    if block < NB:
        return block + 1
    return NB - 1 - block


def halves(value):
    high = value.astype(jnp.bfloat16)
    low = (value - high.astype(jnp.float32)).astype(jnp.bfloat16)
    return high, low


def thirds(value):
    high = value.astype(jnp.bfloat16)
    rest = value - high.astype(jnp.float32)
    middle, low = halves(rest)
    return high, middle, low


def dot(left, right):
    return jnp.dot(left, right, preferred_element_type=jnp.float32)


def dot_one_hot(value, one_hot):
    return sum(dot(part, one_hot) for part in thirds(value))


def kernel(
    place, ends, branches, core, request_row, request_col, deriv, *refs
):
    block_count = 2 * NB
    pieces = refs[:block_count]
    density_out, own_out, mail = refs[block_count : block_count + 3]
    (x, high_a, low_a, high_b, low_b, diag_row_a, diag_row_b, diag_col_a, diag_col_b, halo, density, deriv_held, row_part, deriv_sems, out_sem) = refs[
        block_count + 3 :
    ]
    rows, order = core.shape
    atoms = rows // ORB
    slot_rows = (order - rows) // block_count

    deriv_copies = [
        pltpu.make_async_copy(deriv.at[c], deriv_held.at[c], deriv_sems.at[c]) for c in range(3)
    ]
    for copy in deriv_copies:
        copy.start()

    top = ends[0]
    scale = 1.0 / (ends[0] - ends[1])
    for block in range(block_count):
        halo[block * slot_rows : (block + 1) * slot_rows, :] = pieces[block][...]
    live_row = (request_row[...] >= 0).astype(jnp.float32)
    live_col = (request_col[...] >= 0).astype(jnp.float32)
    eye = lax.broadcasted_iota(jnp.int32, (SUB, SUB), 0) == lax.broadcasted_iota(jnp.int32, (SUB, SUB), 1)

    def put(value, row, col):
        x[row : row + SUB, col : col + SUB] = value
        if row == col:
            line = jnp.where(eye, value, 0.0)
            diag_row_a[:, col : col + SUB] = jnp.broadcast_to(
                jnp.sum(line, axis=0, keepdims=True), (8, SUB)
            )
            diag_col_a[row : row + SUB, :] = jnp.broadcast_to(
                jnp.sum(line, axis=1, keepdims=True), (SUB, SUB)
            )
            value = value - line
        high, low = halves(value)
        high_a[row : row + SUB, col : col + SUB] = high
        low_a[row : row + SUB, col : col + SUB] = low
        if row != col:
            if row // PANEL == col // PANEL:
                x[col : col + SUB, row : row + SUB] = value.T
            high_a[col : col + SUB, row : row + SUB] = high.T
            low_a[col : col + SUB, row : row + SUB] = low.T

    for row in range(0, rows, SUB):
        for col in range(row, rows, SUB):
            value = 0.5 * (
                core[row : row + SUB, col : col + SUB] + core[col : col + SUB, row : row + SUB].T
            )
            if row == col:
                value = value - jnp.where(eye, top, 0.0)
            put(-scale * value, row, col)
    for row in range(0, rows, SUB):
        for col in range(rows, order, SUB):
            value = core[row : row + SUB, col : col + SUB] * live_row[:, col - rows : col - rows + SUB]
            put(-scale * value, row, col)
    for row in range(0, order - rows, SUB):
        for col in range(row, order - rows, SUB):
            value = 0.5 * (
                halo[row : row + SUB, col : col + SUB] + halo[col : col + SUB, row : row + SUB].T
            )
            if row == col:
                value = value - jnp.where(eye, top, 0.0)
            value = value * live_col[row : row + SUB, :] * live_row[:, col : col + SUB]
            put(-scale * value, row + rows, col + rows)

    def stepped(number, now, rows_at, cols_at):
        high, low, diag_row, diag_col = now
        taken = (branches[number] == 1).astype(jnp.float32)
        keep, add = 2.0 * taken, 1.0 - 2.0 * taken
        left_high, left_low = high[rows_at, :], low[rows_at, :]
        right_high, right_low = high[:, cols_at], low[:, cols_at]
        if rows_at == cols_at:
            cross = dot(left_high, right_low)
            off = dot(left_high, right_high) + (cross + cross.T)
        else:
            off = dot(
                jnp.concatenate([left_high, left_high, left_low], axis=1),
                jnp.concatenate([right_high, right_low, right_high], axis=0),
            )
        old = x[rows_at, cols_at]
        factor_col = keep + add * diag_col[rows_at, :]
        factor = jnp.concatenate([factor_col, factor_col], axis=1) + add * diag_row[0:1, cols_at]
        value = old * factor + add * off
        if rows_at.start == cols_at.start:
            on = lax.broadcasted_iota(jnp.int32, value.shape, 0) == lax.broadcasted_iota(
                jnp.int32, value.shape, 1
            )
            value = value - jnp.where(on, add * (old * old), 0.0)
        return value

    def squaring(number, now, later):
        next_high, next_low, next_row, next_col = later
        for start in range(0, order, PANEL):
            cols = slice(start, start + PANEL)
            for at in range(0, start + PANEL, PANEL):
                lines = slice(at, at + PANEL)
                value = stepped(number, now, lines, cols)
                x[lines, cols] = value
                if at == start:
                    on = lax.broadcasted_iota(jnp.int32, value.shape, 0) == lax.broadcasted_iota(
                        jnp.int32, value.shape, 1
                    )
                    line = jnp.where(on, value, 0.0)
                    next_row[:, cols] = jnp.broadcast_to(
                        jnp.sum(line, axis=0, keepdims=True), (8, PANEL)
                    )
                    next_col[cols, :] = jnp.broadcast_to(
                        jnp.sum(line, axis=1, keepdims=True), (PANEL, SUB)
                    )
                    value = value - line
                new_high, new_low = halves(value)
                next_high[lines, cols] = new_high
                next_low[lines, cols] = new_low
                if at < start:
                    next_high[cols, lines] = new_high.T
                    next_low[cols, lines] = new_low.T

    state_a = (high_a, low_a, diag_row_a, diag_col_a)
    state_b = (high_b, low_b, diag_row_b, diag_col_b)

    def two(pair, carry):
        squaring(2 * pair, state_a, state_b)
        squaring(2 * pair + 1, state_b, state_a)
        return carry

    lax.fori_loop(0, (ITERS - 1) // 2, two, 0)
    for start in range(0, order, PANEL):
        cols = slice(start, start + PANEL)
        for at in range(0, min(start + PANEL, rows), PANEL):
            lines = slice(at, min(at + PANEL, rows))
            value = stepped(ITERS - 1, state_a, lines, cols)
            density[lines, cols] = value
            if at < start < rows:
                end = min(start + PANEL, rows)
                density[start:end, lines] = value[:, 0 : end - start].T

    out_copy = pltpu.make_async_copy(density, density_out, out_sem)
    out_copy.start()

    chunk = 64
    line = lax.broadcasted_iota(jnp.int32, (8, order), 0)
    columns = jnp.zeros((8, order), jnp.float32)
    own_rows = jnp.zeros((8, rows), jnp.float32)
    ones = jnp.ones((8, SUB), jnp.bfloat16)
    for c in range(3):
        deriv_copies[c].wait()

        def strip(number, total, c=c):
            at = pl.ds(pl.multiple_of(number * chunk, chunk), chunk)
            weighted = density[at, :] * deriv_held[c, at, :]
            row_part[at, :] = sum(weighted[:, lane : lane + SUB] for lane in range(0, order, SUB))
            return total + jnp.sum(weighted.reshape(chunk // 8, 8, order), axis=0)

        total = lax.fori_loop(0, rows // chunk, strip, jnp.zeros((8, order), jnp.float32))
        columns = jnp.where(line == c, jnp.sum(total, axis=0, keepdims=True), columns)
        row_sums = sum(
            lax.dot_general(ones, part, (((1,), (1,)), ((), ())), preferred_element_type=jnp.float32)
            for part in thirds(row_part[...])
        )
        own_rows = jnp.where(line[:, :rows] == c, row_sums, own_rows)
    atom_ids = lax.broadcasted_iota(jnp.int32, (rows, atoms), 1)
    own_hot = (lax.broadcasted_iota(jnp.int32, (rows, atoms), 0) // ORB == atom_ids).astype(jnp.float32)
    own_out[...] = dot_one_hot(2.0 * (own_rows - columns[:, :rows]), own_hot.astype(jnp.bfloat16))
    asked = request_row[...].astype(jnp.float32)
    letter = jnp.where(line[:, rows:] == 3, asked, -2.0 * columns[:, rows:])
    empty = jnp.where(lax.broadcasted_iota(jnp.int32, (4, SUB - slot_rows), 0) == 3, -1.0, 0.0)
    mail[...] = jnp.zeros(mail.shape, jnp.float32)
    for block in range(block_count):
        content = letter[0:4, block * slot_rows : (block + 1) * slot_rows]
        to = lax.rem(place[0] + (block_offset(block) + mail.shape[0]), mail.shape[0])
        mail[to] = jnp.concatenate([content, empty], axis=1)
    out_copy.wait()


def collect(place, mail, own, forces):
    count = mail.shape[0]
    atoms = own.shape[1]
    letters = jnp.concatenate(
        [mail[lax.rem(place[0] + (count - block_offset(block)), count)] for block in range(2 * NB)],
        axis=1,
    )
    wanted = letters[3:4, :] == lax.broadcasted_iota(jnp.int32, (atoms, 1), 0).astype(jnp.float32)
    wanted = wanted.astype(jnp.float32).astype(jnp.bfloat16)
    sums = sum(
        lax.dot_general(part, wanted, (((1,), (1,)), ((), ())), preferred_element_type=jnp.float32)
        for part in thirds(jnp.concatenate([letters, letters], axis=0))
    )
    forces[...] = own[0:3, :] + sums[0:3, :]


def density_and_terms(place, ends, branches, core, request_row, request_col, deriv, pieces):
    rows, order = core.shape
    atoms = rows // ORB
    block_count = len(pieces)
    vmem = pl.BlockSpec(memory_space=pltpu.VMEM)
    smem = pl.BlockSpec(memory_space=pltpu.SMEM)
    anywhere = pl.BlockSpec(memory_space=pl.ANY)
    square = (order, order)
    return pl.pallas_call(
        kernel,
        out_shape=[
            jax.ShapeDtypeStruct((rows, order), jnp.float32),
            jax.ShapeDtypeStruct((8, atoms), jnp.float32),
            jax.ShapeDtypeStruct((lax.axis_size("dom"), 4, SUB), jnp.float32),
        ],
        in_specs=[smem, smem, smem, vmem, vmem, vmem, anywhere] + [vmem] * block_count,
        out_specs=[anywhere, vmem, vmem],
        scratch_shapes=[
            pltpu.VMEM(square, jnp.float32),
            pltpu.VMEM(square, jnp.bfloat16),
            pltpu.VMEM(square, jnp.bfloat16),
            pltpu.VMEM(square, jnp.bfloat16),
            pltpu.VMEM(square, jnp.bfloat16),
            pltpu.VMEM((8, order), jnp.float32),
            pltpu.VMEM((8, order), jnp.float32),
            pltpu.VMEM((order, SUB), jnp.float32),
            pltpu.VMEM((order, SUB), jnp.float32),
            pltpu.VMEM((order - rows, order - rows), jnp.float32),
            pltpu.VMEM((rows, order), jnp.float32),
            pltpu.VMEM((3, rows, order), jnp.float32),
            pltpu.VMEM((rows, SUB), jnp.float32),
            pltpu.SemaphoreType.DMA((3,)),
            pltpu.SemaphoreType.DMA,
        ],
        compiler_params=pltpu.CompilerParams(vmem_limit_bytes=VMEM_BYTES),
        cost_estimate=pl.CostEstimate(
            flops=2 * 3 * 3 * order**3, bytes_accessed=24_000_000, transcendentals=0
        ),
    )(place, ends, branches, core, request_row, request_col, deriv, *pieces)


def per_device(ham_core, halo_rows, halo_request, deriv, e_low, e_high, branches):
    row_count, order_all = ham_core.shape
    block_count = 2 * NB
    halo = halo_rows[0, :, :, row_count:]
    flat_deriv = deriv.reshape(3, row_count, order_all)
    early = (1, 2, 3, 5, 6)
    late = (0, 4, 7)
    pieces = {block: passed_along(halo[block], "dom", -block_offset(block)) for block in early}
    waiting, flat_deriv = lax.optimization_barrier(([halo[block] for block in late], flat_deriv))
    for block, piece in zip(late, waiting):
        pieces[block] = passed_along(piece, "dom", -block_offset(block))
    request = jnp.repeat(halo_request[0], ORB)
    place = lax.axis_index("dom")[None].astype(jnp.int32)
    density, own, mail = density_and_terms(
        place,
        jnp.concatenate([e_high, e_low]),
        branches,
        ham_core,
        request[None, :],
        request[:, None],
        flat_deriv,
        [pieces[block] for block in range(block_count)],
    )
    arrived = lax.all_to_all(mail, "dom", 0, 0, tiled=True)
    forces = pl.pallas_call(
        collect,
        out_shape=jax.ShapeDtypeStruct((3, own.shape[1]), jnp.float32),
        in_specs=[
            pl.BlockSpec(memory_space=pltpu.SMEM),
            pl.BlockSpec(memory_space=pltpu.VMEM),
            pl.BlockSpec(memory_space=pltpu.VMEM),
        ],
        out_specs=pl.BlockSpec(memory_space=pltpu.VMEM),
    )(place, arrived, own)
    return (density, forces)


def solution(mesh):
    in_specs = (
        P("dom", None),
        P("dom", None, None, None),
        P("dom", None),
        P(None, "dom", None, None),
        P(),
        P(),
        P(),
    )
    out_specs = (P("dom", None), P(None, "dom"))
    return jax.shard_map(
        per_device, mesh=mesh, in_specs=in_specs, out_specs=out_specs, check_vma=False
    )
```

```python
import functools

import jax
import jax.numpy as jnp
from jax import lax
from jax.experimental import pallas as pl
from jax.experimental.pallas import tpu as pltpu
from jax.sharding import PartitionSpec as P

ORB = 4
NB = 4
ITERS = 5
PANEL = 256
SUB = 128
VMEM_BYTES = 56 * 1024 * 1024


def passed_along(value, axis, steps):
    count = lax.axis_size(axis)
    pairs = [(source, (source + steps) % count) for source in range(count)]
    return lax.ppermute(value, axis, pairs)


def block_offset(block):
    if block < NB:
        return block + 1
    return NB - 1 - block


def halves(value):
    high = value.astype(jnp.bfloat16)
    low = (value - high.astype(jnp.float32)).astype(jnp.bfloat16)
    return high, low


def thirds(value):
    high = value.astype(jnp.bfloat16)
    rest = value - high.astype(jnp.float32)
    middle, low = halves(rest)
    return high, middle, low


def dot(left, right):
    return jnp.dot(left, right, preferred_element_type=jnp.float32)


def dot_one_hot(value, one_hot):
    return sum(dot(part, one_hot) for part in thirds(value))


def on_diagonal(shape):
    return lax.broadcasted_iota(jnp.int32, shape, 0) == lax.broadcasted_iota(jnp.int32, shape, 1)


def three_passes(left_high, left_low, right_high, right_low):
    return dot(
        jnp.concatenate([left_high, left_high, left_low], axis=1),
        jnp.concatenate([right_high, right_low, right_high], axis=0),
    )


def square_passes(left_high, left_low, right_high, right_low):
    cross = dot(left_high, right_low)
    return dot(left_high, right_high) + (cross + cross.T)


def step_factors(branches, number):
    taken = (branches[number] == 1).astype(jnp.float32)
    return 2.0 * taken, 1.0 - 2.0 * taken


def panels(start, end):
    cuts = [start] + [at for at in range(0, end, PANEL) if at > start] + [end]
    return [slice(low, high) for low, high in zip(cuts, cuts[1:])]


def spread_lanes(column, width):
    return jnp.concatenate([column] * (width // SUB), axis=1)


def combined(old, off, keep, add, state, rows_at, cols_at):
    diag_row, diag_col = state[2:]
    factor_col = spread_lanes(keep + add * diag_col[rows_at, :], old.shape[1])
    value = old * (factor_col + add * diag_row[0:1, cols_at]) + add * off
    if rows_at.start == cols_at.start:
        value = value - jnp.where(on_diagonal(value.shape), add * (old * old), 0.0)
    return value


def store_matrix(value, state, rows_at, cols_at):
    high_ref, low_ref, diag_row, diag_col = state
    if rows_at.start == cols_at.start:
        size = value.shape[0]
        line = jnp.where(on_diagonal(value.shape), value, 0.0)
        diag_row[:, cols_at] = jnp.broadcast_to(jnp.sum(line, axis=0, keepdims=True), (8, size))
        diag_col[rows_at, :] = jnp.broadcast_to(jnp.sum(line, axis=1, keepdims=True), (size, SUB))
        value = value - line
    high, low = halves(value)
    high_ref[rows_at, cols_at] = high
    low_ref[rows_at, cols_at] = low
    if rows_at.start != cols_at.start:
        high_ref[cols_at, rows_at] = high.T
        low_ref[cols_at, rows_at] = low.T


def start_block(source, row, col, top, scale):
    value = 0.5 * (source[row, col] + source[col, row].T)
    if row.start == col.start:
        value = value - jnp.where(on_diagonal(value.shape), top, 0.0)
    return -scale * value


def cut(size):
    return [slice(at, at + SUB) for at in range(0, size, SUB)]


def shifted(piece, by):
    return slice(piece.start + by, piece.stop + by)


def own_kernel(ends, branches, core, request_row, *refs):
    outs = refs[:9]
    row_out, x_own, x_cross, y_cross, y_halo, high, low, diag_row, diag_col = refs[9:18]
    next_high, next_low, next_row, next_col, sems = refs[18:]
    rows, order = core.shape
    state = (high, low, diag_row, diag_col)
    later = (next_high, next_low, next_row, next_col)
    left, right = slice(0, rows), slice(rows, order)
    copies = []

    def send(number, source):
        copy = pltpu.make_async_copy(source, outs[number], sems.at[number])
        copy.start()
        copies.append(copy)

    top = ends[0]
    scale = 1.0 / (ends[0] - ends[1])
    keep, add = step_factors(branches, 0)
    live_row = (request_row[...] >= 0).astype(jnp.float32)
    for row in cut(rows):
        for col in cut(order - rows):
            value = -scale * (core[row, shifted(col, rows)] * live_row[:, col])
            x_cross[row, col] = value
            store_matrix(value, state, row, shifted(col, rows))
    send(0, high.at[left, right])
    send(1, low.at[left, right])
    send(2, x_cross)
    for row in cut(rows):
        for col in cut(rows):
            if row.start <= col.start:
                value = start_block(core, row, col, top, scale)
                x_own[row, col] = value
                if row.start < col.start and row.start // PANEL == col.start // PANEL:
                    x_own[col, row] = value.T
                store_matrix(value, state, row, col)
    for row in panels(0, rows):
        for col in panels(rows, order):
            at = shifted(col, -rows)
            off = three_passes(high[row, left], low[row, left], high[left, col], low[left, col])
            factor = spread_lanes(keep + add * diag_col[row, :], at.stop - at.start)
            y_cross[row, at] = x_cross[row, at] * factor + add * off
    send(3, y_cross)
    for row in panels(rows, order):
        for col in panels(rows, order):
            if row.start <= col.start:
                passes = square_passes if row.start == col.start else three_passes
                off = passes(high[row, left], low[row, left], high[left, col], low[left, col])
                y_halo[shifted(row, -rows), shifted(col, -rows)] = add * off
    send(4, y_halo)
    for row in panels(0, rows):
        for col in panels(0, rows):
            if row.start <= col.start:
                passes = square_passes if row.start == col.start else three_passes
                off = passes(high[row, :], low[row, :], high[:, col], low[:, col])
                value = combined(x_own[row, col], off, keep, add, state, row, col)
                x_own[row, col] = value
                store_matrix(value, later, row, col)
    send(5, x_own)
    send(6, next_high)
    send(7, next_low)
    send(8, next_col)
    row_out[...] = next_row[...]
    for copy in copies:
        copy.wait()


def kernel(place, ends, branches, request_row, request_col, own_row, deriv, *refs):
    block_count = 2 * NB
    ready = refs[:9]
    pieces = refs[9 : 9 + block_count]
    density_out, own_out, mail = refs[9 + block_count : 12 + block_count]
    (x, high_a, low_a, high_b, low_b, diag_row_a, diag_row_b, diag_col_a, diag_col_b) = refs[
        12 + block_count : 21 + block_count
    ]
    (y_cross, y_halo, halo, density, deriv_held, row_part) = refs[21 + block_count : 27 + block_count]
    ready_sems, piece_sems, deriv_sems, out_sem = refs[27 + block_count :]
    rows, order = density.shape
    atoms = rows // ORB
    slot_rows = (order - rows) // block_count
    left, right = slice(0, rows), slice(rows, order)

    piece_copies = [
        pltpu.make_async_copy(
            pieces[block],
            halo.at[block * slot_rows : (block + 1) * slot_rows, :],
            piece_sems.at[block],
        )
        for block in range(block_count)
    ]
    targets = [
        high_b.at[left, right],
        low_b.at[left, right],
        x.at[left, right],
        y_cross,
        y_halo,
        x.at[left, left],
        high_a.at[left, left],
        low_a.at[left, left],
        diag_col_a.at[left, :],
    ]
    ready_copies = [
        pltpu.make_async_copy(source, target, ready_sems.at[number])
        for number, (source, target) in enumerate(zip(ready, targets))
    ]
    deriv_copies = [
        pltpu.make_async_copy(deriv.at[c], deriv_held.at[c], deriv_sems.at[c]) for c in range(3)
    ]
    for copy in piece_copies + ready_copies + deriv_copies:
        copy.start()
    state_a = (high_a, low_a, diag_row_a, diag_col_a)
    state_b = (high_b, low_b, diag_row_b, diag_col_b)

    top = ends[0]
    scale = 1.0 / (ends[0] - ends[1])
    live_row = (request_row[...] >= 0).astype(jnp.float32)
    live_col = (request_col[...] >= 0).astype(jnp.float32)
    diag_row_a[:, left] = own_row[...]
    for copy in piece_copies:
        copy.wait()
    for row in cut(order - rows):
        for col in cut(order - rows):
            if row.start <= col.start:
                value = start_block(halo, row, col, top, scale)
                value = value * live_col[row, :] * live_row[:, col]
                down, across = shifted(row, rows), shifted(col, rows)
                x[down, across] = value
                if row.start < col.start and down.start // PANEL == across.start // PANEL:
                    x[across, down] = value.T
                store_matrix(value, state_b, down, across)
    keep, add = step_factors(branches, 0)
    for copy in ready_copies[:4]:
        copy.wait()
    for row in panels(0, rows):
        for col in panels(rows, order):
            off = three_passes(
                high_b[row, right], low_b[row, right], high_b[right, col], low_b[right, col]
            )
            value = (
                y_cross[row, shifted(col, -rows)]
                + x[row, col] * (add * diag_row_b[0:1, col])
                + add * off
            )
            x[row, col] = value
            if row.start // PANEL == col.start // PANEL:
                x[col, row] = value.T
            store_matrix(value, state_a, row, col)
    for copy in ready_copies[4:]:
        copy.wait()
    for row in panels(rows, order):
        for col in panels(rows, order):
            if row.start <= col.start:
                passes = square_passes if row.start == col.start else three_passes
                off = passes(
                    high_b[row, right], low_b[row, right], high_b[right, col], low_b[right, col]
                )
                value = combined(x[row, col], off, keep, add, state_b, row, col)
                value = value + y_halo[shifted(row, -rows), shifted(col, -rows)]
                x[row, col] = value
                store_matrix(value, state_a, row, col)

    def stepped(number, now, rows_at, cols_at):
        keep, add = step_factors(branches, number)
        high, low = now[:2]
        passes = square_passes if rows_at == cols_at else three_passes
        off = passes(high[rows_at, :], low[rows_at, :], high[:, cols_at], low[:, cols_at])
        return combined(x[rows_at, cols_at], off, keep, add, now, rows_at, cols_at)

    def squaring(number, now, later):
        for cols in panels(0, order):
            for lines in panels(0, cols.stop):
                value = stepped(number, now, lines, cols)
                x[lines, cols] = value
                store_matrix(value, later, lines, cols)

    now, later = state_a, state_b
    for number in range(1, ITERS - 1):
        squaring(number, now, later)
        now, later = later, now
    for cols in panels(0, order):
        for lines in panels(0, min(cols.stop, rows)):
            value = stepped(ITERS - 1, now, lines, cols)
            density[lines, cols] = value
            if lines.start < cols.start < rows:
                end = min(cols.stop, rows)
                density[cols.start : end, lines] = value[:, 0 : end - cols.start].T

    out_copy = pltpu.make_async_copy(density, density_out, out_sem)
    out_copy.start()

    chunk = 64
    line = lax.broadcasted_iota(jnp.int32, (8, order), 0)
    columns = jnp.zeros((8, order), jnp.float32)
    own_rows = jnp.zeros((8, rows), jnp.float32)
    ones = jnp.ones((8, SUB), jnp.bfloat16)
    for c in range(3):
        deriv_copies[c].wait()

        def strip(number, total, c=c):
            at = pl.ds(pl.multiple_of(number * chunk, chunk), chunk)
            weighted = density[at, :] * deriv_held[c, at, :]
            row_part[at, :] = sum(weighted[:, lane : lane + SUB] for lane in range(0, order, SUB))
            return total + jnp.sum(weighted.reshape(chunk // 8, 8, order), axis=0)

        total = lax.fori_loop(0, rows // chunk, strip, jnp.zeros((8, order), jnp.float32))
        columns = jnp.where(line == c, jnp.sum(total, axis=0, keepdims=True), columns)
        row_sums = sum(
            lax.dot_general(ones, part, (((1,), (1,)), ((), ())), preferred_element_type=jnp.float32)
            for part in thirds(row_part[...])
        )
        own_rows = jnp.where(line[:, :rows] == c, row_sums, own_rows)
    atom_ids = lax.broadcasted_iota(jnp.int32, (rows, atoms), 1)
    own_hot = (lax.broadcasted_iota(jnp.int32, (rows, atoms), 0) // ORB == atom_ids).astype(jnp.float32)
    own_out[...] = dot_one_hot(2.0 * (own_rows - columns[:, :rows]), own_hot.astype(jnp.bfloat16))
    asked = request_row[...].astype(jnp.float32)
    letter = jnp.where(line[:, rows:] == 3, asked, -2.0 * columns[:, rows:])
    empty = jnp.where(lax.broadcasted_iota(jnp.int32, (4, SUB - slot_rows), 0) == 3, -1.0, 0.0)
    mail[...] = jnp.zeros(mail.shape, jnp.float32)
    for block in range(block_count):
        content = letter[0:4, block * slot_rows : (block + 1) * slot_rows]
        to = lax.rem(place[0] + (block_offset(block) + mail.shape[0]), mail.shape[0])
        mail[to] = jnp.concatenate([content, empty], axis=1)
    out_copy.wait()


def collect(place, mail, own, forces):
    count = mail.shape[0]
    atoms = own.shape[1]
    letters = jnp.concatenate(
        [mail[lax.rem(place[0] + (count - block_offset(block)), count)] for block in range(2 * NB)],
        axis=1,
    )
    wanted = letters[3:4, :] == lax.broadcasted_iota(jnp.int32, (atoms, 1), 0).astype(jnp.float32)
    wanted = wanted.astype(jnp.float32).astype(jnp.bfloat16)
    sums = sum(
        lax.dot_general(part, wanted, (((1,), (1,)), ((), ())), preferred_element_type=jnp.float32)
        for part in thirds(jnp.concatenate([letters, letters], axis=0))
    )
    forces[...] = own[0:3, :] + sums[0:3, :]


def own_part(ends, branches, core, request_row):
    rows, order = core.shape
    halo = order - rows
    vmem = pl.BlockSpec(memory_space=pltpu.VMEM)
    smem = pl.BlockSpec(memory_space=pltpu.SMEM)
    anywhere = pl.BlockSpec(memory_space=pl.ANY)
    kinds = [
        ((rows, halo), jnp.bfloat16),
        ((rows, halo), jnp.bfloat16),
        ((rows, halo), jnp.float32),
        ((rows, halo), jnp.float32),
        ((halo, halo), jnp.float32),
        ((rows, rows), jnp.float32),
        ((rows, rows), jnp.bfloat16),
        ((rows, rows), jnp.bfloat16),
        ((rows, SUB), jnp.float32),
    ]
    return pl.pallas_call(
        own_kernel,
        out_shape=[jax.ShapeDtypeStruct(*kind) for kind in kinds]
        + [jax.ShapeDtypeStruct((8, rows), jnp.float32)],
        in_specs=[smem, smem, vmem, vmem],
        out_specs=[anywhere] * len(kinds) + [vmem],
        scratch_shapes=[
            pltpu.VMEM((rows, rows), jnp.float32),
            pltpu.VMEM((rows, halo), jnp.float32),
            pltpu.VMEM((rows, halo), jnp.float32),
            pltpu.VMEM((halo, halo), jnp.float32),
            pltpu.VMEM((order, order), jnp.bfloat16),
            pltpu.VMEM((order, order), jnp.bfloat16),
            pltpu.VMEM((8, order), jnp.float32),
            pltpu.VMEM((order, SUB), jnp.float32),
            pltpu.VMEM((rows, rows), jnp.bfloat16),
            pltpu.VMEM((rows, rows), jnp.bfloat16),
            pltpu.VMEM((8, rows), jnp.float32),
            pltpu.VMEM((rows, SUB), jnp.float32),
            pltpu.SemaphoreType.DMA((len(kinds),)),
        ],
        compiler_params=pltpu.CompilerParams(vmem_limit_bytes=40 * 1024 * 1024),
        cost_estimate=pl.CostEstimate(
            flops=2 * 3 * order**3 // 3, bytes_accessed=13_000_000, transcendentals=0
        ),
    )(ends, branches, core, request_row)


def density_and_terms(place, ends, branches, request_row, request_col, own_row, deriv, ready, pieces):
    rows, order = deriv.shape[1:]
    atoms = rows // ORB
    vmem = pl.BlockSpec(memory_space=pltpu.VMEM)
    smem = pl.BlockSpec(memory_space=pltpu.SMEM)
    anywhere = pl.BlockSpec(memory_space=pl.ANY)
    square = (order, order)
    halo = order - rows
    return pl.pallas_call(
        kernel,
        out_shape=[
            jax.ShapeDtypeStruct((rows, order), jnp.float32),
            jax.ShapeDtypeStruct((8, atoms), jnp.float32),
            jax.ShapeDtypeStruct((lax.axis_size("dom"), 4, SUB), jnp.float32),
        ],
        in_specs=[smem, smem, smem, vmem, vmem, vmem, anywhere]
        + [anywhere] * (len(ready) + len(pieces)),
        out_specs=[anywhere, vmem, vmem],
        scratch_shapes=[
            pltpu.VMEM(square, jnp.float32),
            pltpu.VMEM(square, jnp.bfloat16),
            pltpu.VMEM(square, jnp.bfloat16),
            pltpu.VMEM(square, jnp.bfloat16),
            pltpu.VMEM(square, jnp.bfloat16),
            pltpu.VMEM((8, order), jnp.float32),
            pltpu.VMEM((8, order), jnp.float32),
            pltpu.VMEM((order, SUB), jnp.float32),
            pltpu.VMEM((order, SUB), jnp.float32),
            pltpu.VMEM((rows, halo), jnp.float32),
            pltpu.VMEM((halo, halo), jnp.float32),
            pltpu.VMEM((halo, halo), jnp.float32),
            pltpu.VMEM((rows, order), jnp.float32),
            pltpu.VMEM((3, rows, order), jnp.float32),
            pltpu.VMEM((rows, SUB), jnp.float32),
            pltpu.SemaphoreType.DMA((len(ready),)),
            pltpu.SemaphoreType.DMA((len(pieces),)),
            pltpu.SemaphoreType.DMA((3,)),
            pltpu.SemaphoreType.DMA,
        ],
        compiler_params=pltpu.CompilerParams(vmem_limit_bytes=VMEM_BYTES),
        cost_estimate=pl.CostEstimate(
            flops=2 * 3 * 3 * order**3, bytes_accessed=24_000_000, transcendentals=0
        ),
    )(place, ends, branches, request_row, request_col, own_row, deriv, *ready, *pieces)


def per_device(ham_core, halo_rows, halo_request, deriv, e_low, e_high, branches):
    row_count, order_all = ham_core.shape
    block_count = 2 * NB
    halo = halo_rows[0, :, :, row_count:]
    flat_deriv = deriv.reshape(3, row_count, order_all)
    early = (1, 2, 3, 5, 6)
    late = (0, 4, 7)
    pieces = {block: passed_along(halo[block], "dom", -block_offset(block)) for block in early}
    waiting, flat_deriv = lax.optimization_barrier(([halo[block] for block in late], flat_deriv))
    for block, piece in zip(late, waiting):
        pieces[block] = passed_along(piece, "dom", -block_offset(block))
    request = jnp.repeat(halo_request[0], ORB)
    place = lax.axis_index("dom")[None].astype(jnp.int32)
    ends = jnp.concatenate([e_high, e_low])
    *ready, own_row = own_part(ends, branches, ham_core, request[None, :])
    density, own, mail = density_and_terms(
        place,
        ends,
        branches,
        request[None, :],
        request[:, None],
        own_row,
        flat_deriv,
        ready,
        [pieces[block] for block in range(block_count)],
    )
    arrived = lax.all_to_all(mail, "dom", 0, 0, tiled=True)
    forces = pl.pallas_call(
        collect,
        out_shape=jax.ShapeDtypeStruct((3, own.shape[1]), jnp.float32),
        in_specs=[
            pl.BlockSpec(memory_space=pltpu.SMEM),
            pl.BlockSpec(memory_space=pltpu.VMEM),
            pl.BlockSpec(memory_space=pltpu.VMEM),
        ],
        out_specs=pl.BlockSpec(memory_space=pltpu.VMEM),
    )(place, arrived, own)
    return (density, forces)


def solution(mesh):
    in_specs = (
        P("dom", None),
        P("dom", None, None, None),
        P("dom", None),
        P(None, "dom", None, None),
        P(),
        P(),
        P(),
    )
    out_specs = (P("dom", None), P(None, "dom"))
    return jax.shard_map(
        per_device, mesh=mesh, in_specs=in_specs, out_specs=out_specs, check_vma=False
    )
```

```python
import functools

import jax
import jax.numpy as jnp
from jax import lax
from jax.experimental import pallas as pl
from jax.experimental.pallas import tpu as pltpu
from jax.sharding import PartitionSpec as P

ORB = 4
NB = 4
ITERS = 5
PANEL = 256
SUB = 128
VMEM_BYTES = 48 * 1024 * 1024


def passed_along(value, axis, steps):
    count = lax.axis_size(axis)
    pairs = [(source, (source + steps) % count) for source in range(count)]
    return lax.ppermute(value, axis, pairs)


def block_offset(block):
    if block < NB:
        return block + 1
    return NB - 1 - block


def halves(value):
    high = value.astype(jnp.bfloat16)
    low = (value - high.astype(jnp.float32)).astype(jnp.bfloat16)
    return high, low


def thirds(value):
    high = value.astype(jnp.bfloat16)
    rest = value - high.astype(jnp.float32)
    middle, low = halves(rest)
    return high, middle, low


def dot(left, right):
    return jnp.dot(left, right, preferred_element_type=jnp.float32)


def dot_one_hot(value, one_hot):
    return sum(dot(part, one_hot) for part in thirds(value))


def on_diagonal(shape):
    return lax.broadcasted_iota(jnp.int32, shape, 0) == lax.broadcasted_iota(jnp.int32, shape, 1)


def three_passes(left_high, left_low, right_high, right_low):
    return dot(
        jnp.concatenate([left_high, left_high, left_low], axis=1),
        jnp.concatenate([right_high, right_low, right_high], axis=0),
    )


def square_passes(left_high, left_low, right_high, right_low):
    cross = dot(left_high, right_low)
    return dot(left_high, right_high) + (cross + cross.T)


def step_factors(branches, number):
    taken = (branches[number] == 1).astype(jnp.float32)
    return 2.0 * taken, 1.0 - 2.0 * taken


def panels(start, end):
    cuts = [start] + [at for at in range(0, end, PANEL) if at > start] + [end]
    return [slice(low, high) for low, high in zip(cuts, cuts[1:])]


def spread_lanes(column, width):
    return jnp.concatenate([column] * (width // SUB), axis=1)


def combined(old, off, keep, add, state, rows_at, cols_at, on_diag):
    diag_row, diag_col = state[2:]
    factor_col = spread_lanes(keep + add * diag_col[rows_at, :], old.shape[1])
    value = old * (factor_col + add * diag_row[0:1, cols_at]) + add * off
    if on_diag:
        value = value - jnp.where(on_diagonal(value.shape), add * (old * old), 0.0)
    return value


def store_matrix(value, x, state, rows_at, cols_at, on_diag):
    high_ref, low_ref, diag_row, diag_col = state
    x[rows_at, cols_at] = value
    if on_diag:
        size = value.shape[0]
        line = jnp.where(on_diagonal(value.shape), value, 0.0)
        diag_row[:, cols_at] = jnp.broadcast_to(jnp.sum(line, axis=0, keepdims=True), (8, size))
        diag_col[rows_at, :] = jnp.broadcast_to(jnp.sum(line, axis=1, keepdims=True), (size, SUB))
        value = value - line
    high_ref[rows_at, cols_at], low_ref[rows_at, cols_at] = halves(value)
    if not on_diag:
        value = value.T
        x[cols_at, rows_at] = value
        high_ref[cols_at, rows_at], low_ref[cols_at, rows_at] = halves(value)


def piece_at(number, size):
    return pl.ds(pl.multiple_of(number * size, size), size)


def pairs_loop(count, size, visit):
    def panel(number, carry):
        for step in range((count + 1) // 2):
            other = number + step
            other = jnp.where(other >= count, other - count, other)
            visit(number, other, step == 0)
        return carry

    lax.fori_loop(0, count, panel, 0)


def asked_atoms(request, orbitals):
    atoms = request.shape[1]
    expand = lax.broadcasted_iota(jnp.int32, (orbitals, atoms), 0) // ORB == lax.broadcasted_iota(
        jnp.int32, (orbitals, atoms), 1
    )
    expand = expand.astype(jnp.float32).astype(jnp.bfloat16)
    values = jnp.broadcast_to(request[...].astype(jnp.float32), (8, atoms)).astype(jnp.bfloat16)
    transposed = (((1,), (1,)), ((), ()))
    row = lax.dot_general(values, expand, transposed, preferred_element_type=jnp.float32)
    col = lax.dot_general(expand, values, transposed, preferred_element_type=jnp.float32)
    return row[0:1, :], col[:, 0:1]


def start_block(source, row, col, on_diag, top, scale):
    value = 0.5 * (source[row, col] + source[col, row].T)
    if on_diag:
        value = value - jnp.where(on_diagonal(value.shape), top, 0.0)
    return -scale * value


def shifted(piece, by):
    return slice(piece.start + by, piece.stop + by)


def own_kernel(high_end, low_end, branches, core, request, *refs):
    outs = refs[:9]
    row_out, x_own, x_all, y_cross, y_halo, high, low, diag_row, diag_col = refs[9:18]
    next_high, next_low, next_row, next_col, live, sems = refs[18:]
    rows, order = core.shape
    state = (high, low, diag_row, diag_col)
    later = (next_high, next_low, next_row, next_col)
    left, right = slice(0, rows), slice(rows, order)
    copies = []

    def send(number, source):
        copy = pltpu.make_async_copy(source, outs[number], sems.at[number])
        copy.start()
        copies.append(copy)

    top = high_end[0]
    scale = 1.0 / (high_end[0] - low_end[0])
    keep, add = step_factors(branches, 0)
    asked_row, _ = asked_atoms(request, order - rows)
    live[:, right] = jnp.broadcast_to((asked_row >= 0).astype(jnp.float32), (8, order - rows))

    def cross_lines(number, carry):
        row = piece_at(number, SUB)
        for start in range(rows, order, SUB):
            col = slice(start, start + SUB)
            value = -scale * (core[row, col] * live[0:1, col])
            store_matrix(value, x_all, state, row, col, False)
        return carry

    lax.fori_loop(0, rows // SUB, cross_lines, 0)
    send(0, high.at[left, right])
    send(1, low.at[left, right])
    send(2, x_all.at[left, right])

    def own_block(number, other, on_diag):
        row, col = piece_at(number, SUB), piece_at(other, SUB)
        value = start_block(core, row, col, on_diag, top, scale)
        store_matrix(value, x_all, state, row, col, on_diag)

    pairs_loop(rows // SUB, SUB, own_block)
    for row in panels(0, rows):
        for col in panels(rows, order):
            at = shifted(col, -rows)
            off = three_passes(high[row, left], low[row, left], high[left, col], low[left, col])
            factor = spread_lanes(keep + add * diag_col[row, :], at.stop - at.start)
            y_cross[row, at] = x_all[row, col] * factor + add * off
    send(3, y_cross)
    for row in panels(rows, order):
        for col in panels(rows, order):
            if row.start <= col.start:
                passes = square_passes if row.start == col.start else three_passes
                off = passes(high[row, left], low[row, left], high[left, col], low[left, col])
                y_halo[shifted(row, -rows), shifted(col, -rows)] = add * off
    send(4, y_halo)
    for row in panels(0, rows):
        for col in panels(0, rows):
            if row.start <= col.start:
                passes = square_passes if row.start == col.start else three_passes
                off = passes(high[row, :], low[row, :], high[:, col], low[:, col])
                on_diag = row.start == col.start
                value = combined(x_all[row, col], off, keep, add, state, row, col, on_diag)
                store_matrix(value, x_own, later, row, col, on_diag)
    send(5, x_own)
    send(6, next_high)
    send(7, next_low)
    send(8, next_col)
    row_out[...] = next_row[...]
    for copy in copies:
        copy.wait()


def kernel(place, high_end, low_end, branches, request, own_row, deriv, *refs):
    block_count = 2 * NB
    ready = refs[:9]
    pieces = refs[9 : 9 + block_count]
    density_out, own_out, mail = refs[9 + block_count : 12 + block_count]
    (x, high_a, low_a, high_b, low_b, diag_row_a, diag_row_b, diag_col_a, diag_col_b) = refs[
        12 + block_count : 21 + block_count
    ]
    (y_cross, y_halo, halo, density, deriv_held, row_part) = refs[21 + block_count : 27 + block_count]
    live_row, live_col, ready_sems, piece_sems, deriv_sems, out_sem = refs[27 + block_count :]
    rows, order = density.shape
    atoms = rows // ORB
    slot_rows = (order - rows) // block_count
    left, right = slice(0, rows), slice(rows, order)

    piece_copies = [
        pltpu.make_async_copy(
            pieces[block],
            halo.at[block * slot_rows : (block + 1) * slot_rows, :],
            piece_sems.at[block],
        )
        for block in range(block_count)
    ]
    targets = [
        high_b.at[left, right],
        low_b.at[left, right],
        x.at[left, right],
        y_cross,
        y_halo,
        x.at[left, left],
        high_a.at[left, left],
        low_a.at[left, left],
        diag_col_a.at[left, :],
    ]
    ready_copies = [
        pltpu.make_async_copy(source, target, ready_sems.at[number])
        for number, (source, target) in enumerate(zip(ready, targets))
    ]
    deriv_copies = [
        pltpu.make_async_copy(deriv.at[c], deriv_held.at[c], deriv_sems.at[c]) for c in range(3)
    ]
    for copy in piece_copies + ready_copies:
        copy.start()
    state_a = (high_a, low_a, diag_row_a, diag_col_a)
    state_b = (high_b, low_b, diag_row_b, diag_col_b)

    top = high_end[0]
    scale = 1.0 / (high_end[0] - low_end[0])
    asked_row, asked_col = asked_atoms(request, order - rows)
    live_row[...] = jnp.broadcast_to((asked_row >= 0).astype(jnp.float32), (8, order - rows))
    live_col[...] = jnp.broadcast_to((asked_col >= 0).astype(jnp.float32), (order - rows, SUB))
    diag_row_a[:, left] = own_row[...]
    for copy in piece_copies:
        copy.wait()

    def halo_block(number, other, on_diag):
        row, col = piece_at(number, SUB), piece_at(other, SUB)
        value = start_block(halo, row, col, on_diag, top, scale)
        value = value * live_col[row, :] * live_row[0:1, col]
        first = rows // SUB
        down, across = piece_at(number + first, SUB), piece_at(other + first, SUB)
        store_matrix(value, x, state_b, down, across, on_diag)

    pairs_loop((order - rows) // SUB, SUB, halo_block)
    keep, add = step_factors(branches, 0)
    for copy in ready_copies[:4]:
        copy.wait()
    for copy in deriv_copies:
        copy.start()
    for row in panels(0, rows):
        for col in panels(rows, order):
            off = three_passes(
                high_b[row, right], low_b[row, right], high_b[right, col], low_b[right, col]
            )
            value = (
                y_cross[row, shifted(col, -rows)]
                + x[row, col] * (add * diag_row_b[0:1, col])
                + add * off
            )
            store_matrix(value, x, state_a, row, col, False)
    for copy in ready_copies[4:]:
        copy.wait()
    for row in panels(rows, order):
        for col in panels(rows, order):
            if row.start <= col.start:
                passes = square_passes if row.start == col.start else three_passes
                off = passes(
                    high_b[row, right], low_b[row, right], high_b[right, col], low_b[right, col]
                )
                on_diag = row.start == col.start
                value = combined(x[row, col], off, keep, add, state_b, row, col, on_diag)
                value = value + y_halo[shifted(row, -rows), shifted(col, -rows)]
                store_matrix(value, x, state_a, row, col, on_diag)

    def stepped(number, now, rows_at, cols_at, on_diag):
        keep, add = step_factors(branches, number)
        high, low = now[:2]
        passes = square_passes if on_diag else three_passes
        off = passes(high[rows_at, :], low[rows_at, :], high[:, cols_at], low[:, cols_at])
        return combined(x[rows_at, cols_at], off, keep, add, now, rows_at, cols_at, on_diag)

    def squaring(number, now, later):
        def block(line, other, on_diag):
            row, col = piece_at(line, PANEL), piece_at(other, PANEL)
            value = stepped(number, now, row, col, on_diag)
            store_matrix(value, x, later, row, col, on_diag)

        pairs_loop(order // PANEL, PANEL, block)

    now, later = state_a, state_b
    for number in range(1, ITERS - 1):
        squaring(number, now, later)
        now, later = later, now

    whole = rows // PANEL
    for col in range(whole):
        for row in range(col + 1):
            lines, cols = slice(row * PANEL, row * PANEL + PANEL), slice(col * PANEL, col * PANEL + PANEL)
            value = stepped(ITERS - 1, now, lines, cols, row == col)
            density[lines, cols] = value
            if row < col:
                density[cols, lines] = value.T

    def last_panel(number, carry):
        cols = piece_at(number, PANEL)
        for lines in panels(0, rows):
            keep, add = step_factors(branches, ITERS - 1)
            high, low = now[:2]
            off = three_passes(high[lines, :], low[lines, :], high[:, cols], low[:, cols])
            old = x[lines, cols]
            value = combined(old, off, keep, add, now, lines, cols, False)
            if lines.start == whole * PANEL:
                same = jnp.logical_and(on_diagonal(value.shape), number == whole)
                value = value - jnp.where(same, add * (old * old), 0.0)
            density[lines, cols] = value
        return carry

    lax.fori_loop(whole, order // PANEL, last_panel, 0)
    for lines in panels(0, whole * PANEL):
        density[whole * PANEL : rows, lines] = density[lines, whole * PANEL : rows].T

    out_copy = pltpu.make_async_copy(density, density_out, out_sem)
    out_copy.start()

    chunk = 64
    line = lax.broadcasted_iota(jnp.int32, (8, order), 0)
    columns = jnp.zeros((8, order), jnp.float32)
    own_rows = jnp.zeros((8, rows), jnp.float32)
    ones = jnp.ones((8, SUB), jnp.bfloat16)
    for c in range(3):
        deriv_copies[c].wait()

        def strip(number, total, c=c):
            at = pl.ds(pl.multiple_of(number * chunk, chunk), chunk)
            weighted = density[at, :] * deriv_held[c, at, :]
            row_part[at, :] = sum(weighted[:, lane : lane + SUB] for lane in range(0, order, SUB))
            return total + jnp.sum(weighted.reshape(chunk // 8, 8, order), axis=0)

        total = lax.fori_loop(0, rows // chunk, strip, jnp.zeros((8, order), jnp.float32))
        columns = jnp.where(line == c, jnp.sum(total, axis=0, keepdims=True), columns)
        row_sums = sum(
            lax.dot_general(ones, part, (((1,), (1,)), ((), ())), preferred_element_type=jnp.float32)
            for part in thirds(row_part[...])
        )
        own_rows = jnp.where(line[:, :rows] == c, row_sums, own_rows)
    atom_ids = lax.broadcasted_iota(jnp.int32, (rows, atoms), 1)
    own_hot = (lax.broadcasted_iota(jnp.int32, (rows, atoms), 0) // ORB == atom_ids).astype(jnp.float32)
    own_out[...] = dot_one_hot(2.0 * (own_rows - columns[:, :rows]), own_hot.astype(jnp.bfloat16))
    letter = jnp.where(line[:, rows:] == 3, asked_row, -2.0 * columns[:, rows:])
    empty = jnp.where(lax.broadcasted_iota(jnp.int32, (4, SUB - slot_rows), 0) == 3, -1.0, 0.0)
    mail[...] = jnp.zeros(mail.shape, jnp.float32)
    for block in range(block_count):
        content = letter[0:4, block * slot_rows : (block + 1) * slot_rows]
        to = lax.rem(place[0] + (block_offset(block) + mail.shape[0]), mail.shape[0])
        mail[to] = jnp.concatenate([content, empty], axis=1)
    out_copy.wait()


def collect(place, mail, own, forces):
    count = mail.shape[0]
    atoms = own.shape[1]
    letters = jnp.concatenate(
        [mail[lax.rem(place[0] + (count - block_offset(block)), count)] for block in range(2 * NB)],
        axis=1,
    )
    wanted = letters[3:4, :] == lax.broadcasted_iota(jnp.int32, (atoms, 1), 0).astype(jnp.float32)
    wanted = wanted.astype(jnp.float32).astype(jnp.bfloat16)
    sums = sum(
        lax.dot_general(part, wanted, (((1,), (1,)), ((), ())), preferred_element_type=jnp.float32)
        for part in thirds(jnp.concatenate([letters, letters], axis=0))
    )
    forces[...] = own[0:3, :] + sums[0:3, :]


def own_part(high_end, low_end, branches, core, request):
    rows, order = core.shape
    halo = order - rows
    vmem = pl.BlockSpec(memory_space=pltpu.VMEM)
    smem = pl.BlockSpec(memory_space=pltpu.SMEM)
    anywhere = pl.BlockSpec(memory_space=pl.ANY)
    kinds = [
        ((rows, halo), jnp.bfloat16),
        ((rows, halo), jnp.bfloat16),
        ((rows, halo), jnp.float32),
        ((rows, halo), jnp.float32),
        ((halo, halo), jnp.float32),
        ((rows, rows), jnp.float32),
        ((rows, rows), jnp.bfloat16),
        ((rows, rows), jnp.bfloat16),
        ((rows, SUB), jnp.float32),
    ]
    return pl.pallas_call(
        own_kernel,
        out_shape=[jax.ShapeDtypeStruct(*kind) for kind in kinds]
        + [jax.ShapeDtypeStruct((8, rows), jnp.float32)],
        in_specs=[smem, smem, smem, vmem, vmem],
        out_specs=[pl.BlockSpec(memory_space=pltpu.HBM)] * len(kinds) + [vmem],
        scratch_shapes=[
            pltpu.VMEM((rows, rows), jnp.float32),
            pltpu.VMEM((order, order), jnp.float32),
            pltpu.VMEM((rows, halo), jnp.float32),
            pltpu.VMEM((halo, halo), jnp.float32),
            pltpu.VMEM((order, order), jnp.bfloat16),
            pltpu.VMEM((order, order), jnp.bfloat16),
            pltpu.VMEM((8, order), jnp.float32),
            pltpu.VMEM((order, SUB), jnp.float32),
            pltpu.VMEM((rows, rows), jnp.bfloat16),
            pltpu.VMEM((rows, rows), jnp.bfloat16),
            pltpu.VMEM((8, rows), jnp.float32),
            pltpu.VMEM((rows, SUB), jnp.float32),
            pltpu.VMEM((8, order), jnp.float32),
            pltpu.SemaphoreType.DMA((len(kinds),)),
        ],
        compiler_params=pltpu.CompilerParams(vmem_limit_bytes=60 * 1024 * 1024),
        cost_estimate=pl.CostEstimate(
            flops=2 * 3 * order**3 // 3, bytes_accessed=13_000_000, transcendentals=0
        ),
    )(high_end, low_end, branches, core, request)


def density_and_terms(place, high_end, low_end, branches, request, own_row, deriv, ready, pieces):
    rows, order = deriv.shape[1:]
    atoms = rows // ORB
    vmem = pl.BlockSpec(memory_space=pltpu.VMEM)
    smem = pl.BlockSpec(memory_space=pltpu.SMEM)
    anywhere = pl.BlockSpec(memory_space=pl.ANY)
    square = (order, order)
    halo = order - rows
    return pl.pallas_call(
        kernel,
        out_shape=[
            jax.ShapeDtypeStruct((rows, order), jnp.float32),
            jax.ShapeDtypeStruct((8, atoms), jnp.float32),
            jax.ShapeDtypeStruct((lax.axis_size("dom"), 4, SUB), jnp.float32),
        ],
        in_specs=[smem, smem, smem, smem, vmem, vmem, anywhere]
        + [anywhere] * (len(ready) + len(pieces)),
        out_specs=[anywhere, vmem, vmem],
        scratch_shapes=[
            pltpu.VMEM(square, jnp.float32),
            pltpu.VMEM(square, jnp.bfloat16),
            pltpu.VMEM(square, jnp.bfloat16),
            pltpu.VMEM(square, jnp.bfloat16),
            pltpu.VMEM(square, jnp.bfloat16),
            pltpu.VMEM((8, order), jnp.float32),
            pltpu.VMEM((8, order), jnp.float32),
            pltpu.VMEM((order, SUB), jnp.float32),
            pltpu.VMEM((order, SUB), jnp.float32),
            pltpu.VMEM((rows, halo), jnp.float32),
            pltpu.VMEM((halo, halo), jnp.float32),
            pltpu.VMEM((halo, halo), jnp.float32),
            pltpu.VMEM((rows, order), jnp.float32),
            pltpu.VMEM((3, rows, order), jnp.float32),
            pltpu.VMEM((rows, SUB), jnp.float32),
            pltpu.VMEM((8, halo), jnp.float32),
            pltpu.VMEM((halo, SUB), jnp.float32),
            pltpu.SemaphoreType.DMA((len(ready),)),
            pltpu.SemaphoreType.DMA((len(pieces),)),
            pltpu.SemaphoreType.DMA((3,)),
            pltpu.SemaphoreType.DMA,
        ],
        compiler_params=pltpu.CompilerParams(vmem_limit_bytes=VMEM_BYTES),
        cost_estimate=pl.CostEstimate(
            flops=2 * 3 * 3 * order**3, bytes_accessed=24_000_000, transcendentals=0
        ),
    )(place, high_end, low_end, branches, request, own_row, deriv, *ready, *pieces)


def per_device(ham_core, halo_rows, halo_request, deriv, e_low, e_high, branches):
    row_count, order_all = ham_core.shape
    block_count = 2 * NB
    halo = halo_rows[0, :, :, row_count:]
    flat_deriv = deriv.reshape(3, row_count, order_all)
    early = (1, 2, 3, 5, 6)
    late = (0, 4, 7)
    pieces = {block: passed_along(halo[block], "dom", -block_offset(block)) for block in early}
    waiting, flat_deriv = lax.optimization_barrier(([halo[block] for block in late], flat_deriv))
    for block, piece in zip(late, waiting):
        pieces[block] = passed_along(piece, "dom", -block_offset(block))
    place = lax.axis_index("dom")[None].astype(jnp.int32)
    *ready, own_row = own_part(e_high, e_low, branches, ham_core, halo_request)
    density, own, mail = density_and_terms(
        place,
        e_high,
        e_low,
        branches,
        halo_request,
        own_row,
        flat_deriv,
        ready,
        [pieces[block] for block in range(block_count)],
    )
    arrived = lax.all_to_all(mail, "dom", 0, 0, tiled=True)
    forces = pl.pallas_call(
        collect,
        out_shape=jax.ShapeDtypeStruct((3, own.shape[1]), jnp.float32),
        in_specs=[
            pl.BlockSpec(memory_space=pltpu.SMEM),
            pl.BlockSpec(memory_space=pltpu.VMEM),
            pl.BlockSpec(memory_space=pltpu.VMEM),
        ],
        out_specs=pl.BlockSpec(memory_space=pltpu.VMEM),
    )(place, arrived, own)
    return (density, forces)


def solution(mesh):
    in_specs = (
        P("dom", None),
        P("dom", None, None, None),
        P("dom", None),
        P(None, "dom", None, None),
        P(),
        P(),
        P(),
    )
    out_specs = (P("dom", None), P(None, "dom"))
    return jax.shard_map(
        per_device, mesh=mesh, in_specs=in_specs, out_specs=out_specs, check_vma=False
    )
```

```python
import functools

import jax
import jax.numpy as jnp
from jax import lax
from jax.experimental import pallas as pl
from jax.experimental.pallas import tpu as pltpu
from jax.sharding import PartitionSpec as P

ORB = 4
NB = 4
ITERS = 5
PANEL = 256
SUB = 128
VMEM_BYTES = 38 * 1024 * 1024
OWN_VMEM_BYTES = 16 * 1024 * 1024


def passed_along(value, axis, steps):
    count = lax.axis_size(axis)
    pairs = [(source, (source + steps) % count) for source in range(count)]
    return lax.ppermute(value, axis, pairs)


def block_offset(block):
    if block < NB:
        return block + 1
    return NB - 1 - block


def halves(value):
    high = value.astype(jnp.bfloat16)
    low = (value - high.astype(jnp.float32)).astype(jnp.bfloat16)
    return high, low


def thirds(value):
    high = value.astype(jnp.bfloat16)
    rest = value - high.astype(jnp.float32)
    middle, low = halves(rest)
    return high, middle, low


def dot(left, right):
    return jnp.dot(left, right, preferred_element_type=jnp.float32)


def dot_one_hot(value, one_hot):
    return sum(dot(part, one_hot) for part in thirds(value))


def on_diagonal(shape):
    return lax.broadcasted_iota(jnp.int32, shape, 0) == lax.broadcasted_iota(jnp.int32, shape, 1)


def three_passes(left_high, left_low, right_high, right_low):
    return dot(
        jnp.concatenate([left_high, left_high, left_low], axis=1),
        jnp.concatenate([right_high, right_low, right_high], axis=0),
    )


def square_passes(left_high, left_low, right_high, right_low):
    cross = dot(left_high, right_low)
    return dot(left_high, right_high) + (cross + cross.T)


def step_factors(branches, number):
    taken = (branches[number] == 1).astype(jnp.float32)
    return 2.0 * taken, 1.0 - 2.0 * taken


def panels(start, end):
    cuts = [start] + [at for at in range(0, end, PANEL) if at > start] + [end]
    return [slice(low, high) for low, high in zip(cuts, cuts[1:])]


def spread_lanes(column, width):
    return jnp.concatenate([column] * (width // SUB), axis=1)


def combined(old, off, keep, add, state, rows_at, cols_at):
    diag_row, diag_col = state[2:]
    factor_col = spread_lanes(keep + add * diag_col[rows_at, :], old.shape[1])
    value = old * (factor_col + add * diag_row[0:1, cols_at]) + add * off
    if rows_at.start == cols_at.start:
        value = value - jnp.where(on_diagonal(value.shape), add * (old * old), 0.0)
    return value


def store_matrix(value, state, rows_at, cols_at):
    high_ref, low_ref, diag_row, diag_col = state
    if rows_at.start == cols_at.start:
        size = value.shape[0]
        line = jnp.where(on_diagonal(value.shape), value, 0.0)
        diag_row[:, cols_at] = jnp.broadcast_to(jnp.sum(line, axis=0, keepdims=True), (8, size))
        diag_col[rows_at, :] = jnp.broadcast_to(jnp.sum(line, axis=1, keepdims=True), (size, SUB))
        value = value - line
    high, low = halves(value)
    high_ref[rows_at, cols_at] = high
    low_ref[rows_at, cols_at] = low
    if rows_at.start != cols_at.start:
        high_ref[cols_at, rows_at] = high.T
        low_ref[cols_at, rows_at] = low.T


def start_block(source, row, col, top, scale):
    value = 0.5 * (source[row, col] + source[col, row].T)
    if row.start == col.start:
        value = value - jnp.where(on_diagonal(value.shape), top, 0.0)
    return -scale * value


def cut(size):
    return [slice(at, at + SUB) for at in range(0, size, SUB)]


def shifted(piece, by):
    return slice(piece.start + by, piece.stop + by)


def asked_atoms(request, orbitals):
    atoms = request.shape[1]
    expand = lax.broadcasted_iota(jnp.int32, (orbitals, atoms), 0) // ORB == lax.broadcasted_iota(
        jnp.int32, (orbitals, atoms), 1
    )
    expand = expand.astype(jnp.float32).astype(jnp.bfloat16)
    values = jnp.broadcast_to(request[...].astype(jnp.float32), (8, atoms)).astype(jnp.bfloat16)
    transposed = (((1,), (1,)), ((), ()))
    row = lax.dot_general(values, expand, transposed, preferred_element_type=jnp.float32)
    col = lax.dot_general(expand, values, transposed, preferred_element_type=jnp.float32)
    return row[0:1, :], col[:, 0:1]


def own_kernel(
    high_end, low_end, branches, core, request, high_cross, low_cross, x_cross, y_cross, y_halo,
    x_own, next_high, next_low, next_col, next_row, high, low, diag_row, diag_col
):
    rows, order = core.shape
    state = (high, low, diag_row, diag_col)
    later = (next_high, next_low, next_row, next_col)
    left, right = slice(0, rows), slice(rows, order)
    top = high_end[0]
    scale = 1.0 / (high_end[0] - low_end[0])
    keep, add = step_factors(branches, 0)
    asked_row, _ = asked_atoms(request, order - rows)
    live_row = (asked_row >= 0).astype(jnp.float32)
    for row in cut(rows):
        for col in cut(order - rows):
            value = -scale * (core[row, shifted(col, rows)] * live_row[:, col])
            x_cross[row, col] = value
            store_matrix(value, state, row, shifted(col, rows))
    for row in cut(rows):
        for col in cut(rows):
            if row.start <= col.start:
                value = start_block(core, row, col, top, scale)
                x_own[row, col] = value
                if row.start < col.start and row.start // PANEL == col.start // PANEL:
                    x_own[col, row] = value.T
                store_matrix(value, state, row, col)
    high_cross[...] = high[left, right]
    low_cross[...] = low[left, right]
    for row in panels(0, rows):
        for col in panels(rows, order):
            at = shifted(col, -rows)
            off = three_passes(high[row, left], low[row, left], high[left, col], low[left, col])
            factor = spread_lanes(keep + add * diag_col[row, :], at.stop - at.start)
            y_cross[row, at] = x_cross[row, at] * factor + add * off
    for row in panels(rows, order):
        for col in panels(rows, order):
            if row.start <= col.start:
                passes = square_passes if row.start == col.start else three_passes
                off = passes(high[row, left], low[row, left], high[left, col], low[left, col])
                y_halo[shifted(row, -rows), shifted(col, -rows)] = add * off
    for row in panels(0, rows):
        for col in panels(0, rows):
            if row.start <= col.start:
                passes = square_passes if row.start == col.start else three_passes
                off = passes(high[row, :], low[row, :], high[:, col], low[:, col])
                value = combined(x_own[row, col], off, keep, add, state, row, col)
                x_own[row, col] = value
                store_matrix(value, later, row, col)


def kernel(place, high_end, low_end, branches, request, deriv, *refs):
    block_count = 2 * NB
    (high_cross, low_cross, x_cross, y_cross, y_halo, x_own, high_own, low_own, own_col, own_row) = refs[:10]
    pieces = refs[10 : 10 + block_count]
    density_out, own_out, mail = refs[10 + block_count : 13 + block_count]
    (x, high_a, low_a, high_b, low_b, diag_row_a, diag_row_b, diag_col_a, diag_col_b) = refs[
        13 + block_count : 22 + block_count
    ]
    (high_c, low_c, diag_row_c, diag_col_c, halo, deriv_held, row_part, deriv_sems, out_sem) = refs[
        22 + block_count :
    ]
    order = x.shape[0]
    rows = x_own.shape[0]
    atoms = rows // ORB
    slot_rows = (order - rows) // block_count
    left, right = slice(0, rows), slice(rows, order)

    deriv_copies = [
        pltpu.make_async_copy(deriv.at[c], deriv_held.at[c], deriv_sems.at[c]) for c in range(3)
    ]
    for copy in deriv_copies:
        copy.start()
    state_a = (high_a, low_a, diag_row_a, diag_col_a)
    state_b = (high_b, low_b, diag_row_b, diag_col_b)
    state_c = (high_c, low_c, diag_row_c, diag_col_c)

    top = high_end[0]
    scale = 1.0 / (high_end[0] - low_end[0])
    for block in range(block_count):
        halo[block * slot_rows : (block + 1) * slot_rows, :] = pieces[block][...]
    asked_row, asked_col = asked_atoms(request, order - rows)
    live_row = (asked_row >= 0).astype(jnp.float32)
    live_col = (asked_col >= 0).astype(jnp.float32)
    for row in cut(order - rows):
        for col in cut(order - rows):
            if row.start <= col.start:
                value = start_block(halo, row, col, top, scale)
                value = value * live_col[row, :] * live_row[:, col]
                down, across = shifted(row, rows), shifted(col, rows)
                x[down, across] = value
                if row.start < col.start and down.start // PANEL == across.start // PANEL:
                    x[across, down] = value.T
                store_matrix(value, state_c, row, col)
    x[left, left] = x_own[...]
    high_a[left, left] = high_own[...]
    low_a[left, left] = low_own[...]
    diag_col_a[left, :] = own_col[...]
    diag_row_a[:, left] = own_row[...]
    keep, add = step_factors(branches, 0)
    for row in panels(0, rows):
        for col in panels(rows, order):
            at = shifted(col, -rows)
            off = three_passes(high_cross[row, :], low_cross[row, :], high_c[:, at], low_c[:, at])
            value = y_cross[row, at] + x_cross[row, at] * (add * diag_row_c[0:1, at]) + add * off
            x[row, col] = value
            if row.start // PANEL == col.start // PANEL:
                x[col, row] = value.T
            store_matrix(value, state_a, row, col)
    for row in panels(rows, order):
        for col in panels(rows, order):
            if row.start <= col.start:
                down, across = shifted(row, -rows), shifted(col, -rows)
                passes = square_passes if row.start == col.start else three_passes
                off = passes(high_c[down, :], low_c[down, :], high_c[:, across], low_c[:, across])
                value = combined(x[row, col], off, keep, add, state_c, down, across)
                value = value + y_halo[down, across]
                x[row, col] = value
                store_matrix(value, state_a, row, col)

    def stepped(number, now, rows_at, cols_at):
        keep, add = step_factors(branches, number)
        high, low = now[:2]
        passes = square_passes if rows_at == cols_at else three_passes
        off = passes(high[rows_at, :], low[rows_at, :], high[:, cols_at], low[:, cols_at])
        return combined(x[rows_at, cols_at], off, keep, add, now, rows_at, cols_at)

    def squaring(number, now, later):
        for cols in panels(0, order):
            for lines in panels(0, cols.stop):
                value = stepped(number, now, lines, cols)
                x[lines, cols] = value
                store_matrix(value, later, lines, cols)

    now, later = state_a, state_b
    for number in range(1, ITERS - 1):
        squaring(number, now, later)
        now, later = later, now
    for cols in panels(0, order):
        for lines in panels(0, min(cols.stop, rows)):
            value = stepped(ITERS - 1, now, lines, cols)
            x[lines, cols] = value
            if lines.start < cols.start < rows:
                end = min(cols.stop, rows)
                x[cols.start : end, lines] = value[:, 0 : end - cols.start].T

    out_copy = pltpu.make_async_copy(x.at[left, :], density_out, out_sem)
    out_copy.start()

    chunk = 64
    line = lax.broadcasted_iota(jnp.int32, (8, order), 0)
    columns = jnp.zeros((8, order), jnp.float32)
    own_rows = jnp.zeros((8, rows), jnp.float32)
    ones = jnp.ones((8, SUB), jnp.bfloat16)
    for c in range(3):
        deriv_copies[c].wait()

        def strip(number, total, c=c):
            at = pl.ds(pl.multiple_of(number * chunk, chunk), chunk)
            weighted = x[at, :] * deriv_held[c, at, :]
            row_part[at, :] = sum(weighted[:, lane : lane + SUB] for lane in range(0, order, SUB))
            return total + jnp.sum(weighted.reshape(chunk // 8, 8, order), axis=0)

        total = lax.fori_loop(0, rows // chunk, strip, jnp.zeros((8, order), jnp.float32))
        columns = jnp.where(line == c, jnp.sum(total, axis=0, keepdims=True), columns)
        row_sums = sum(
            lax.dot_general(ones, part, (((1,), (1,)), ((), ())), preferred_element_type=jnp.float32)
            for part in thirds(row_part[...])
        )
        own_rows = jnp.where(line[:, :rows] == c, row_sums, own_rows)
    atom_ids = lax.broadcasted_iota(jnp.int32, (rows, atoms), 1)
    own_hot = (lax.broadcasted_iota(jnp.int32, (rows, atoms), 0) // ORB == atom_ids).astype(jnp.float32)
    own_out[...] = dot_one_hot(2.0 * (own_rows - columns[:, :rows]), own_hot.astype(jnp.bfloat16))
    letter = jnp.where(line[:, rows:] == 3, asked_row, -2.0 * columns[:, rows:])
    empty = jnp.where(lax.broadcasted_iota(jnp.int32, (4, SUB - slot_rows), 0) == 3, -1.0, 0.0)
    mail[...] = jnp.zeros(mail.shape, jnp.float32)
    for block in range(block_count):
        content = letter[0:4, block * slot_rows : (block + 1) * slot_rows]
        to = lax.rem(place[0] + (block_offset(block) + mail.shape[0]), mail.shape[0])
        mail[to] = jnp.concatenate([content, empty], axis=1)
    out_copy.wait()


def collect(place, mail, own, forces):
    count = mail.shape[0]
    atoms = own.shape[1]
    letters = jnp.concatenate(
        [mail[lax.rem(place[0] + (count - block_offset(block)), count)] for block in range(2 * NB)],
        axis=1,
    )
    wanted = letters[3:4, :] == lax.broadcasted_iota(jnp.int32, (atoms, 1), 0).astype(jnp.float32)
    wanted = wanted.astype(jnp.float32).astype(jnp.bfloat16)
    sums = sum(
        lax.dot_general(part, wanted, (((1,), (1,)), ((), ())), preferred_element_type=jnp.float32)
        for part in thirds(jnp.concatenate([letters, letters], axis=0))
    )
    forces[...] = own[0:3, :] + sums[0:3, :]


def own_part(high_end, low_end, branches, core, request):
    rows, order = core.shape
    halo = order - rows
    vmem = pl.BlockSpec(memory_space=pltpu.VMEM)
    smem = pl.BlockSpec(memory_space=pltpu.SMEM)
    kinds = [
        ((rows, halo), jnp.bfloat16),
        ((rows, halo), jnp.bfloat16),
        ((rows, halo), jnp.float32),
        ((rows, halo), jnp.float32),
        ((halo, halo), jnp.float32),
        ((rows, rows), jnp.float32),
        ((rows, rows), jnp.bfloat16),
        ((rows, rows), jnp.bfloat16),
        ((rows, SUB), jnp.float32),
        ((8, rows), jnp.float32),
    ]
    return pl.pallas_call(
        own_kernel,
        out_shape=[jax.ShapeDtypeStruct(*kind) for kind in kinds],
        in_specs=[smem, smem, smem, vmem, vmem],
        out_specs=[vmem] * len(kinds),
        scratch_shapes=[
            pltpu.VMEM((order, order), jnp.bfloat16),
            pltpu.VMEM((order, order), jnp.bfloat16),
            pltpu.VMEM((8, order), jnp.float32),
            pltpu.VMEM((order, SUB), jnp.float32),
        ],
        compiler_params=pltpu.CompilerParams(vmem_limit_bytes=OWN_VMEM_BYTES),
        cost_estimate=pl.CostEstimate(
            flops=2 * 3 * order**3 // 3, bytes_accessed=13_000_000, transcendentals=0
        ),
    )(high_end, low_end, branches, core, request)


def density_and_terms(place, high_end, low_end, branches, request, deriv, ready, pieces):
    rows, order = deriv.shape[1:]
    atoms = rows // ORB
    vmem = pl.BlockSpec(memory_space=pltpu.VMEM)
    smem = pl.BlockSpec(memory_space=pltpu.SMEM)
    anywhere = pl.BlockSpec(memory_space=pl.ANY)
    square = (order, order)
    halo = order - rows
    return pl.pallas_call(
        kernel,
        out_shape=[
            jax.ShapeDtypeStruct((rows, order), jnp.float32),
            jax.ShapeDtypeStruct((8, atoms), jnp.float32),
            jax.ShapeDtypeStruct((lax.axis_size("dom"), 4, SUB), jnp.float32),
        ],
        in_specs=[smem, smem, smem, smem, vmem, anywhere] + [vmem] * (len(ready) + len(pieces)),
        out_specs=[anywhere, vmem, vmem],
        scratch_shapes=[
            pltpu.VMEM(square, jnp.float32),
            pltpu.VMEM(square, jnp.bfloat16),
            pltpu.VMEM(square, jnp.bfloat16),
            pltpu.VMEM(square, jnp.bfloat16),
            pltpu.VMEM(square, jnp.bfloat16),
            pltpu.VMEM((8, order), jnp.float32),
            pltpu.VMEM((8, order), jnp.float32),
            pltpu.VMEM((order, SUB), jnp.float32),
            pltpu.VMEM((order, SUB), jnp.float32),
            pltpu.VMEM((halo, halo), jnp.bfloat16),
            pltpu.VMEM((halo, halo), jnp.bfloat16),
            pltpu.VMEM((8, halo), jnp.float32),
            pltpu.VMEM((halo, SUB), jnp.float32),
            pltpu.VMEM((halo, halo), jnp.float32),
            pltpu.VMEM((3, rows, order), jnp.float32),
            pltpu.VMEM((rows, SUB), jnp.float32),
            pltpu.SemaphoreType.DMA((3,)),
            pltpu.SemaphoreType.DMA,
        ],
        compiler_params=pltpu.CompilerParams(vmem_limit_bytes=VMEM_BYTES),
        cost_estimate=pl.CostEstimate(
            flops=2 * 3 * 3 * order**3, bytes_accessed=24_000_000, transcendentals=0
        ),
    )(place, high_end, low_end, branches, request, deriv, *ready, *pieces)


def per_device(ham_core, halo_rows, halo_request, deriv, e_low, e_high, branches):
    row_count, order_all = ham_core.shape
    block_count = 2 * NB
    halo = halo_rows[0, :, :, row_count:]
    flat_deriv = deriv.reshape(3, row_count, order_all)
    early = (1, 2, 3, 5, 6)
    late = (0, 4, 7)
    pieces = {block: passed_along(halo[block], "dom", -block_offset(block)) for block in early}
    waiting, flat_deriv = lax.optimization_barrier(([halo[block] for block in late], flat_deriv))
    for block, piece in zip(late, waiting):
        pieces[block] = passed_along(piece, "dom", -block_offset(block))
    place = lax.axis_index("dom")[None].astype(jnp.int32)
    ready = own_part(e_high, e_low, branches, ham_core, halo_request)
    density, own, mail = density_and_terms(
        place,
        e_high,
        e_low,
        branches,
        halo_request,
        flat_deriv,
        ready,
        [pieces[block] for block in range(block_count)],
    )
    arrived = lax.all_to_all(mail, "dom", 0, 0, tiled=True)
    forces = pl.pallas_call(
        collect,
        out_shape=jax.ShapeDtypeStruct((3, own.shape[1]), jnp.float32),
        in_specs=[
            pl.BlockSpec(memory_space=pltpu.SMEM),
            pl.BlockSpec(memory_space=pltpu.VMEM),
            pl.BlockSpec(memory_space=pltpu.VMEM),
        ],
        out_specs=pl.BlockSpec(memory_space=pltpu.VMEM),
    )(place, arrived, own)
    return (density, forces)


def solution(mesh):
    in_specs = (
        P("dom", None),
        P("dom", None, None, None),
        P("dom", None),
        P(None, "dom", None, None),
        P(),
        P(),
        P(),
    )
    out_specs = (P("dom", None), P(None, "dom"))
    return jax.shard_map(
        per_device, mesh=mesh, in_specs=in_specs, out_specs=out_specs, check_vma=False
    )
```

```python
import functools

import jax
import jax.numpy as jnp
from jax import lax
from jax.experimental import pallas as pl
from jax.experimental.pallas import tpu as pltpu
from jax.sharding import PartitionSpec as P

ORB = 4
NB = 4
ITERS = 5
PANEL = 256
SUB = 128
VMEM_BYTES = 40 * 1024 * 1024
OWN_VMEM_BYTES = 16 * 1024 * 1024


def passed_along(value, axis, steps):
    count = lax.axis_size(axis)
    pairs = [(source, (source + steps) % count) for source in range(count)]
    return lax.ppermute(value, axis, pairs)


def block_offset(block):
    if block < NB:
        return block + 1
    return NB - 1 - block


def halves(value):
    high = value.astype(jnp.bfloat16)
    low = (value - high.astype(jnp.float32)).astype(jnp.bfloat16)
    return high, low


def thirds(value):
    high = value.astype(jnp.bfloat16)
    rest = value - high.astype(jnp.float32)
    middle, low = halves(rest)
    return high, middle, low


def dot(left, right):
    return jnp.dot(left, right, preferred_element_type=jnp.float32)


def dot_one_hot(value, one_hot):
    return sum(dot(part, one_hot) for part in thirds(value))


def on_diagonal(shape):
    return lax.broadcasted_iota(jnp.int32, shape, 0) == lax.broadcasted_iota(jnp.int32, shape, 1)


def three_passes(left_high, left_low, right_high, right_low):
    return dot(
        jnp.concatenate([left_high, left_high, left_low], axis=1),
        jnp.concatenate([right_high, right_low, right_high], axis=0),
    )


def square_passes(left_high, left_low, right_high, right_low):
    cross = dot(left_high, right_low)
    return dot(left_high, right_high) + (cross + cross.T)


def step_factors(branches, number):
    taken = (branches[number] == 1).astype(jnp.float32)
    return 2.0 * taken, 1.0 - 2.0 * taken


def panels(start, end):
    cuts = [start] + [at for at in range(0, end, PANEL) if at > start] + [end]
    return [slice(low, high) for low, high in zip(cuts, cuts[1:])]


def spread_lanes(column, width):
    return jnp.concatenate([column] * (width // SUB), axis=1)


def combined(old, off, keep, add, state, rows_at, cols_at, on_diag):
    diag_row, diag_col = state[2:]
    factor_col = spread_lanes(keep + add * diag_col[rows_at, :], old.shape[1])
    value = old * (factor_col + add * diag_row[0:1, cols_at]) + add * off
    if on_diag:
        value = value - jnp.where(on_diagonal(value.shape), add * (old * old), 0.0)
    return value


def store_matrix(value, state, rows_at, cols_at):
    high_ref, low_ref, diag_row, diag_col = state
    if rows_at.start == cols_at.start:
        size = value.shape[0]
        line = jnp.where(on_diagonal(value.shape), value, 0.0)
        diag_row[:, cols_at] = jnp.broadcast_to(jnp.sum(line, axis=0, keepdims=True), (8, size))
        diag_col[rows_at, :] = jnp.broadcast_to(jnp.sum(line, axis=1, keepdims=True), (size, SUB))
        value = value - line
    high, low = halves(value)
    high_ref[rows_at, cols_at] = high
    low_ref[rows_at, cols_at] = low
    if rows_at.start != cols_at.start:
        high_ref[cols_at, rows_at] = high.T
        low_ref[cols_at, rows_at] = low.T


def store_mirrored(value, x, state, rows_at, cols_at, on_diag):
    high_ref, low_ref, diag_row, diag_col = state
    x[rows_at, cols_at] = value
    if on_diag:
        size = value.shape[0]
        line = jnp.where(on_diagonal(value.shape), value, 0.0)
        diag_row[:, cols_at] = jnp.broadcast_to(jnp.sum(line, axis=0, keepdims=True), (8, size))
        diag_col[rows_at, :] = jnp.broadcast_to(jnp.sum(line, axis=1, keepdims=True), (size, SUB))
        value = value - line
    high_ref[rows_at, cols_at], low_ref[rows_at, cols_at] = halves(value)
    if not on_diag:
        value = value.T
        x[cols_at, rows_at] = value
        high_ref[cols_at, rows_at], low_ref[cols_at, rows_at] = halves(value)


def panel_at(number):
    return pl.ds(pl.multiple_of(number * PANEL, PANEL), PANEL)


def start_block(source, row, col, top, scale):
    value = 0.5 * (source[row, col] + source[col, row].T)
    if row.start == col.start:
        value = value - jnp.where(on_diagonal(value.shape), top, 0.0)
    return -scale * value


def cut(size):
    return [slice(at, at + SUB) for at in range(0, size, SUB)]


def shifted(piece, by):
    return slice(piece.start + by, piece.stop + by)


def asked_atoms(request, orbitals):
    atoms = request.shape[1]
    expand = lax.broadcasted_iota(jnp.int32, (orbitals, atoms), 0) // ORB == lax.broadcasted_iota(
        jnp.int32, (orbitals, atoms), 1
    )
    expand = expand.astype(jnp.float32).astype(jnp.bfloat16)
    values = jnp.broadcast_to(request[...].astype(jnp.float32), (8, atoms)).astype(jnp.bfloat16)
    transposed = (((1,), (1,)), ((), ()))
    row = lax.dot_general(values, expand, transposed, preferred_element_type=jnp.float32)
    col = lax.dot_general(expand, values, transposed, preferred_element_type=jnp.float32)
    return row[0:1, :], col[:, 0:1]


def own_kernel(
    high_end, low_end, branches, core, request, high_cross, low_cross, x_cross, y_cross, y_halo,
    x_own, next_high, next_low, next_col, next_row, high, low, diag_row, diag_col
):
    rows, order = core.shape
    state = (high, low, diag_row, diag_col)
    later = (next_high, next_low, next_row, next_col)
    left, right = slice(0, rows), slice(rows, order)
    top = high_end[0]
    scale = 1.0 / (high_end[0] - low_end[0])
    keep, add = step_factors(branches, 0)
    asked_row, _ = asked_atoms(request, order - rows)
    live_row = (asked_row >= 0).astype(jnp.float32)
    for row in cut(rows):
        for col in cut(order - rows):
            value = -scale * (core[row, shifted(col, rows)] * live_row[:, col])
            x_cross[row, col] = value
            store_matrix(value, state, row, shifted(col, rows))
    for row in cut(rows):
        for col in cut(rows):
            if row.start <= col.start:
                value = start_block(core, row, col, top, scale)
                x_own[row, col] = value
                if row.start < col.start and row.start // PANEL == col.start // PANEL:
                    x_own[col, row] = value.T
                store_matrix(value, state, row, col)
    high_cross[...] = high[left, right]
    low_cross[...] = low[left, right]
    for row in panels(0, rows):
        for col in panels(rows, order):
            at = shifted(col, -rows)
            off = three_passes(high[row, left], low[row, left], high[left, col], low[left, col])
            factor = spread_lanes(keep + add * diag_col[row, :], at.stop - at.start)
            y_cross[row, at] = x_cross[row, at] * factor + add * off
    for row in panels(rows, order):
        for col in panels(rows, order):
            if row.start <= col.start:
                passes = square_passes if row.start == col.start else three_passes
                off = passes(high[row, left], low[row, left], high[left, col], low[left, col])
                y_halo[shifted(row, -rows), shifted(col, -rows)] = add * off
    for row in panels(0, rows):
        for col in panels(0, rows):
            if row.start <= col.start:
                passes = square_passes if row.start == col.start else three_passes
                off = passes(high[row, :], low[row, :], high[:, col], low[:, col])
                value = combined(
                    x_own[row, col], off, keep, add, state, row, col, row.start == col.start
                )
                x_own[row, col] = value
                store_matrix(value, later, row, col)


def kernel(place, high_end, low_end, branches, request, deriv, *refs):
    block_count = 2 * NB
    (high_cross, low_cross, x_cross, y_cross, y_halo, x_own, high_own, low_own, own_col, own_row) = refs[:10]
    pieces = refs[10 : 10 + block_count]
    density_out, own_out, mail = refs[10 + block_count : 13 + block_count]
    (x_a, x_b, high_a, low_a, high_b, low_b, diag_row_a, diag_row_b, diag_col_a, diag_col_b) = refs[
        13 + block_count : 23 + block_count
    ]
    waiting, deriv_held, row_part, deriv_sems, out_sem = refs[23 + block_count :]
    order = x_a.shape[0]
    rows = x_own.shape[0]
    atoms = rows // ORB
    slot_rows = (order - rows) // block_count
    left, right = slice(0, rows), slice(rows, order)

    deriv_copies = [
        pltpu.make_async_copy(deriv.at[c], deriv_held.at[c], deriv_sems.at[c]) for c in range(3)
    ]
    for copy in deriv_copies:
        copy.start()
    state_a = (high_a, low_a, diag_row_a, diag_col_a)
    state_b = (high_b, low_b, diag_row_b, diag_col_b)

    top = high_end[0]
    scale = 1.0 / (high_end[0] - low_end[0])
    for block in range(block_count):
        x_b[block * slot_rows : (block + 1) * slot_rows, left] = pieces[block][...]
    asked_row, asked_col = asked_atoms(request, order - rows)
    live_row = (asked_row >= 0).astype(jnp.float32)
    live_col = (asked_col >= 0).astype(jnp.float32)
    for row in cut(order - rows):
        for col in cut(order - rows):
            if row.start <= col.start:
                value = start_block(x_b, row, col, top, scale)
                value = value * live_col[row, :] * live_row[:, col]
                down, across = shifted(row, rows), shifted(col, rows)
                x_b[down, across] = value
                if row.start < col.start and down.start // PANEL == across.start // PANEL:
                    x_b[across, down] = value.T
                store_matrix(value, state_b, row, col)
    x_a[left, left] = x_own[...]
    high_a[left, left] = high_own[...]
    low_a[left, left] = low_own[...]
    diag_col_a[left, :] = own_col[...]
    diag_row_a[:, left] = own_row[...]
    keep, add = step_factors(branches, 0)
    for row in panels(0, rows):
        for col in panels(rows, order):
            at = shifted(col, -rows)
            off = three_passes(high_cross[row, :], low_cross[row, :], high_b[left, at], low_b[left, at])
            value = y_cross[row, at] + x_cross[row, at] * (add * diag_row_b[0:1, at]) + add * off
            store_mirrored(value, x_a, state_a, row, col, False)
    for row in panels(rows, order):
        for col in panels(rows, order):
            if row.start <= col.start:
                down, across = shifted(row, -rows), shifted(col, -rows)
                passes = square_passes if row.start == col.start else three_passes
                off = passes(high_b[down, left], low_b[down, left], high_b[left, across], low_b[left, across])
                on_diag = row.start == col.start
                value = combined(x_b[row, col], off, keep, add, state_b, down, across, on_diag)
                value = value + y_halo[down, across]
                store_mirrored(value, x_a, state_a, row, col, on_diag)

    count = order // PANEL
    waiting[...] = jnp.zeros(waiting.shape, jnp.float32)

    def squaring(number, x_now, now, x_later, later):
        keep, add = step_factors(branches, number)
        high, low = now[:2]

        def place_of(panel, step):
            other = panel + step
            return panel_at(panel), panel_at(jnp.where(other >= count, other - count, other))

        def product(panel, step):
            row, col = place_of(panel, step)
            passes = square_passes if step == 0 else three_passes
            return passes(high[row, :], low[row, :], high[:, col], low[:, col])

        def finish(off, panel, step):
            row, col = place_of(panel, step)
            value = combined(x_now[row, col], off, keep, add, now, row, col, step == 0)
            store_mirrored(value, x_later, later, row, col, step == 0)

        last = count // 2

        def turn(panel, carry):
            finish(waiting[...], jnp.where(panel == 0, count - 1, panel - 1), last)
            for step in range(last):
                finish(product(panel, step), panel, step)
            waiting[...] = product(panel, last)
            return carry

        lax.fori_loop(0, count, turn, 0)
        finish(waiting[...], jnp.int32(count - 1), last)

    def two(pair, carry):
        squaring(2 * pair + 1, x_a, state_a, x_b, state_b)
        squaring(2 * pair + 2, x_b, state_b, x_a, state_a)
        return carry

    lax.fori_loop(0, (ITERS - 1) // 2, two, 0)
    x = x_a

    out_copy = pltpu.make_async_copy(x.at[left, :], density_out, out_sem)
    out_copy.start()

    chunk = 64
    line = lax.broadcasted_iota(jnp.int32, (8, order), 0)
    columns = jnp.zeros((8, order), jnp.float32)
    own_rows = jnp.zeros((8, rows), jnp.float32)
    ones = jnp.ones((8, SUB), jnp.bfloat16)
    for c in range(3):
        deriv_copies[c].wait()

        def strip(number, total, c=c):
            at = pl.ds(pl.multiple_of(number * chunk, chunk), chunk)
            weighted = x[at, :] * deriv_held[c, at, :]
            row_part[at, :] = sum(weighted[:, lane : lane + SUB] for lane in range(0, order, SUB))
            return total + jnp.sum(weighted.reshape(chunk // 8, 8, order), axis=0)

        total = lax.fori_loop(0, rows // chunk, strip, jnp.zeros((8, order), jnp.float32))
        columns = jnp.where(line == c, jnp.sum(total, axis=0, keepdims=True), columns)
        row_sums = sum(
            lax.dot_general(ones, part, (((1,), (1,)), ((), ())), preferred_element_type=jnp.float32)
            for part in thirds(row_part[...])
        )
        own_rows = jnp.where(line[:, :rows] == c, row_sums, own_rows)
    atom_ids = lax.broadcasted_iota(jnp.int32, (rows, atoms), 1)
    own_hot = (lax.broadcasted_iota(jnp.int32, (rows, atoms), 0) // ORB == atom_ids).astype(jnp.float32)
    own_out[...] = dot_one_hot(2.0 * (own_rows - columns[:, :rows]), own_hot.astype(jnp.bfloat16))
    letter = jnp.where(line[:, rows:] == 3, asked_row, -2.0 * columns[:, rows:])
    empty = jnp.where(lax.broadcasted_iota(jnp.int32, (4, SUB - slot_rows), 0) == 3, -1.0, 0.0)
    mail[...] = jnp.zeros(mail.shape, jnp.float32)
    for block in range(block_count):
        content = letter[0:4, block * slot_rows : (block + 1) * slot_rows]
        to = lax.rem(place[0] + (block_offset(block) + mail.shape[0]), mail.shape[0])
        mail[to] = jnp.concatenate([content, empty], axis=1)
    out_copy.wait()


def collect(place, mail, own, forces):
    count = mail.shape[0]
    atoms = own.shape[1]
    letters = jnp.concatenate(
        [mail[lax.rem(place[0] + (count - block_offset(block)), count)] for block in range(2 * NB)],
        axis=1,
    )
    wanted = letters[3:4, :] == lax.broadcasted_iota(jnp.int32, (atoms, 1), 0).astype(jnp.float32)
    wanted = wanted.astype(jnp.float32).astype(jnp.bfloat16)
    sums = sum(
        lax.dot_general(part, wanted, (((1,), (1,)), ((), ())), preferred_element_type=jnp.float32)
        for part in thirds(jnp.concatenate([letters, letters], axis=0))
    )
    forces[...] = own[0:3, :] + sums[0:3, :]


def own_part(high_end, low_end, branches, core, request):
    rows, order = core.shape
    halo = order - rows
    vmem = pl.BlockSpec(memory_space=pltpu.VMEM)
    smem = pl.BlockSpec(memory_space=pltpu.SMEM)
    kinds = [
        ((rows, halo), jnp.bfloat16),
        ((rows, halo), jnp.bfloat16),
        ((rows, halo), jnp.float32),
        ((rows, halo), jnp.float32),
        ((halo, halo), jnp.float32),
        ((rows, rows), jnp.float32),
        ((rows, rows), jnp.bfloat16),
        ((rows, rows), jnp.bfloat16),
        ((rows, SUB), jnp.float32),
        ((8, rows), jnp.float32),
    ]
    return pl.pallas_call(
        own_kernel,
        out_shape=[jax.ShapeDtypeStruct(*kind) for kind in kinds],
        in_specs=[smem, smem, smem, vmem, vmem],
        out_specs=[vmem] * len(kinds),
        scratch_shapes=[
            pltpu.VMEM((order, order), jnp.bfloat16),
            pltpu.VMEM((order, order), jnp.bfloat16),
            pltpu.VMEM((8, order), jnp.float32),
            pltpu.VMEM((order, SUB), jnp.float32),
        ],
        compiler_params=pltpu.CompilerParams(vmem_limit_bytes=OWN_VMEM_BYTES),
        cost_estimate=pl.CostEstimate(
            flops=2 * 3 * order**3 // 3, bytes_accessed=13_000_000, transcendentals=0
        ),
    )(high_end, low_end, branches, core, request)


def density_and_terms(place, high_end, low_end, branches, request, deriv, ready, pieces):
    rows, order = deriv.shape[1:]
    atoms = rows // ORB
    vmem = pl.BlockSpec(memory_space=pltpu.VMEM)
    smem = pl.BlockSpec(memory_space=pltpu.SMEM)
    anywhere = pl.BlockSpec(memory_space=pl.ANY)
    square = (order, order)
    return pl.pallas_call(
        kernel,
        out_shape=[
            jax.ShapeDtypeStruct((rows, order), jnp.float32),
            jax.ShapeDtypeStruct((8, atoms), jnp.float32),
            jax.ShapeDtypeStruct((lax.axis_size("dom"), 4, SUB), jnp.float32),
        ],
        in_specs=[smem, smem, smem, smem, vmem, anywhere] + [vmem] * (len(ready) + len(pieces)),
        out_specs=[anywhere, vmem, vmem],
        scratch_shapes=[
            pltpu.VMEM(square, jnp.float32),
            pltpu.VMEM(square, jnp.float32),
            pltpu.VMEM(square, jnp.bfloat16),
            pltpu.VMEM(square, jnp.bfloat16),
            pltpu.VMEM(square, jnp.bfloat16),
            pltpu.VMEM(square, jnp.bfloat16),
            pltpu.VMEM((8, order), jnp.float32),
            pltpu.VMEM((8, order), jnp.float32),
            pltpu.VMEM((order, SUB), jnp.float32),
            pltpu.VMEM((order, SUB), jnp.float32),
            pltpu.VMEM((PANEL, PANEL), jnp.float32),
            pltpu.VMEM((3, rows, order), jnp.float32),
            pltpu.VMEM((rows, SUB), jnp.float32),
            pltpu.SemaphoreType.DMA((3,)),
            pltpu.SemaphoreType.DMA,
        ],
        compiler_params=pltpu.CompilerParams(vmem_limit_bytes=VMEM_BYTES),
        cost_estimate=pl.CostEstimate(
            flops=2 * 3 * 3 * order**3, bytes_accessed=24_000_000, transcendentals=0
        ),
    )(place, high_end, low_end, branches, request, deriv, *ready, *pieces)


def per_device(ham_core, halo_rows, halo_request, deriv, e_low, e_high, branches):
    row_count, order_all = ham_core.shape
    block_count = 2 * NB
    halo = halo_rows[0, :, :, row_count:]
    flat_deriv = deriv.reshape(3, row_count, order_all)
    early = (1, 2, 3, 5, 6)
    late = (0, 4, 7)
    pieces = {block: passed_along(halo[block], "dom", -block_offset(block)) for block in early}
    waiting, flat_deriv = lax.optimization_barrier(([halo[block] for block in late], flat_deriv))
    for block, piece in zip(late, waiting):
        pieces[block] = passed_along(piece, "dom", -block_offset(block))
    place = lax.axis_index("dom")[None].astype(jnp.int32)
    ready = own_part(e_high, e_low, branches, ham_core, halo_request)
    density, own, mail = density_and_terms(
        place,
        e_high,
        e_low,
        branches,
        halo_request,
        flat_deriv,
        ready,
        [pieces[block] for block in range(block_count)],
    )
    arrived = lax.all_to_all(mail, "dom", 0, 0, tiled=True)
    forces = pl.pallas_call(
        collect,
        out_shape=jax.ShapeDtypeStruct((3, own.shape[1]), jnp.float32),
        in_specs=[
            pl.BlockSpec(memory_space=pltpu.SMEM),
            pl.BlockSpec(memory_space=pltpu.VMEM),
            pl.BlockSpec(memory_space=pltpu.VMEM),
        ],
        out_specs=pl.BlockSpec(memory_space=pltpu.VMEM),
    )(place, arrived, own)
    return (density, forces)


def solution(mesh):
    in_specs = (
        P("dom", None),
        P("dom", None, None, None),
        P("dom", None),
        P(None, "dom", None, None),
        P(),
        P(),
        P(),
    )
    out_specs = (P("dom", None), P(None, "dom"))
    return jax.shard_map(
        per_device, mesh=mesh, in_specs=in_specs, out_specs=out_specs, check_vma=False
    )
```

```python
import functools

import jax
import jax.numpy as jnp
from jax import lax
from jax.experimental import pallas as pl
from jax.experimental.pallas import tpu as pltpu
from jax.sharding import PartitionSpec as P

ORB = 4
NB = 4
ITERS = 5
PANEL = 256
SUB = 128
VMEM_BYTES = 38 * 1024 * 1024
OWN_VMEM_BYTES = 16 * 1024 * 1024


def passed_along(value, axis, steps):
    count = lax.axis_size(axis)
    pairs = [(source, (source + steps) % count) for source in range(count)]
    return lax.ppermute(value, axis, pairs)


def block_offset(block):
    if block < NB:
        return block + 1
    return NB - 1 - block


def halves(value):
    high = value.astype(jnp.bfloat16)
    low = (value - high.astype(jnp.float32)).astype(jnp.bfloat16)
    return high, low


def thirds(value):
    high = value.astype(jnp.bfloat16)
    rest = value - high.astype(jnp.float32)
    middle, low = halves(rest)
    return high, middle, low


def dot(left, right):
    return jnp.dot(left, right, preferred_element_type=jnp.float32)


def dot_one_hot(value, one_hot):
    return sum(dot(part, one_hot) for part in thirds(value))


def on_diagonal(shape):
    return lax.broadcasted_iota(jnp.int32, shape, 0) == lax.broadcasted_iota(jnp.int32, shape, 1)


def three_passes(left_high, left_low, right_high, right_low):
    return dot(
        jnp.concatenate([left_high, left_high, left_low], axis=1),
        jnp.concatenate([right_high, right_low, right_high], axis=0),
    )


def square_passes(left_high, left_low, right_high, right_low):
    cross = dot(left_high, right_low)
    return dot(left_high, right_high) + (cross + cross.T)


def step_factors(branches, number):
    taken = (branches[number] == 1).astype(jnp.float32)
    return 2.0 * taken, 1.0 - 2.0 * taken


def panels(start, end):
    cuts = [start] + [at for at in range(0, end, PANEL) if at > start] + [end]
    return [slice(low, high) for low, high in zip(cuts, cuts[1:])]


def spread_lanes(column, width):
    return jnp.concatenate([column] * (width // SUB), axis=1)


def combined(old, off, keep, add, state, rows_at, cols_at, on_diag):
    diag_row, diag_col = state[2:]
    factor_col = spread_lanes(keep + add * diag_col[rows_at, :], old.shape[1])
    value = old * (factor_col + add * diag_row[0:1, cols_at]) + add * off
    if on_diag:
        value = value - jnp.where(on_diagonal(value.shape), add * (old * old), 0.0)
    return value


def store_matrix(value, state, rows_at, cols_at):
    high_ref, low_ref, diag_row, diag_col = state
    if rows_at.start == cols_at.start:
        size = value.shape[0]
        line = jnp.where(on_diagonal(value.shape), value, 0.0)
        diag_row[:, cols_at] = jnp.broadcast_to(jnp.sum(line, axis=0, keepdims=True), (8, size))
        diag_col[rows_at, :] = jnp.broadcast_to(jnp.sum(line, axis=1, keepdims=True), (size, SUB))
        value = value - line
    high, low = halves(value)
    high_ref[rows_at, cols_at] = high
    low_ref[rows_at, cols_at] = low
    if rows_at.start != cols_at.start:
        high_ref[cols_at, rows_at] = high.T
        low_ref[cols_at, rows_at] = low.T


def start_block(source, row, col, top, scale):
    value = 0.5 * (source[row, col] + source[col, row].T)
    if row.start == col.start:
        value = value - jnp.where(on_diagonal(value.shape), top, 0.0)
    return -scale * value


def cut(size):
    return [slice(at, at + SUB) for at in range(0, size, SUB)]


def shifted(piece, by):
    return slice(piece.start + by, piece.stop + by)


def asked_atoms(request, orbitals):
    atoms = request.shape[1]
    expand = lax.broadcasted_iota(jnp.int32, (orbitals, atoms), 0) // ORB == lax.broadcasted_iota(
        jnp.int32, (orbitals, atoms), 1
    )
    expand = expand.astype(jnp.float32).astype(jnp.bfloat16)
    values = jnp.broadcast_to(request[...].astype(jnp.float32), (8, atoms)).astype(jnp.bfloat16)
    transposed = (((1,), (1,)), ((), ()))
    row = lax.dot_general(values, expand, transposed, preferred_element_type=jnp.float32)
    col = lax.dot_general(expand, values, transposed, preferred_element_type=jnp.float32)
    return row[0:1, :], col[:, 0:1]


def own_kernel(
    high_end, low_end, branches, core, request, high_cross, low_cross, x_cross, y_cross, y_halo,
    x_own, next_high, next_low, next_col, next_row, high, low, diag_row, diag_col
):
    rows, order = core.shape
    state = (high, low, diag_row, diag_col)
    later = (next_high, next_low, next_row, next_col)
    left, right = slice(0, rows), slice(rows, order)
    top = high_end[0]
    scale = 1.0 / (high_end[0] - low_end[0])
    keep, add = step_factors(branches, 0)
    asked_row, _ = asked_atoms(request, order - rows)
    live_row = (asked_row >= 0).astype(jnp.float32)
    for row in cut(rows):
        for col in cut(order - rows):
            value = -scale * (core[row, shifted(col, rows)] * live_row[:, col])
            x_cross[row, col] = value
            store_matrix(value, state, row, shifted(col, rows))
    for row in cut(rows):
        for col in cut(rows):
            if row.start <= col.start:
                value = start_block(core, row, col, top, scale)
                x_own[row, col] = value
                if row.start < col.start and row.start // PANEL == col.start // PANEL:
                    x_own[col, row] = value.T
                store_matrix(value, state, row, col)
    high_cross[...] = high[left, right]
    low_cross[...] = low[left, right]
    for row in panels(0, rows):
        for col in panels(rows, order):
            at = shifted(col, -rows)
            off = three_passes(high[row, left], low[row, left], high[left, col], low[left, col])
            factor = spread_lanes(keep + add * diag_col[row, :], at.stop - at.start)
            y_cross[row, at] = x_cross[row, at] * factor + add * off
    for row in panels(rows, order):
        for col in panels(rows, order):
            if row.start <= col.start:
                passes = square_passes if row.start == col.start else three_passes
                off = passes(high[row, left], low[row, left], high[left, col], low[left, col])
                y_halo[shifted(row, -rows), shifted(col, -rows)] = add * off
    for row in panels(0, rows):
        for col in panels(0, rows):
            if row.start <= col.start:
                passes = square_passes if row.start == col.start else three_passes
                off = passes(high[row, :], low[row, :], high[:, col], low[:, col])
                value = combined(
                    x_own[row, col], off, keep, add, state, row, col, row.start == col.start
                )
                x_own[row, col] = value
                store_matrix(value, later, row, col)


def kernel(place, high_end, low_end, branches, request, *refs):
    deriv, refs = refs[:3], refs[3:]
    block_count = 2 * NB
    (high_cross, low_cross, x_cross, y_cross, y_halo, x_own, high_own, low_own, own_col, own_row) = refs[:10]
    pieces = refs[10 : 10 + block_count]
    density_out, own_out, mail = refs[10 + block_count : 13 + block_count]
    (x, high_a, low_a, high_b, low_b, diag_row_a, diag_row_b, diag_col_a, diag_col_b) = refs[
        13 + block_count : 22 + block_count
    ]
    halo, deriv_held, row_part, deriv_sems, out_sem = refs[22 + block_count :]
    order = x.shape[0]
    rows = x_own.shape[0]
    atoms = rows // ORB
    slot_rows = (order - rows) // block_count
    left, right = slice(0, rows), slice(rows, order)

    deriv_copies = [
        pltpu.make_async_copy(deriv[c], deriv_held.at[c], deriv_sems.at[c]) for c in range(3)
    ]
    for copy in deriv_copies:
        copy.start()
    state_a = (high_a, low_a, diag_row_a, diag_col_a)
    state_b = (high_b, low_b, diag_row_b, diag_col_b)

    top = high_end[0]
    scale = 1.0 / (high_end[0] - low_end[0])
    for block in range(block_count):
        halo[block * slot_rows : (block + 1) * slot_rows, :] = pieces[block][...]
    asked_row, asked_col = asked_atoms(request, order - rows)
    live_row = (asked_row >= 0).astype(jnp.float32)
    live_col = (asked_col >= 0).astype(jnp.float32)
    for row in cut(order - rows):
        for col in cut(order - rows):
            if row.start <= col.start:
                value = start_block(halo, row, col, top, scale)
                value = value * live_col[row, :] * live_row[:, col]
                down, across = shifted(row, rows), shifted(col, rows)
                x[down, across] = value
                if row.start < col.start and down.start // PANEL == across.start // PANEL:
                    x[across, down] = value.T
                store_matrix(value, state_b, row, col)
    x[left, left] = x_own[...]
    high_a[left, left] = high_own[...]
    low_a[left, left] = low_own[...]
    diag_col_a[left, :] = own_col[...]
    diag_row_a[:, left] = own_row[...]
    keep, add = step_factors(branches, 0)
    for row in panels(0, rows):
        for col in panels(rows, order):
            at = shifted(col, -rows)
            off = three_passes(high_cross[row, :], low_cross[row, :], high_b[left, at], low_b[left, at])
            value = y_cross[row, at] + x_cross[row, at] * (add * diag_row_b[0:1, at]) + add * off
            x[row, col] = value
            if row.start // PANEL == col.start // PANEL:
                x[col, row] = value.T
            store_matrix(value, state_a, row, col)
    for row in panels(rows, order):
        for col in panels(rows, order):
            if row.start <= col.start:
                down, across = shifted(row, -rows), shifted(col, -rows)
                passes = square_passes if row.start == col.start else three_passes
                off = passes(high_b[down, left], low_b[down, left], high_b[left, across], low_b[left, across])
                on_diag = row.start == col.start
                value = combined(x[row, col], off, keep, add, state_b, down, across, on_diag)
                value = value + y_halo[down, across]
                x[row, col] = value
                store_matrix(value, state_a, row, col)

    def block_step(number, now, later, lines, cols):
        keep, add = step_factors(branches, number)
        high, low = now[:2]
        on_diag = lines.start == cols.start
        passes = square_passes if on_diag else three_passes
        off = passes(high[lines, :], low[lines, :], high[:, cols], low[:, cols])
        value = combined(x[lines, cols], off, keep, add, now, lines, cols, on_diag)
        x[lines, cols] = value
        store_matrix(value, later, lines, cols)

    def squaring(number, now, later, unless_last):
        away = []
        for cols in panels(0, order):
            for lines in panels(0, cols.stop):
                if lines.start >= rows:
                    away.append((lines, cols))
                else:
                    block_step(number, now, later, lines, cols)

        def others():
            for lines, cols in away:
                block_step(number, now, later, lines, cols)

        if unless_last:
            pl.when(number < ITERS - 1)(others)
        else:
            others()

    def two(pair, carry):
        squaring(2 * pair + 1, state_a, state_b, False)
        squaring(2 * pair + 2, state_b, state_a, True)
        return carry

    lax.fori_loop(0, (ITERS - 1) // 2, two, 0)
    for cols in panels(0, rows):
        for lines in panels(0, cols.start) if cols.start > 0 else []:
            x[cols, lines] = x[lines, cols].T

    out_copy = pltpu.make_async_copy(x.at[left, :], density_out, out_sem)
    out_copy.start()

    chunk = 64
    line = lax.broadcasted_iota(jnp.int32, (8, order), 0)
    columns = jnp.zeros((8, order), jnp.float32)
    own_rows = jnp.zeros((8, rows), jnp.float32)
    ones = jnp.ones((8, SUB), jnp.bfloat16)
    for c in range(3):
        deriv_copies[c].wait()

        def strip(number, total, c=c):
            at = pl.ds(pl.multiple_of(number * chunk, chunk), chunk)
            weighted = x[at, :] * deriv_held[c, at, :]
            row_part[at, :] = sum(weighted[:, lane : lane + SUB] for lane in range(0, order, SUB))
            return total + jnp.sum(weighted.reshape(chunk // 8, 8, order), axis=0)

        total = lax.fori_loop(0, rows // chunk, strip, jnp.zeros((8, order), jnp.float32))
        columns = jnp.where(line == c, jnp.sum(total, axis=0, keepdims=True), columns)
        row_sums = sum(
            lax.dot_general(ones, part, (((1,), (1,)), ((), ())), preferred_element_type=jnp.float32)
            for part in thirds(row_part[...])
        )
        own_rows = jnp.where(line[:, :rows] == c, row_sums, own_rows)
    atom_ids = lax.broadcasted_iota(jnp.int32, (rows, atoms), 1)
    own_hot = (lax.broadcasted_iota(jnp.int32, (rows, atoms), 0) // ORB == atom_ids).astype(jnp.float32)
    own_out[...] = dot_one_hot(2.0 * (own_rows - columns[:, :rows]), own_hot.astype(jnp.bfloat16))
    letter = jnp.where(line[:, rows:] == 3, asked_row, -2.0 * columns[:, rows:])
    empty = jnp.where(lax.broadcasted_iota(jnp.int32, (4, SUB - slot_rows), 0) == 3, -1.0, 0.0)
    mail[...] = jnp.zeros(mail.shape, jnp.float32)
    for block in range(block_count):
        content = letter[0:4, block * slot_rows : (block + 1) * slot_rows]
        to = lax.rem(place[0] + (block_offset(block) + mail.shape[0]), mail.shape[0])
        mail[to] = jnp.concatenate([content, empty], axis=1)
    out_copy.wait()


def collect(place, mail, own, forces):
    count = mail.shape[0]
    atoms = own.shape[1]
    letters = jnp.concatenate(
        [mail[lax.rem(place[0] + (count - block_offset(block)), count)] for block in range(2 * NB)],
        axis=1,
    )
    wanted = letters[3:4, :] == lax.broadcasted_iota(jnp.int32, (atoms, 1), 0).astype(jnp.float32)
    wanted = wanted.astype(jnp.float32).astype(jnp.bfloat16)
    sums = sum(
        lax.dot_general(part, wanted, (((1,), (1,)), ((), ())), preferred_element_type=jnp.float32)
        for part in thirds(jnp.concatenate([letters, letters], axis=0))
    )
    forces[...] = own[0:3, :] + sums[0:3, :]


def own_part(high_end, low_end, branches, core, request):
    rows, order = core.shape
    halo = order - rows
    vmem = pl.BlockSpec(memory_space=pltpu.VMEM)
    smem = pl.BlockSpec(memory_space=pltpu.SMEM)
    kinds = [
        ((rows, halo), jnp.bfloat16),
        ((rows, halo), jnp.bfloat16),
        ((rows, halo), jnp.float32),
        ((rows, halo), jnp.float32),
        ((halo, halo), jnp.float32),
        ((rows, rows), jnp.float32),
        ((rows, rows), jnp.bfloat16),
        ((rows, rows), jnp.bfloat16),
        ((rows, SUB), jnp.float32),
        ((8, rows), jnp.float32),
    ]
    return pl.pallas_call(
        own_kernel,
        out_shape=[jax.ShapeDtypeStruct(*kind) for kind in kinds],
        in_specs=[smem, smem, smem, vmem, vmem],
        out_specs=[vmem] * len(kinds),
        scratch_shapes=[
            pltpu.VMEM((order, order), jnp.bfloat16),
            pltpu.VMEM((order, order), jnp.bfloat16),
            pltpu.VMEM((8, order), jnp.float32),
            pltpu.VMEM((order, SUB), jnp.float32),
        ],
        compiler_params=pltpu.CompilerParams(vmem_limit_bytes=OWN_VMEM_BYTES),
        cost_estimate=pl.CostEstimate(
            flops=2 * 3 * order**3 // 3, bytes_accessed=13_000_000, transcendentals=0
        ),
    )(high_end, low_end, branches, core, request)


def density_and_terms(place, high_end, low_end, branches, request, deriv, ready, pieces):
    rows, order = deriv[0].shape
    atoms = rows // ORB
    vmem = pl.BlockSpec(memory_space=pltpu.VMEM)
    smem = pl.BlockSpec(memory_space=pltpu.SMEM)
    anywhere = pl.BlockSpec(memory_space=pl.ANY)
    square = (order, order)
    return pl.pallas_call(
        kernel,
        out_shape=[
            jax.ShapeDtypeStruct((rows, order), jnp.float32),
            jax.ShapeDtypeStruct((8, atoms), jnp.float32),
            jax.ShapeDtypeStruct((lax.axis_size("dom"), 4, SUB), jnp.float32),
        ],
        in_specs=[smem, smem, smem, smem, vmem] + [anywhere] * 3 + [vmem] * (len(ready) + len(pieces)),
        out_specs=[anywhere, vmem, vmem],
        scratch_shapes=[
            pltpu.VMEM(square, jnp.float32),
            pltpu.VMEM(square, jnp.bfloat16),
            pltpu.VMEM(square, jnp.bfloat16),
            pltpu.VMEM(square, jnp.bfloat16),
            pltpu.VMEM(square, jnp.bfloat16),
            pltpu.VMEM((8, order), jnp.float32),
            pltpu.VMEM((8, order), jnp.float32),
            pltpu.VMEM((order, SUB), jnp.float32),
            pltpu.VMEM((order, SUB), jnp.float32),
            pltpu.VMEM((order - rows, order - rows), jnp.float32),
            pltpu.VMEM((3, rows, order), jnp.float32),
            pltpu.VMEM((rows, SUB), jnp.float32),
            pltpu.SemaphoreType.DMA((3,)),
            pltpu.SemaphoreType.DMA,
        ],
        compiler_params=pltpu.CompilerParams(vmem_limit_bytes=VMEM_BYTES),
        cost_estimate=pl.CostEstimate(
            flops=2 * 3 * 3 * order**3, bytes_accessed=24_000_000, transcendentals=0
        ),
    )(place, high_end, low_end, branches, request, *deriv, *ready, *pieces)


def per_device(ham_core, halo_rows, halo_request, deriv, e_low, e_high, branches):
    row_count, order_all = ham_core.shape
    block_count = 2 * NB
    early = (6, 3, 2, 1, 5)
    late = (0, 4, 7)
    first = halo_rows[0, early[0], :, row_count:]
    pieces = {early[0]: passed_along(first, "dom", -block_offset(early[0]))}
    rest, _ = lax.optimization_barrier((halo_rows, first))
    halo = rest[0, :, :, row_count:]
    for block in early[1:]:
        pieces[block] = passed_along(halo[block], "dom", -block_offset(block))
    ready = own_part(e_high, e_low, branches, ham_core, halo_request)
    flat_deriv = [deriv[c].reshape(row_count, order_all) for c in range(3)]
    waiting, ready, flat_deriv[0] = lax.optimization_barrier(
        ([halo[block] for block in late], ready, flat_deriv[0])
    )
    for block, piece in zip(late, waiting):
        pieces[block] = passed_along(piece, "dom", -block_offset(block))
    place = lax.axis_index("dom")[None].astype(jnp.int32)
    density, own, mail = density_and_terms(
        place,
        e_high,
        e_low,
        branches,
        halo_request,
        flat_deriv,
        ready,
        [pieces[block] for block in range(block_count)],
    )
    arrived = lax.all_to_all(mail, "dom", 0, 0, tiled=True)
    forces = pl.pallas_call(
        collect,
        out_shape=jax.ShapeDtypeStruct((3, own.shape[1]), jnp.float32),
        in_specs=[
            pl.BlockSpec(memory_space=pltpu.SMEM),
            pl.BlockSpec(memory_space=pltpu.VMEM),
            pl.BlockSpec(memory_space=pltpu.VMEM),
        ],
        out_specs=pl.BlockSpec(memory_space=pltpu.VMEM),
    )(place, arrived, own)
    return (density, forces)


def solution(mesh):
    in_specs = (
        P("dom", None),
        P("dom", None, None, None),
        P("dom", None),
        P(None, "dom", None, None),
        P(),
        P(),
        P(),
    )
    out_specs = (P("dom", None), P(None, "dom"))
    return jax.shard_map(
        per_device, mesh=mesh, in_specs=in_specs, out_specs=out_specs, check_vma=False
    )
```

```python
import functools

import jax
import jax.numpy as jnp
from jax import lax
from jax.experimental import pallas as pl
from jax.experimental.pallas import tpu as pltpu
from jax.sharding import PartitionSpec as P

ORB = 4
NB = 4
ITERS = 5
PANEL = 256
SUB = 128
VMEM_BYTES = 38 * 1024 * 1024
OWN_VMEM_BYTES = 16 * 1024 * 1024


def passed_along(value, axis, steps):
    count = lax.axis_size(axis)
    pairs = [(source, (source + steps) % count) for source in range(count)]
    return lax.ppermute(value, axis, pairs)


def block_offset(block):
    if block < NB:
        return block + 1
    return NB - 1 - block


def halves(value):
    high = value.astype(jnp.bfloat16)
    low = (value - high.astype(jnp.float32)).astype(jnp.bfloat16)
    return high, low


def thirds(value):
    high = value.astype(jnp.bfloat16)
    rest = value - high.astype(jnp.float32)
    middle, low = halves(rest)
    return high, middle, low


def dot(left, right):
    return jnp.dot(left, right, preferred_element_type=jnp.float32)


def dot_one_hot(value, one_hot):
    return sum(dot(part, one_hot) for part in thirds(value))


def on_diagonal(shape):
    return lax.broadcasted_iota(jnp.int32, shape, 0) == lax.broadcasted_iota(jnp.int32, shape, 1)


def three_passes(left_high, left_low, right_high, right_low):
    return dot(
        jnp.concatenate([left_high, left_high, left_low], axis=1),
        jnp.concatenate([right_high, right_low, right_high], axis=0),
    )


def square_passes(left_high, left_low, right_high, right_low):
    cross = dot(left_high, right_low)
    return dot(left_high, right_high) + (cross + cross.T)


def step_factors(branches, number):
    taken = (branches[number] == 1).astype(jnp.float32)
    return 2.0 * taken, 1.0 - 2.0 * taken


def panels(start, end):
    cuts = [start] + [at for at in range(0, end, PANEL) if at > start] + [end]
    return [slice(low, high) for low, high in zip(cuts, cuts[1:])]


def spread_lanes(column, width):
    return jnp.concatenate([column] * (width // SUB), axis=1)


def combined(old, off, keep, add, state, rows_at, cols_at, on_diag):
    diag_row, diag_col = state[2:]
    factor_col = spread_lanes(keep + add * diag_col[rows_at, :], old.shape[1])
    value = old * (factor_col + add * diag_row[0:1, cols_at]) + add * off
    if on_diag:
        value = value - jnp.where(on_diagonal(value.shape), add * (old * old), 0.0)
    return value


def store_matrix(value, state, rows_at, cols_at):
    high_ref, low_ref, diag_row, diag_col = state
    if rows_at.start == cols_at.start:
        size = value.shape[0]
        line = jnp.where(on_diagonal(value.shape), value, 0.0)
        diag_row[:, cols_at] = jnp.broadcast_to(jnp.sum(line, axis=0, keepdims=True), (8, size))
        diag_col[rows_at, :] = jnp.broadcast_to(jnp.sum(line, axis=1, keepdims=True), (size, SUB))
        value = value - line
    high, low = halves(value)
    high_ref[rows_at, cols_at] = high
    low_ref[rows_at, cols_at] = low
    if rows_at.start != cols_at.start:
        high_ref[cols_at, rows_at] = high.T
        low_ref[cols_at, rows_at] = low.T


def start_block(source, row, col, top, scale):
    value = 0.5 * (source[row, col] + source[col, row].T)
    if row.start == col.start:
        value = value - jnp.where(on_diagonal(value.shape), top, 0.0)
    return -scale * value


def cut(size):
    return [slice(at, at + SUB) for at in range(0, size, SUB)]


def shifted(piece, by):
    return slice(piece.start + by, piece.stop + by)


def asked_atoms(request, orbitals):
    atoms = request.shape[1]
    expand = lax.broadcasted_iota(jnp.int32, (orbitals, atoms), 0) // ORB == lax.broadcasted_iota(
        jnp.int32, (orbitals, atoms), 1
    )
    expand = expand.astype(jnp.float32).astype(jnp.bfloat16)
    values = jnp.broadcast_to(request[...].astype(jnp.float32), (8, atoms)).astype(jnp.bfloat16)
    transposed = (((1,), (1,)), ((), ()))
    row = lax.dot_general(values, expand, transposed, preferred_element_type=jnp.float32)
    col = lax.dot_general(expand, values, transposed, preferred_element_type=jnp.float32)
    return row[0:1, :], col[:, 0:1]


def own_kernel(
    high_end, low_end, branches, core, request, high_cross, low_cross, x_cross, y_cross, y_halo,
    x_own, next_high, next_low, next_col, next_row, high, low, diag_row, diag_col
):
    rows, order = core.shape
    state = (high, low, diag_row, diag_col)
    later = (next_high, next_low, next_row, next_col)
    left, right = slice(0, rows), slice(rows, order)
    top = high_end[0]
    scale = 1.0 / (high_end[0] - low_end[0])
    keep, add = step_factors(branches, 0)
    asked_row, _ = asked_atoms(request, order - rows)
    live_row = (asked_row >= 0).astype(jnp.float32)
    for row in cut(rows):
        for col in cut(order - rows):
            value = -scale * (core[row, shifted(col, rows)] * live_row[:, col])
            x_cross[row, col] = value
            store_matrix(value, state, row, shifted(col, rows))
    for row in cut(rows):
        for col in cut(rows):
            if row.start <= col.start:
                value = start_block(core, row, col, top, scale)
                x_own[row, col] = value
                if row.start < col.start and row.start // PANEL == col.start // PANEL:
                    x_own[col, row] = value.T
                store_matrix(value, state, row, col)
    high_cross[...] = high[left, right]
    low_cross[...] = low[left, right]
    for row in panels(0, rows):
        for col in panels(rows, order):
            at = shifted(col, -rows)
            off = three_passes(high[row, left], low[row, left], high[left, col], low[left, col])
            factor = spread_lanes(keep + add * diag_col[row, :], at.stop - at.start)
            y_cross[row, at] = x_cross[row, at] * factor + add * off
    for row in panels(rows, order):
        for col in panels(rows, order):
            if row.start <= col.start:
                passes = square_passes if row.start == col.start else three_passes
                off = passes(high[row, left], low[row, left], high[left, col], low[left, col])
                y_halo[shifted(row, -rows), shifted(col, -rows)] = add * off
    for row in panels(0, rows):
        for col in panels(0, rows):
            if row.start <= col.start:
                passes = square_passes if row.start == col.start else three_passes
                off = passes(high[row, :], low[row, :], high[:, col], low[:, col])
                value = combined(
                    x_own[row, col], off, keep, add, state, row, col, row.start == col.start
                )
                x_own[row, col] = value
                store_matrix(value, later, row, col)


def kernel(place, high_end, low_end, branches, request, deriv, *refs):
    block_count = 2 * NB
    (high_cross, low_cross, x_cross, y_cross, y_halo, x_own, high_own, low_own, own_col, own_row) = refs[:10]
    pieces = refs[10 : 10 + block_count]
    density_out, own_out, mail = refs[10 + block_count : 13 + block_count]
    (x, high_a, low_a, high_b, low_b, diag_row_a, diag_row_b, diag_col_a, diag_col_b) = refs[
        13 + block_count : 22 + block_count
    ]
    halo, deriv_held, row_part, deriv_sems, out_sem = refs[22 + block_count :]
    order = x.shape[0]
    rows = x_own.shape[0]
    atoms = rows // ORB
    slot_rows = (order - rows) // block_count
    left, right = slice(0, rows), slice(rows, order)

    deriv_copies = [
        pltpu.make_async_copy(deriv.at[c], deriv_held.at[c], deriv_sems.at[c]) for c in range(3)
    ]
    for copy in deriv_copies:
        copy.start()
    state_a = (high_a, low_a, diag_row_a, diag_col_a)
    state_b = (high_b, low_b, diag_row_b, diag_col_b)

    top = high_end[0]
    scale = 1.0 / (high_end[0] - low_end[0])
    for block in range(block_count):
        halo[block * slot_rows : (block + 1) * slot_rows, :] = pieces[block][...]
    asked_row, asked_col = asked_atoms(request, order - rows)
    live_row = (asked_row >= 0).astype(jnp.float32)
    live_col = (asked_col >= 0).astype(jnp.float32)
    for row in cut(order - rows):
        for col in cut(order - rows):
            if row.start <= col.start:
                value = start_block(halo, row, col, top, scale)
                value = value * live_col[row, :] * live_row[:, col]
                down, across = shifted(row, rows), shifted(col, rows)
                x[down, across] = value
                if row.start < col.start and down.start // PANEL == across.start // PANEL:
                    x[across, down] = value.T
                store_matrix(value, state_b, row, col)
    x[left, left] = x_own[...]
    high_a[left, left] = high_own[...]
    low_a[left, left] = low_own[...]
    diag_col_a[left, :] = own_col[...]
    diag_row_a[:, left] = own_row[...]
    keep, add = step_factors(branches, 0)
    for row in panels(0, rows):
        for col in panels(rows, order):
            at = shifted(col, -rows)
            off = three_passes(high_cross[row, :], low_cross[row, :], high_b[left, at], low_b[left, at])
            value = y_cross[row, at] + x_cross[row, at] * (add * diag_row_b[0:1, at]) + add * off
            x[row, col] = value
            if row.start // PANEL == col.start // PANEL:
                x[col, row] = value.T
            store_matrix(value, state_a, row, col)
    for row in panels(rows, order):
        for col in panels(rows, order):
            if row.start <= col.start:
                down, across = shifted(row, -rows), shifted(col, -rows)
                passes = square_passes if row.start == col.start else three_passes
                off = passes(high_b[down, left], low_b[down, left], high_b[left, across], low_b[left, across])
                on_diag = row.start == col.start
                value = combined(x[row, col], off, keep, add, state_b, down, across, on_diag)
                value = value + y_halo[down, across]
                x[row, col] = value
                store_matrix(value, state_a, row, col)

    def block_step(number, now, later, lines, cols):
        keep, add = step_factors(branches, number)
        high, low = now[:2]
        on_diag = lines.start == cols.start
        passes = square_passes if on_diag else three_passes
        off = passes(high[lines, :], low[lines, :], high[:, cols], low[:, cols])
        value = combined(x[lines, cols], off, keep, add, now, lines, cols, on_diag)
        x[lines, cols] = value
        store_matrix(value, later, lines, cols)

    def squaring(number, now, later, unless_last):
        away = []
        for cols in panels(0, order):
            for lines in panels(0, cols.stop):
                if lines.start >= rows:
                    away.append((lines, cols))
                else:
                    block_step(number, now, later, lines, cols)

        def others():
            for lines, cols in away:
                block_step(number, now, later, lines, cols)

        if unless_last:
            pl.when(number < ITERS - 1)(others)
        else:
            others()

    def two(pair, carry):
        squaring(2 * pair + 1, state_a, state_b, False)
        squaring(2 * pair + 2, state_b, state_a, True)
        return carry

    lax.fori_loop(0, (ITERS - 1) // 2, two, 0)
    for cols in panels(0, rows):
        for lines in panels(0, cols.start) if cols.start > 0 else []:
            x[cols, lines] = x[lines, cols].T

    out_copy = pltpu.make_async_copy(x.at[left, :], density_out, out_sem)
    out_copy.start()

    chunk = 64
    line = lax.broadcasted_iota(jnp.int32, (8, order), 0)
    columns = jnp.zeros((8, order), jnp.float32)
    own_rows = jnp.zeros((8, rows), jnp.float32)
    ones = jnp.ones((8, SUB), jnp.bfloat16)
    for c in range(3):
        deriv_copies[c].wait()

        def strip(number, total, c=c):
            at = pl.ds(pl.multiple_of(number * chunk, chunk), chunk)
            weighted = x[at, :] * deriv_held[c, at, :]
            row_part[at, :] = sum(weighted[:, lane : lane + SUB] for lane in range(0, order, SUB))
            return total + jnp.sum(weighted.reshape(chunk // 8, 8, order), axis=0)

        total = lax.fori_loop(0, rows // chunk, strip, jnp.zeros((8, order), jnp.float32))
        columns = jnp.where(line == c, jnp.sum(total, axis=0, keepdims=True), columns)
        row_sums = sum(
            lax.dot_general(ones, part, (((1,), (1,)), ((), ())), preferred_element_type=jnp.float32)
            for part in thirds(row_part[...])
        )
        own_rows = jnp.where(line[:, :rows] == c, row_sums, own_rows)
    atom_ids = lax.broadcasted_iota(jnp.int32, (rows, atoms), 1)
    own_hot = (lax.broadcasted_iota(jnp.int32, (rows, atoms), 0) // ORB == atom_ids).astype(jnp.float32)
    own_out[...] = dot_one_hot(2.0 * (own_rows - columns[:, :rows]), own_hot.astype(jnp.bfloat16))
    letter = jnp.where(line[:, rows:] == 3, asked_row, -2.0 * columns[:, rows:])
    empty = jnp.where(lax.broadcasted_iota(jnp.int32, (4, SUB - slot_rows), 0) == 3, -1.0, 0.0)
    mail[...] = jnp.zeros(mail.shape, jnp.float32)
    for block in range(block_count):
        content = letter[0:4, block * slot_rows : (block + 1) * slot_rows]
        to = lax.rem(place[0] + (block_offset(block) + mail.shape[0]), mail.shape[0])
        mail[to] = jnp.concatenate([content, empty], axis=1)
    out_copy.wait()


def collect(place, mail, own, forces):
    count = mail.shape[0]
    atoms = own.shape[1]
    letters = jnp.concatenate(
        [mail[lax.rem(place[0] + (count - block_offset(block)), count)] for block in range(2 * NB)],
        axis=1,
    )
    wanted = letters[3:4, :] == lax.broadcasted_iota(jnp.int32, (atoms, 1), 0).astype(jnp.float32)
    wanted = wanted.astype(jnp.float32).astype(jnp.bfloat16)
    sums = sum(
        lax.dot_general(part, wanted, (((1,), (1,)), ((), ())), preferred_element_type=jnp.float32)
        for part in thirds(jnp.concatenate([letters, letters], axis=0))
    )
    forces[...] = own[0:3, :] + sums[0:3, :]


def own_part(high_end, low_end, branches, core, request):
    rows, order = core.shape
    halo = order - rows
    vmem = pl.BlockSpec(memory_space=pltpu.VMEM)
    smem = pl.BlockSpec(memory_space=pltpu.SMEM)
    kinds = [
        ((rows, halo), jnp.bfloat16),
        ((rows, halo), jnp.bfloat16),
        ((rows, halo), jnp.float32),
        ((rows, halo), jnp.float32),
        ((halo, halo), jnp.float32),
        ((rows, rows), jnp.float32),
        ((rows, rows), jnp.bfloat16),
        ((rows, rows), jnp.bfloat16),
        ((rows, SUB), jnp.float32),
        ((8, rows), jnp.float32),
    ]
    return pl.pallas_call(
        own_kernel,
        out_shape=[jax.ShapeDtypeStruct(*kind) for kind in kinds],
        in_specs=[smem, smem, smem, vmem, vmem],
        out_specs=[vmem] * len(kinds),
        scratch_shapes=[
            pltpu.VMEM((order, order), jnp.bfloat16),
            pltpu.VMEM((order, order), jnp.bfloat16),
            pltpu.VMEM((8, order), jnp.float32),
            pltpu.VMEM((order, SUB), jnp.float32),
        ],
        compiler_params=pltpu.CompilerParams(vmem_limit_bytes=OWN_VMEM_BYTES),
        cost_estimate=pl.CostEstimate(
            flops=2 * 3 * order**3 // 3, bytes_accessed=13_000_000, transcendentals=0
        ),
    )(high_end, low_end, branches, core, request)


def density_and_terms(place, high_end, low_end, branches, request, deriv, ready, pieces):
    rows, order = deriv.shape[1:]
    atoms = rows // ORB
    vmem = pl.BlockSpec(memory_space=pltpu.VMEM)
    smem = pl.BlockSpec(memory_space=pltpu.SMEM)
    anywhere = pl.BlockSpec(memory_space=pl.ANY)
    square = (order, order)
    return pl.pallas_call(
        kernel,
        out_shape=[
            jax.ShapeDtypeStruct((rows, order), jnp.float32),
            jax.ShapeDtypeStruct((8, atoms), jnp.float32),
            jax.ShapeDtypeStruct((lax.axis_size("dom"), 4, SUB), jnp.float32),
        ],
        in_specs=[smem, smem, smem, smem, vmem, anywhere] + [vmem] * (len(ready) + len(pieces)),
        out_specs=[anywhere, vmem, vmem],
        scratch_shapes=[
            pltpu.VMEM(square, jnp.float32),
            pltpu.VMEM(square, jnp.bfloat16),
            pltpu.VMEM(square, jnp.bfloat16),
            pltpu.VMEM(square, jnp.bfloat16),
            pltpu.VMEM(square, jnp.bfloat16),
            pltpu.VMEM((8, order), jnp.float32),
            pltpu.VMEM((8, order), jnp.float32),
            pltpu.VMEM((order, SUB), jnp.float32),
            pltpu.VMEM((order, SUB), jnp.float32),
            pltpu.VMEM((order - rows, order - rows), jnp.float32),
            pltpu.VMEM((3, rows, order), jnp.float32),
            pltpu.VMEM((rows, SUB), jnp.float32),
            pltpu.SemaphoreType.DMA((3,)),
            pltpu.SemaphoreType.DMA,
        ],
        compiler_params=pltpu.CompilerParams(vmem_limit_bytes=VMEM_BYTES),
        cost_estimate=pl.CostEstimate(
            flops=2 * 3 * 3 * order**3, bytes_accessed=24_000_000, transcendentals=0
        ),
    )(place, high_end, low_end, branches, request, deriv, *ready, *pieces)


def per_device(ham_core, halo_rows, halo_request, deriv, e_low, e_high, branches):
    row_count, order_all = ham_core.shape
    block_count = 2 * NB
    early = (6, 3, 2, 1, 5)
    late = (0, 4, 7)
    first = halo_rows[0, early[0], :, row_count:]
    pieces = {early[0]: passed_along(first, "dom", -block_offset(early[0]))}
    rest, _ = lax.optimization_barrier((halo_rows, first))
    halo = rest[0, :, :, row_count:]
    for block in early[1:]:
        pieces[block] = passed_along(halo[block], "dom", -block_offset(block))
    *ready, own_row = own_part(e_high, e_low, branches, ham_core, halo_request)
    waiting, own_row = lax.optimization_barrier(([halo[block] for block in late], own_row))
    for block, piece in zip(late, waiting):
        pieces[block] = passed_along(piece, "dom", -block_offset(block))
    place = lax.axis_index("dom")[None].astype(jnp.int32)
    density, own, mail = density_and_terms(
        place,
        e_high,
        e_low,
        branches,
        halo_request,
        deriv.reshape(3, row_count, order_all),
        [*ready, own_row],
        [pieces[block] for block in range(block_count)],
    )
    arrived = lax.all_to_all(mail, "dom", 0, 0, tiled=True)
    forces = pl.pallas_call(
        collect,
        out_shape=jax.ShapeDtypeStruct((3, own.shape[1]), jnp.float32),
        in_specs=[
            pl.BlockSpec(memory_space=pltpu.SMEM),
            pl.BlockSpec(memory_space=pltpu.VMEM),
            pl.BlockSpec(memory_space=pltpu.VMEM),
        ],
        out_specs=pl.BlockSpec(memory_space=pltpu.VMEM),
    )(place, arrived, own)
    return (density, forces)


def solution(mesh):
    in_specs = (
        P("dom", None),
        P("dom", None, None, None),
        P("dom", None),
        P(None, "dom", None, None),
        P(),
        P(),
        P(),
    )
    out_specs = (P("dom", None), P(None, "dom"))
    return jax.shard_map(
        per_device, mesh=mesh, in_specs=in_specs, out_specs=out_specs, check_vma=False
    )
```

```python
import functools

import jax
import jax.numpy as jnp
from jax import lax
from jax.experimental import pallas as pl
from jax.experimental.pallas import tpu as pltpu
from jax.sharding import PartitionSpec as P

ORB = 4
NB = 4
ITERS = 5
PANEL = 256
SUB = 128
VMEM_BYTES = 38 * 1024 * 1024
OWN_VMEM_BYTES = 16 * 1024 * 1024


def passed_along(value, axis, steps):
    count = lax.axis_size(axis)
    pairs = [(source, (source + steps) % count) for source in range(count)]
    return lax.ppermute(value, axis, pairs)


def block_offset(block):
    if block < NB:
        return block + 1
    return NB - 1 - block


def halves(value):
    high = value.astype(jnp.bfloat16)
    low = (value - high.astype(jnp.float32)).astype(jnp.bfloat16)
    return high, low


def thirds(value):
    high = value.astype(jnp.bfloat16)
    rest = value - high.astype(jnp.float32)
    middle, low = halves(rest)
    return high, middle, low


def dot(left, right):
    return jnp.dot(left, right, preferred_element_type=jnp.float32)


def dot_one_hot(value, one_hot):
    return sum(dot(part, one_hot) for part in thirds(value))


def on_diagonal(shape):
    return lax.broadcasted_iota(jnp.int32, shape, 0) == lax.broadcasted_iota(jnp.int32, shape, 1)


def three_passes(left_high, left_low, right_high, right_low):
    return dot(
        jnp.concatenate([left_high, left_high, left_low], axis=1),
        jnp.concatenate([right_high, right_low, right_high], axis=0),
    )


def square_passes(left_high, left_low, right_high, right_low):
    cross = dot(left_high, right_low)
    return dot(left_high, right_high) + (cross + cross.T)


def step_factors(branches, number):
    taken = (branches[number] == 1).astype(jnp.float32)
    return 2.0 * taken, 1.0 - 2.0 * taken


def panels(start, end):
    cuts = [start] + [at for at in range(0, end, PANEL) if at > start] + [end]
    return [slice(low, high) for low, high in zip(cuts, cuts[1:])]


def spread_lanes(column, width):
    return jnp.concatenate([column] * (width // SUB), axis=1)


def combined(old, off, keep, add, state, rows_at, cols_at, on_diag):
    diag_row, diag_col = state[2:]
    factor_col = spread_lanes(keep + add * diag_col[rows_at, :], old.shape[1])
    value = old * (factor_col + add * diag_row[0:1, cols_at]) + add * off
    if on_diag:
        value = value - jnp.where(on_diagonal(value.shape), add * (old * old), 0.0)
    return value


def store_matrix(value, state, rows_at, cols_at):
    high_ref, low_ref, diag_row, diag_col = state
    if rows_at.start == cols_at.start:
        size = value.shape[0]
        line = jnp.where(on_diagonal(value.shape), value, 0.0)
        diag_row[:, cols_at] = jnp.broadcast_to(jnp.sum(line, axis=0, keepdims=True), (8, size))
        diag_col[rows_at, :] = jnp.broadcast_to(jnp.sum(line, axis=1, keepdims=True), (size, SUB))
        value = value - line
    high, low = halves(value)
    high_ref[rows_at, cols_at] = high
    low_ref[rows_at, cols_at] = low
    if rows_at.start != cols_at.start:
        high_ref[cols_at, rows_at] = high.T
        low_ref[cols_at, rows_at] = low.T


def start_block(source, row, col, top, scale):
    value = 0.5 * (source[row, col] + source[col, row].T)
    if row.start == col.start:
        value = value - jnp.where(on_diagonal(value.shape), top, 0.0)
    return -scale * value


def cut(size):
    return [slice(at, at + SUB) for at in range(0, size, SUB)]


def shifted(piece, by):
    return slice(piece.start + by, piece.stop + by)


def asked_atoms(request, orbitals):
    atoms = request.shape[1]
    expand = lax.broadcasted_iota(jnp.int32, (orbitals, atoms), 0) // ORB == lax.broadcasted_iota(
        jnp.int32, (orbitals, atoms), 1
    )
    expand = expand.astype(jnp.float32).astype(jnp.bfloat16)
    values = jnp.broadcast_to(request[...].astype(jnp.float32), (8, atoms)).astype(jnp.bfloat16)
    transposed = (((1,), (1,)), ((), ()))
    row = lax.dot_general(values, expand, transposed, preferred_element_type=jnp.float32)
    col = lax.dot_general(expand, values, transposed, preferred_element_type=jnp.float32)
    return row[0:1, :], col[:, 0:1]


def own_kernel(
    high_end, low_end, branches, core, request, high_cross, low_cross, x_cross, y_cross, y_halo,
    x_own, next_high, next_low, next_col, next_row, high, low, diag_row, diag_col
):
    rows, order = core.shape
    state = (high, low, diag_row, diag_col)
    later = (next_high, next_low, next_row, next_col)
    left, right = slice(0, rows), slice(rows, order)
    top = high_end[0]
    scale = 1.0 / (high_end[0] - low_end[0])
    keep, add = step_factors(branches, 0)
    asked_row, _ = asked_atoms(request, order - rows)
    live_row = (asked_row >= 0).astype(jnp.float32)
    for row in cut(rows):
        for col in cut(order - rows):
            value = -scale * (core[row, shifted(col, rows)] * live_row[:, col])
            x_cross[row, col] = value
            store_matrix(value, state, row, shifted(col, rows))
    for row in cut(rows):
        for col in cut(rows):
            if row.start <= col.start:
                value = start_block(core, row, col, top, scale)
                x_own[row, col] = value
                if row.start < col.start and row.start // PANEL == col.start // PANEL:
                    x_own[col, row] = value.T
                store_matrix(value, state, row, col)
    high_cross[...] = high[left, right]
    low_cross[...] = low[left, right]
    for row in panels(0, rows):
        for col in panels(rows, order):
            at = shifted(col, -rows)
            off = three_passes(high[row, left], low[row, left], high[left, col], low[left, col])
            factor = spread_lanes(keep + add * diag_col[row, :], at.stop - at.start)
            y_cross[row, at] = x_cross[row, at] * factor + add * off
    for row in panels(rows, order):
        for col in panels(rows, order):
            if row.start <= col.start:
                passes = square_passes if row.start == col.start else three_passes
                off = passes(high[row, left], low[row, left], high[left, col], low[left, col])
                y_halo[shifted(row, -rows), shifted(col, -rows)] = add * off
    for row in panels(0, rows):
        for col in panels(0, rows):
            if row.start <= col.start:
                passes = square_passes if row.start == col.start else three_passes
                off = passes(high[row, :], low[row, :], high[:, col], low[:, col])
                value = combined(
                    x_own[row, col], off, keep, add, state, row, col, row.start == col.start
                )
                x_own[row, col] = value
                store_matrix(value, later, row, col)


def kernel(place, high_end, low_end, branches, request, deriv, *refs):
    block_count = 2 * NB
    (high_cross, low_cross, x_cross, y_cross, y_halo, x_own, high_own, low_own, own_col, own_row) = refs[:10]
    pieces = refs[10 : 10 + block_count]
    density_out, own_out, mail = refs[10 + block_count : 13 + block_count]
    (x, high_a, low_a, high_b, low_b, diag_row_a, diag_row_b, diag_col_a, diag_col_b) = refs[
        13 + block_count : 22 + block_count
    ]
    halo, deriv_held, row_part, deriv_sems, out_sem = refs[22 + block_count :]
    order = x.shape[0]
    rows = x_own.shape[0]
    atoms = rows // ORB
    slot_rows = (order - rows) // block_count
    left, right = slice(0, rows), slice(rows, order)

    deriv_copies = [
        pltpu.make_async_copy(deriv.at[c], deriv_held.at[c], deriv_sems.at[c]) for c in range(3)
    ]
    for copy in deriv_copies:
        copy.start()
    state_a = (high_a, low_a, diag_row_a, diag_col_a)
    state_b = (high_b, low_b, diag_row_b, diag_col_b)

    top = high_end[0]
    scale = 1.0 / (high_end[0] - low_end[0])
    for block in range(block_count):
        halo[block * slot_rows : (block + 1) * slot_rows, :] = pieces[block][...]
    asked_row, asked_col = asked_atoms(request, order - rows)
    live_row = (asked_row >= 0).astype(jnp.float32)
    live_col = (asked_col >= 0).astype(jnp.float32)
    for row in cut(order - rows):
        for col in cut(order - rows):
            if row.start <= col.start:
                value = start_block(halo, row, col, top, scale)
                value = value * live_col[row, :] * live_row[:, col]
                down, across = shifted(row, rows), shifted(col, rows)
                x[down, across] = value
                if row.start < col.start and down.start // PANEL == across.start // PANEL:
                    x[across, down] = value.T
                store_matrix(value, state_b, row, col)
    x[left, left] = x_own[...]
    high_a[left, left] = high_own[...]
    low_a[left, left] = low_own[...]
    diag_col_a[left, :] = own_col[...]
    diag_row_a[:, left] = own_row[...]
    keep, add = step_factors(branches, 0)
    for row in panels(0, rows):
        for col in panels(rows, order):
            at = shifted(col, -rows)
            off = three_passes(high_cross[row, :], low_cross[row, :], high_b[left, at], low_b[left, at])
            value = y_cross[row, at] + x_cross[row, at] * (add * diag_row_b[0:1, at]) + add * off
            x[row, col] = value
            if row.start // PANEL == col.start // PANEL:
                x[col, row] = value.T
            store_matrix(value, state_a, row, col)
    for row in panels(rows, order):
        for col in panels(rows, order):
            if row.start <= col.start:
                down, across = shifted(row, -rows), shifted(col, -rows)
                passes = square_passes if row.start == col.start else three_passes
                off = passes(high_b[down, left], low_b[down, left], high_b[left, across], low_b[left, across])
                on_diag = row.start == col.start
                value = combined(x[row, col], off, keep, add, state_b, down, across, on_diag)
                value = value + y_halo[down, across]
                x[row, col] = value
                store_matrix(value, state_a, row, col)

    def block_step(number, now, later, lines, cols):
        keep, add = step_factors(branches, number)
        high, low = now[:2]
        on_diag = lines.start == cols.start
        passes = square_passes if on_diag else three_passes
        off = passes(high[lines, :], low[lines, :], high[:, cols], low[:, cols])
        value = combined(x[lines, cols], off, keep, add, now, lines, cols, on_diag)
        x[lines, cols] = value
        store_matrix(value, later, lines, cols)

    def squaring(number, now, later, unless_last):
        away = []
        for cols in panels(0, order):
            for lines in panels(0, cols.stop):
                if lines.start >= rows:
                    away.append((lines, cols))
                else:
                    block_step(number, now, later, lines, cols)

        def others():
            for lines, cols in away:
                block_step(number, now, later, lines, cols)

        if unless_last:
            pl.when(number < ITERS - 1)(others)
        else:
            others()

    def two(pair, carry):
        squaring(2 * pair + 1, state_a, state_b, False)
        squaring(2 * pair + 2, state_b, state_a, True)
        return carry

    lax.fori_loop(0, (ITERS - 1) // 2, two, 0)
    for cols in panels(0, rows):
        for lines in panels(0, cols.start) if cols.start > 0 else []:
            x[cols, lines] = x[lines, cols].T

    out_copy = pltpu.make_async_copy(x.at[left, :], density_out, out_sem)
    out_copy.start()

    chunk = 64
    line = lax.broadcasted_iota(jnp.int32, (8, order), 0)
    columns = jnp.zeros((8, order), jnp.float32)
    own_rows = jnp.zeros((8, rows), jnp.float32)
    ones = jnp.ones((8, SUB), jnp.bfloat16)
    for c in range(3):
        deriv_copies[c].wait()

        def strip(number, total, c=c):
            at = pl.ds(pl.multiple_of(number * chunk, chunk), chunk)
            weighted = x[at, :] * deriv_held[c, at, :]
            row_part[at, :] = sum(weighted[:, lane : lane + SUB] for lane in range(0, order, SUB))
            return total + jnp.sum(weighted.reshape(chunk // 8, 8, order), axis=0)

        total = lax.fori_loop(0, rows // chunk, strip, jnp.zeros((8, order), jnp.float32))
        columns = jnp.where(line == c, jnp.sum(total, axis=0, keepdims=True), columns)
        row_sums = sum(
            lax.dot_general(ones, part, (((1,), (1,)), ((), ())), preferred_element_type=jnp.float32)
            for part in thirds(row_part[...])
        )
        own_rows = jnp.where(line[:, :rows] == c, row_sums, own_rows)
    atom_ids = lax.broadcasted_iota(jnp.int32, (rows, atoms), 1)
    own_hot = (lax.broadcasted_iota(jnp.int32, (rows, atoms), 0) // ORB == atom_ids).astype(jnp.float32)
    own_out[...] = dot_one_hot(2.0 * (own_rows - columns[:, :rows]), own_hot.astype(jnp.bfloat16))
    letter = jnp.where(line[:, rows:] == 3, asked_row, -2.0 * columns[:, rows:])
    empty = jnp.where(lax.broadcasted_iota(jnp.int32, (4, SUB - slot_rows), 0) == 3, -1.0, 0.0)
    mail[...] = jnp.zeros(mail.shape, jnp.float32)
    for block in range(block_count):
        content = letter[0:4, block * slot_rows : (block + 1) * slot_rows]
        to = lax.rem(place[0] + (block_offset(block) + mail.shape[0]), mail.shape[0])
        mail[to] = jnp.concatenate([content, empty], axis=1)
    out_copy.wait()


def collect(place, mail, own, forces):
    count = mail.shape[0]
    atoms = own.shape[1]
    letters = jnp.concatenate(
        [mail[lax.rem(place[0] + (count - block_offset(block)), count)] for block in range(2 * NB)],
        axis=1,
    )
    wanted = letters[3:4, :] == lax.broadcasted_iota(jnp.int32, (atoms, 1), 0).astype(jnp.float32)
    wanted = wanted.astype(jnp.float32).astype(jnp.bfloat16)
    sums = sum(
        lax.dot_general(part, wanted, (((1,), (1,)), ((), ())), preferred_element_type=jnp.float32)
        for part in thirds(jnp.concatenate([letters, letters], axis=0))
    )
    forces[...] = own[0:3, :] + sums[0:3, :]


def own_part(high_end, low_end, branches, core, request):
    rows, order = core.shape
    halo = order - rows
    vmem = pl.BlockSpec(memory_space=pltpu.VMEM)
    smem = pl.BlockSpec(memory_space=pltpu.SMEM)
    kinds = [
        ((rows, halo), jnp.bfloat16),
        ((rows, halo), jnp.bfloat16),
        ((rows, halo), jnp.float32),
        ((rows, halo), jnp.float32),
        ((halo, halo), jnp.float32),
        ((rows, rows), jnp.float32),
        ((rows, rows), jnp.bfloat16),
        ((rows, rows), jnp.bfloat16),
        ((rows, SUB), jnp.float32),
        ((8, rows), jnp.float32),
    ]
    return pl.pallas_call(
        own_kernel,
        out_shape=[jax.ShapeDtypeStruct(*kind) for kind in kinds],
        in_specs=[smem, smem, smem, vmem, vmem],
        out_specs=[vmem] * len(kinds),
        scratch_shapes=[
            pltpu.VMEM((order, order), jnp.bfloat16),
            pltpu.VMEM((order, order), jnp.bfloat16),
            pltpu.VMEM((8, order), jnp.float32),
            pltpu.VMEM((order, SUB), jnp.float32),
        ],
        compiler_params=pltpu.CompilerParams(vmem_limit_bytes=OWN_VMEM_BYTES),
        cost_estimate=pl.CostEstimate(
            flops=2 * 3 * order**3 // 3, bytes_accessed=13_000_000, transcendentals=0
        ),
    )(high_end, low_end, branches, core, request)


def density_and_terms(place, high_end, low_end, branches, request, deriv, ready, pieces):
    rows, order = deriv.shape[1:]
    atoms = rows // ORB
    vmem = pl.BlockSpec(memory_space=pltpu.VMEM)
    smem = pl.BlockSpec(memory_space=pltpu.SMEM)
    anywhere = pl.BlockSpec(memory_space=pl.ANY)
    square = (order, order)
    return pl.pallas_call(
        kernel,
        out_shape=[
            jax.ShapeDtypeStruct((rows, order), jnp.float32),
            jax.ShapeDtypeStruct((8, atoms), jnp.float32),
            jax.ShapeDtypeStruct((lax.axis_size("dom"), 4, SUB), jnp.float32),
        ],
        in_specs=[smem, smem, smem, smem, vmem, anywhere] + [vmem] * (len(ready) + len(pieces)),
        out_specs=[anywhere, vmem, vmem],
        scratch_shapes=[
            pltpu.VMEM(square, jnp.float32),
            pltpu.VMEM(square, jnp.bfloat16),
            pltpu.VMEM(square, jnp.bfloat16),
            pltpu.VMEM(square, jnp.bfloat16),
            pltpu.VMEM(square, jnp.bfloat16),
            pltpu.VMEM((8, order), jnp.float32),
            pltpu.VMEM((8, order), jnp.float32),
            pltpu.VMEM((order, SUB), jnp.float32),
            pltpu.VMEM((order, SUB), jnp.float32),
            pltpu.VMEM((order - rows, order - rows), jnp.float32),
            pltpu.VMEM((3, rows, order), jnp.float32),
            pltpu.VMEM((rows, SUB), jnp.float32),
            pltpu.SemaphoreType.DMA((3,)),
            pltpu.SemaphoreType.DMA,
        ],
        compiler_params=pltpu.CompilerParams(vmem_limit_bytes=VMEM_BYTES),
        cost_estimate=pl.CostEstimate(
            flops=2 * 3 * 3 * order**3, bytes_accessed=24_000_000, transcendentals=0
        ),
    )(place, high_end, low_end, branches, request, deriv, *ready, *pieces)


def per_device(ham_core, halo_rows, halo_request, deriv, e_low, e_high, branches):
    row_count, order_all = ham_core.shape
    block_count = 2 * NB
    halo = halo_rows[0, :, :, row_count:]
    flat_deriv = deriv.reshape(3, row_count, order_all)
    early = (1, 2, 3, 5, 6)
    late = (0, 4, 7)
    pieces = {block: passed_along(halo[block], "dom", -block_offset(block)) for block in early}
    waiting, flat_deriv = lax.optimization_barrier(([halo[block] for block in late], flat_deriv))
    for block, piece in zip(late, waiting):
        pieces[block] = passed_along(piece, "dom", -block_offset(block))
    place = lax.axis_index("dom")[None].astype(jnp.int32)
    ready = own_part(e_high, e_low, branches, ham_core, halo_request)
    density, own, mail = density_and_terms(
        place,
        e_high,
        e_low,
        branches,
        halo_request,
        flat_deriv,
        ready,
        [pieces[block] for block in range(block_count)],
    )
    arrived = lax.all_to_all(mail, "dom", 0, 0, tiled=True)
    forces = pl.pallas_call(
        collect,
        out_shape=jax.ShapeDtypeStruct((3, own.shape[1]), jnp.float32),
        in_specs=[
            pl.BlockSpec(memory_space=pltpu.SMEM),
            pl.BlockSpec(memory_space=pltpu.VMEM),
            pl.BlockSpec(memory_space=pltpu.VMEM),
        ],
        out_specs=pl.BlockSpec(memory_space=pltpu.VMEM),
    )(place, arrived, own)
    return (density, forces)


def solution(mesh):
    in_specs = (
        P("dom", None),
        P("dom", None, None, None),
        P("dom", None),
        P(None, "dom", None, None),
        P(),
        P(),
        P(),
    )
    out_specs = (P("dom", None), P(None, "dom"))
    return jax.shard_map(
        per_device, mesh=mesh, in_specs=in_specs, out_specs=out_specs, check_vma=False
    )
```

```python
import functools

import jax
import jax.numpy as jnp
from jax import lax
from jax.experimental import pallas as pl
from jax.experimental.pallas import tpu as pltpu
from jax.sharding import PartitionSpec as P

ORB = 4
NB = 4
ITERS = 5
PANEL = 256
SUB = 128
VMEM_BYTES = 38 * 1024 * 1024
OWN_VMEM_BYTES = 16 * 1024 * 1024


def passed_along(value, axis, steps):
    count = lax.axis_size(axis)
    pairs = [(source, (source + steps) % count) for source in range(count)]
    return lax.ppermute(value, axis, pairs)


def block_offset(block):
    if block < NB:
        return block + 1
    return NB - 1 - block


def halves(value):
    high = value.astype(jnp.bfloat16)
    low = (value - high.astype(jnp.float32)).astype(jnp.bfloat16)
    return high, low


def thirds(value):
    high = value.astype(jnp.bfloat16)
    rest = value - high.astype(jnp.float32)
    middle, low = halves(rest)
    return high, middle, low


def dot(left, right):
    return jnp.dot(left, right, preferred_element_type=jnp.float32)


def dot_one_hot(value, one_hot):
    return sum(dot(part, one_hot) for part in thirds(value))


def on_diagonal(shape):
    return lax.broadcasted_iota(jnp.int32, shape, 0) == lax.broadcasted_iota(jnp.int32, shape, 1)


def three_passes(left_high, left_low, right_high, right_low):
    return dot(
        jnp.concatenate([left_high, left_high, left_low], axis=1),
        jnp.concatenate([right_high, right_low, right_high], axis=0),
    )


def square_passes(left_high, left_low, right_high, right_low):
    cross = dot(left_high, right_low)
    return dot(left_high, right_high) + (cross + cross.T)


def step_factors(branches, number):
    taken = (branches[number] == 1).astype(jnp.float32)
    return 2.0 * taken, 1.0 - 2.0 * taken


def panels(start, end):
    cuts = [start] + [at for at in range(0, end, PANEL) if at > start] + [end]
    return [slice(low, high) for low, high in zip(cuts, cuts[1:])]


def spread_lanes(column, width):
    return jnp.concatenate([column] * (width // SUB), axis=1)


def combined(old, off, keep, add, state, rows_at, cols_at, on_diag):
    diag_row, diag_col = state[2:]
    factor_col = spread_lanes(keep + add * diag_col[rows_at, :], old.shape[1])
    value = old * (factor_col + add * diag_row[0:1, cols_at]) + add * off
    if on_diag:
        value = value - jnp.where(on_diagonal(value.shape), add * (old * old), 0.0)
    return value


def store_matrix(value, state, rows_at, cols_at):
    high_ref, low_ref, diag_row, diag_col = state
    if rows_at.start == cols_at.start:
        size = value.shape[0]
        line = jnp.where(on_diagonal(value.shape), value, 0.0)
        diag_row[:, cols_at] = jnp.broadcast_to(jnp.sum(line, axis=0, keepdims=True), (8, size))
        diag_col[rows_at, :] = jnp.broadcast_to(jnp.sum(line, axis=1, keepdims=True), (size, SUB))
        value = value - line
    high, low = halves(value)
    high_ref[rows_at, cols_at] = high
    low_ref[rows_at, cols_at] = low
    if rows_at.start != cols_at.start:
        high_ref[cols_at, rows_at] = high.T
        low_ref[cols_at, rows_at] = low.T


def start_block(source, row, col, top, scale):
    value = 0.5 * (source[row, col] + source[col, row].T)
    if row.start == col.start:
        value = value - jnp.where(on_diagonal(value.shape), top, 0.0)
    return -scale * value


def cut(size):
    return [slice(at, at + SUB) for at in range(0, size, SUB)]


def shifted(piece, by):
    return slice(piece.start + by, piece.stop + by)


def asked_atoms(request, orbitals):
    atoms = request.shape[1]
    expand = lax.broadcasted_iota(jnp.int32, (orbitals, atoms), 0) // ORB == lax.broadcasted_iota(
        jnp.int32, (orbitals, atoms), 1
    )
    expand = expand.astype(jnp.float32).astype(jnp.bfloat16)
    values = jnp.broadcast_to(request[...].astype(jnp.float32), (8, atoms)).astype(jnp.bfloat16)
    transposed = (((1,), (1,)), ((), ()))
    row = lax.dot_general(values, expand, transposed, preferred_element_type=jnp.float32)
    col = lax.dot_general(expand, values, transposed, preferred_element_type=jnp.float32)
    return row[0:1, :], col[:, 0:1]


def own_kernel(
    high_end, low_end, branches, core, request, high_cross, low_cross, x_cross, y_cross, y_halo,
    x_own, next_high, next_low, next_col, next_row, high, low, diag_row, diag_col
):
    rows, order = core.shape
    state = (high, low, diag_row, diag_col)
    later = (next_high, next_low, next_row, next_col)
    left, right = slice(0, rows), slice(rows, order)
    top = high_end[0]
    scale = 1.0 / (high_end[0] - low_end[0])
    keep, add = step_factors(branches, 0)
    asked_row, _ = asked_atoms(request, order - rows)
    live_row = (asked_row >= 0).astype(jnp.float32)
    for row in cut(rows):
        for col in cut(order - rows):
            value = -scale * (core[row, shifted(col, rows)] * live_row[:, col])
            x_cross[row, col] = value
            store_matrix(value, state, row, shifted(col, rows))
    for row in cut(rows):
        for col in cut(rows):
            if row.start <= col.start:
                value = start_block(core, row, col, top, scale)
                x_own[row, col] = value
                if row.start < col.start and row.start // PANEL == col.start // PANEL:
                    x_own[col, row] = value.T
                store_matrix(value, state, row, col)
    high_cross[...] = high[left, right]
    low_cross[...] = low[left, right]
    for row in panels(0, rows):
        for col in panels(rows, order):
            at = shifted(col, -rows)
            off = three_passes(high[row, left], low[row, left], high[left, col], low[left, col])
            factor = spread_lanes(keep + add * diag_col[row, :], at.stop - at.start)
            y_cross[row, at] = x_cross[row, at] * factor + add * off
    for row in panels(rows, order):
        for col in panels(rows, order):
            if row.start <= col.start:
                passes = square_passes if row.start == col.start else three_passes
                off = passes(high[row, left], low[row, left], high[left, col], low[left, col])
                y_halo[shifted(row, -rows), shifted(col, -rows)] = add * off
    for row in panels(0, rows):
        for col in panels(0, rows):
            if row.start <= col.start:
                passes = square_passes if row.start == col.start else three_passes
                off = passes(high[row, :], low[row, :], high[:, col], low[:, col])
                value = combined(
                    x_own[row, col], off, keep, add, state, row, col, row.start == col.start
                )
                x_own[row, col] = value
                store_matrix(value, later, row, col)


def kernel(place, high_end, low_end, branches, request, deriv, *refs):
    block_count = 2 * NB
    (high_cross, low_cross, x_cross, y_cross, y_halo, x_own, high_own, low_own, own_col, own_row) = refs[:10]
    pieces = refs[10 : 10 + block_count]
    density_out, own_out, mail = refs[10 + block_count : 13 + block_count]
    (x, high_a, low_a, high_b, low_b, diag_row_a, diag_row_b, diag_col_a, diag_col_b) = refs[
        13 + block_count : 22 + block_count
    ]
    halo, deriv_held, row_part, deriv_sems, out_sem = refs[22 + block_count :]
    order = x.shape[0]
    rows = x_own.shape[0]
    atoms = rows // ORB
    slot_rows = (order - rows) // block_count
    left, right = slice(0, rows), slice(rows, order)

    deriv_copies = [
        pltpu.make_async_copy(deriv.at[c], deriv_held.at[c], deriv_sems.at[c]) for c in range(3)
    ]
    for copy in deriv_copies:
        copy.start()
    state_a = (high_a, low_a, diag_row_a, diag_col_a)
    state_b = (high_b, low_b, diag_row_b, diag_col_b)

    top = high_end[0]
    scale = 1.0 / (high_end[0] - low_end[0])
    for block in range(block_count):
        halo[block * slot_rows : (block + 1) * slot_rows, :] = pieces[block][...]
    asked_row, asked_col = asked_atoms(request, order - rows)
    live_row = (asked_row >= 0).astype(jnp.float32)
    live_col = (asked_col >= 0).astype(jnp.float32)
    for row in cut(order - rows):
        for col in cut(order - rows):
            if row.start <= col.start:
                value = start_block(halo, row, col, top, scale)
                value = value * live_col[row, :] * live_row[:, col]
                down, across = shifted(row, rows), shifted(col, rows)
                x[down, across] = value
                if row.start < col.start and down.start // PANEL == across.start // PANEL:
                    x[across, down] = value.T
                store_matrix(value, state_b, row, col)
    x[left, left] = x_own[...]
    high_a[left, left] = high_own[...]
    low_a[left, left] = low_own[...]
    diag_col_a[left, :] = own_col[...]
    diag_row_a[:, left] = own_row[...]
    keep, add = step_factors(branches, 0)
    for row in panels(0, rows):
        for col in panels(rows, order):
            at = shifted(col, -rows)
            off = three_passes(high_cross[row, :], low_cross[row, :], high_b[left, at], low_b[left, at])
            value = y_cross[row, at] + x_cross[row, at] * (add * diag_row_b[0:1, at]) + add * off
            x[row, col] = value
            if row.start // PANEL == col.start // PANEL:
                x[col, row] = value.T
            store_matrix(value, state_a, row, col)
    for row in panels(rows, order):
        for col in panels(rows, order):
            if row.start <= col.start:
                down, across = shifted(row, -rows), shifted(col, -rows)
                passes = square_passes if row.start == col.start else three_passes
                off = passes(high_b[down, left], low_b[down, left], high_b[left, across], low_b[left, across])
                on_diag = row.start == col.start
                value = combined(x[row, col], off, keep, add, state_b, down, across, on_diag)
                value = value + y_halo[down, across]
                x[row, col] = value
                store_matrix(value, state_a, row, col)

    def block_step(number, now, later, lines, cols):
        keep, add = step_factors(branches, number)
        high, low = now[:2]
        on_diag = lines.start == cols.start
        passes = square_passes if on_diag else three_passes
        off = passes(high[lines, :], low[lines, :], high[:, cols], low[:, cols])
        value = combined(x[lines, cols], off, keep, add, now, lines, cols, on_diag)
        x[lines, cols] = value
        store_matrix(value, later, lines, cols)

    def squaring(number, now, later, unless_last):
        away = []
        for cols in panels(0, order):
            for lines in panels(0, cols.stop):
                if lines.start >= rows:
                    away.append((lines, cols))
                else:
                    block_step(number, now, later, lines, cols)

        def others():
            for lines, cols in away:
                block_step(number, now, later, lines, cols)

        if unless_last:
            pl.when(number < ITERS - 1)(others)
        else:
            others()

    def two(pair, carry):
        squaring(2 * pair + 1, state_a, state_b, False)
        squaring(2 * pair + 2, state_b, state_a, True)
        return carry

    lax.fori_loop(0, (ITERS - 1) // 2, two, 0)
    for cols in panels(0, rows):
        for lines in panels(0, cols.start) if cols.start > 0 else []:
            x[cols, lines] = x[lines, cols].T

    out_copy = pltpu.make_async_copy(x.at[left, :], density_out, out_sem)
    out_copy.start()

    chunk = 64
    line = lax.broadcasted_iota(jnp.int32, (8, order), 0)
    columns = jnp.zeros((8, order), jnp.float32)
    own_rows = jnp.zeros((8, rows), jnp.float32)
    ones = jnp.ones((8, SUB), jnp.bfloat16)
    for c in range(3):
        deriv_copies[c].wait()

        def strip(number, total, c=c):
            at = pl.ds(pl.multiple_of(number * chunk, chunk), chunk)
            some = pl.ds(pl.multiple_of(number * (chunk // ORB), chunk // ORB), chunk // ORB)
            weighted = x[at, :] * deriv_held[c, some].reshape(chunk, order)
            row_part[at, :] = sum(weighted[:, lane : lane + SUB] for lane in range(0, order, SUB))
            return total + jnp.sum(weighted.reshape(chunk // 8, 8, order), axis=0)

        total = lax.fori_loop(0, rows // chunk, strip, jnp.zeros((8, order), jnp.float32))
        columns = jnp.where(line == c, jnp.sum(total, axis=0, keepdims=True), columns)
        row_sums = sum(
            lax.dot_general(ones, part, (((1,), (1,)), ((), ())), preferred_element_type=jnp.float32)
            for part in thirds(row_part[...])
        )
        own_rows = jnp.where(line[:, :rows] == c, row_sums, own_rows)
    atom_ids = lax.broadcasted_iota(jnp.int32, (rows, atoms), 1)
    own_hot = (lax.broadcasted_iota(jnp.int32, (rows, atoms), 0) // ORB == atom_ids).astype(jnp.float32)
    own_out[...] = dot_one_hot(2.0 * (own_rows - columns[:, :rows]), own_hot.astype(jnp.bfloat16))
    letter = jnp.where(line[:, rows:] == 3, asked_row, -2.0 * columns[:, rows:])
    empty = jnp.where(lax.broadcasted_iota(jnp.int32, (4, SUB - slot_rows), 0) == 3, -1.0, 0.0)
    mail[...] = jnp.zeros(mail.shape, jnp.float32)
    for block in range(block_count):
        content = letter[0:4, block * slot_rows : (block + 1) * slot_rows]
        to = lax.rem(place[0] + (block_offset(block) + mail.shape[0]), mail.shape[0])
        mail[to] = jnp.concatenate([content, empty], axis=1)
    out_copy.wait()


def collect(place, mail, own, forces):
    count = mail.shape[0]
    atoms = own.shape[1]
    letters = jnp.concatenate(
        [mail[lax.rem(place[0] + (count - block_offset(block)), count)] for block in range(2 * NB)],
        axis=1,
    )
    wanted = letters[3:4, :] == lax.broadcasted_iota(jnp.int32, (atoms, 1), 0).astype(jnp.float32)
    wanted = wanted.astype(jnp.float32).astype(jnp.bfloat16)
    sums = sum(
        lax.dot_general(part, wanted, (((1,), (1,)), ((), ())), preferred_element_type=jnp.float32)
        for part in thirds(jnp.concatenate([letters, letters], axis=0))
    )
    forces[...] = own[0:3, :] + sums[0:3, :]


def own_part(high_end, low_end, branches, core, request):
    rows, order = core.shape
    halo = order - rows
    vmem = pl.BlockSpec(memory_space=pltpu.VMEM)
    smem = pl.BlockSpec(memory_space=pltpu.SMEM)
    kinds = [
        ((rows, halo), jnp.bfloat16),
        ((rows, halo), jnp.bfloat16),
        ((rows, halo), jnp.float32),
        ((rows, halo), jnp.float32),
        ((halo, halo), jnp.float32),
        ((rows, rows), jnp.float32),
        ((rows, rows), jnp.bfloat16),
        ((rows, rows), jnp.bfloat16),
        ((rows, SUB), jnp.float32),
        ((8, rows), jnp.float32),
    ]
    return pl.pallas_call(
        own_kernel,
        out_shape=[jax.ShapeDtypeStruct(*kind) for kind in kinds],
        in_specs=[smem, smem, smem, vmem, vmem],
        out_specs=[vmem] * len(kinds),
        scratch_shapes=[
            pltpu.VMEM((order, order), jnp.bfloat16),
            pltpu.VMEM((order, order), jnp.bfloat16),
            pltpu.VMEM((8, order), jnp.float32),
            pltpu.VMEM((order, SUB), jnp.float32),
        ],
        compiler_params=pltpu.CompilerParams(vmem_limit_bytes=OWN_VMEM_BYTES),
        cost_estimate=pl.CostEstimate(
            flops=2 * 3 * order**3 // 3, bytes_accessed=13_000_000, transcendentals=0
        ),
    )(high_end, low_end, branches, core, request)


def density_and_terms(place, high_end, low_end, branches, request, deriv, ready, pieces):
    rows, order = deriv.shape[1] * ORB, deriv.shape[3]
    atoms = rows // ORB
    vmem = pl.BlockSpec(memory_space=pltpu.VMEM)
    smem = pl.BlockSpec(memory_space=pltpu.SMEM)
    anywhere = pl.BlockSpec(memory_space=pl.ANY)
    square = (order, order)
    return pl.pallas_call(
        kernel,
        out_shape=[
            jax.ShapeDtypeStruct((rows, order), jnp.float32),
            jax.ShapeDtypeStruct((8, atoms), jnp.float32),
            jax.ShapeDtypeStruct((lax.axis_size("dom"), 4, SUB), jnp.float32),
        ],
        in_specs=[smem, smem, smem, smem, vmem, anywhere] + [vmem] * (len(ready) + len(pieces)),
        out_specs=[anywhere, vmem, vmem],
        scratch_shapes=[
            pltpu.VMEM(square, jnp.float32),
            pltpu.VMEM(square, jnp.bfloat16),
            pltpu.VMEM(square, jnp.bfloat16),
            pltpu.VMEM(square, jnp.bfloat16),
            pltpu.VMEM(square, jnp.bfloat16),
            pltpu.VMEM((8, order), jnp.float32),
            pltpu.VMEM((8, order), jnp.float32),
            pltpu.VMEM((order, SUB), jnp.float32),
            pltpu.VMEM((order, SUB), jnp.float32),
            pltpu.VMEM((order - rows, order - rows), jnp.float32),
            pltpu.VMEM((3, atoms, ORB, order), jnp.float32),
            pltpu.VMEM((rows, SUB), jnp.float32),
            pltpu.SemaphoreType.DMA((3,)),
            pltpu.SemaphoreType.DMA,
        ],
        compiler_params=pltpu.CompilerParams(vmem_limit_bytes=VMEM_BYTES),
        cost_estimate=pl.CostEstimate(
            flops=2 * 3 * 3 * order**3, bytes_accessed=24_000_000, transcendentals=0
        ),
    )(place, high_end, low_end, branches, request, deriv, *ready, *pieces)


def per_device(ham_core, halo_rows, halo_request, deriv, e_low, e_high, branches):
    row_count, order_all = ham_core.shape
    block_count = 2 * NB
    halo = halo_rows[0, :, :, row_count:]
    early = (6, 3, 2, 1, 5)
    late = (0, 4, 7)
    pieces = {block: passed_along(halo[block], "dom", -block_offset(block)) for block in early}
    *ready, own_row = own_part(e_high, e_low, branches, ham_core, halo_request)
    waiting, own_row = lax.optimization_barrier(([halo[block] for block in late], own_row))
    for block, piece in zip(late, waiting):
        pieces[block] = passed_along(piece, "dom", -block_offset(block))
    place = lax.axis_index("dom")[None].astype(jnp.int32)
    density, own, mail = density_and_terms(
        place,
        e_high,
        e_low,
        branches,
        halo_request,
        deriv,
        [*ready, own_row],
        [pieces[block] for block in range(block_count)],
    )
    arrived = lax.all_to_all(mail, "dom", 0, 0, tiled=True)
    forces = pl.pallas_call(
        collect,
        out_shape=jax.ShapeDtypeStruct((3, own.shape[1]), jnp.float32),
        in_specs=[
            pl.BlockSpec(memory_space=pltpu.SMEM),
            pl.BlockSpec(memory_space=pltpu.VMEM),
            pl.BlockSpec(memory_space=pltpu.VMEM),
        ],
        out_specs=pl.BlockSpec(memory_space=pltpu.VMEM),
    )(place, arrived, own)
    return (density, forces)


def solution(mesh):
    in_specs = (
        P("dom", None),
        P("dom", None, None, None),
        P("dom", None),
        P(None, "dom", None, None),
        P(),
        P(),
        P(),
    )
    out_specs = (P("dom", None), P(None, "dom"))
    return jax.shard_map(
        per_device, mesh=mesh, in_specs=in_specs, out_specs=out_specs, check_vma=False
    )
```

```python
import functools

import jax
import jax.numpy as jnp
from jax import lax
from jax.experimental import pallas as pl
from jax.experimental.pallas import tpu as pltpu
from jax.sharding import PartitionSpec as P

ORB = 4
NB = 4
ITERS = 5
PANEL = 256
SUB = 128
VMEM_BYTES = 38 * 1024 * 1024
OWN_VMEM_BYTES = 16 * 1024 * 1024


def passed_along(value, axis, steps):
    count = lax.axis_size(axis)
    pairs = [(source, (source + steps) % count) for source in range(count)]
    return lax.ppermute(value, axis, pairs)


def block_offset(block):
    if block < NB:
        return block + 1
    return NB - 1 - block


def halves(value):
    high = value.astype(jnp.bfloat16)
    low = (value - high.astype(jnp.float32)).astype(jnp.bfloat16)
    return high, low


def thirds(value):
    high = value.astype(jnp.bfloat16)
    rest = value - high.astype(jnp.float32)
    middle, low = halves(rest)
    return high, middle, low


def dot(left, right):
    return jnp.dot(left, right, preferred_element_type=jnp.float32)


def dot_one_hot(value, one_hot):
    return sum(dot(part, one_hot) for part in thirds(value))


def on_diagonal(shape):
    return lax.broadcasted_iota(jnp.int32, shape, 0) == lax.broadcasted_iota(jnp.int32, shape, 1)


def three_passes(left_high, left_low, right_high, right_low):
    return dot(
        jnp.concatenate([left_high, left_high, left_low], axis=1),
        jnp.concatenate([right_high, right_low, right_high], axis=0),
    )


def square_passes(left_high, left_low, right_high, right_low):
    cross = dot(left_high, right_low)
    return dot(left_high, right_high) + (cross + cross.T)


def step_factors(branches, number):
    taken = (branches[number] == 1).astype(jnp.float32)
    return 2.0 * taken, 1.0 - 2.0 * taken


def panels(start, end):
    cuts = [start] + [at for at in range(0, end, PANEL) if at > start] + [end]
    return [slice(low, high) for low, high in zip(cuts, cuts[1:])]


def spread_lanes(column, width):
    return jnp.concatenate([column] * (width // SUB), axis=1)


def combined(old, off, keep, add, state, rows_at, cols_at, on_diag):
    diag_row, diag_col = state[2:]
    factor_col = spread_lanes(keep + add * diag_col[rows_at, :], old.shape[1])
    value = old * (factor_col + add * diag_row[0:1, cols_at]) + add * off
    if on_diag:
        value = value - jnp.where(on_diagonal(value.shape), add * (old * old), 0.0)
    return value


def store_matrix(value, state, rows_at, cols_at):
    high_ref, low_ref, diag_row, diag_col = state
    if rows_at.start == cols_at.start:
        size = value.shape[0]
        line = jnp.where(on_diagonal(value.shape), value, 0.0)
        diag_row[:, cols_at] = jnp.broadcast_to(jnp.sum(line, axis=0, keepdims=True), (8, size))
        diag_col[rows_at, :] = jnp.broadcast_to(jnp.sum(line, axis=1, keepdims=True), (size, SUB))
        value = value - line
    high, low = halves(value)
    high_ref[rows_at, cols_at] = high
    low_ref[rows_at, cols_at] = low
    if rows_at.start != cols_at.start:
        high_ref[cols_at, rows_at] = high.T
        low_ref[cols_at, rows_at] = low.T


def start_block(source, row, col, top, scale):
    value = 0.5 * (source[row, col] + source[col, row].T)
    if row.start == col.start:
        value = value - jnp.where(on_diagonal(value.shape), top, 0.0)
    return -scale * value


def cut(size):
    return [slice(at, at + SUB) for at in range(0, size, SUB)]


def shifted(piece, by):
    return slice(piece.start + by, piece.stop + by)


def asked_atoms(request, orbitals):
    atoms = request.shape[1]
    expand = lax.broadcasted_iota(jnp.int32, (orbitals, atoms), 0) // ORB == lax.broadcasted_iota(
        jnp.int32, (orbitals, atoms), 1
    )
    expand = expand.astype(jnp.float32).astype(jnp.bfloat16)
    values = jnp.broadcast_to(request[...].astype(jnp.float32), (8, atoms)).astype(jnp.bfloat16)
    transposed = (((1,), (1,)), ((), ()))
    row = lax.dot_general(values, expand, transposed, preferred_element_type=jnp.float32)
    col = lax.dot_general(expand, values, transposed, preferred_element_type=jnp.float32)
    return row[0:1, :], col[:, 0:1]


def own_kernel(
    high_end, low_end, branches, core, request, high_cross, low_cross, x_cross, y_cross, y_halo,
    x_own, next_high, next_low, next_col, next_row, high, low, diag_row, diag_col
):
    rows, order = core.shape
    state = (high, low, diag_row, diag_col)
    later = (next_high, next_low, next_row, next_col)
    left, right = slice(0, rows), slice(rows, order)
    top = high_end[0]
    scale = 1.0 / (high_end[0] - low_end[0])
    keep, add = step_factors(branches, 0)
    asked_row, _ = asked_atoms(request, order - rows)
    live_row = (asked_row >= 0).astype(jnp.float32)
    for row in cut(rows):
        for col in cut(order - rows):
            value = -scale * (core[row, shifted(col, rows)] * live_row[:, col])
            x_cross[row, col] = value
            store_matrix(value, state, row, shifted(col, rows))
    for row in cut(rows):
        for col in cut(rows):
            if row.start <= col.start:
                value = start_block(core, row, col, top, scale)
                x_own[row, col] = value
                if row.start < col.start and row.start // PANEL == col.start // PANEL:
                    x_own[col, row] = value.T
                store_matrix(value, state, row, col)
    high_cross[...] = high[left, right]
    low_cross[...] = low[left, right]
    for row in panels(0, rows):
        for col in panels(rows, order):
            at = shifted(col, -rows)
            off = three_passes(high[row, left], low[row, left], high[left, col], low[left, col])
            factor = spread_lanes(keep + add * diag_col[row, :], at.stop - at.start)
            y_cross[row, at] = x_cross[row, at] * factor + add * off
    for row in panels(rows, order):
        for col in panels(rows, order):
            if row.start <= col.start:
                passes = square_passes if row.start == col.start else three_passes
                off = passes(high[row, left], low[row, left], high[left, col], low[left, col])
                y_halo[shifted(row, -rows), shifted(col, -rows)] = add * off
    for row in panels(0, rows):
        for col in panels(0, rows):
            if row.start <= col.start:
                passes = square_passes if row.start == col.start else three_passes
                off = passes(high[row, :], low[row, :], high[:, col], low[:, col])
                value = combined(
                    x_own[row, col], off, keep, add, state, row, col, row.start == col.start
                )
                x_own[row, col] = value
                store_matrix(value, later, row, col)


def kernel(place, high_end, low_end, branches, request, deriv, *refs):
    block_count = 2 * NB
    (high_cross, low_cross, x_cross, y_cross, y_halo, x_own, high_own, low_own, own_col, own_row) = refs[:10]
    pieces = refs[10 : 10 + block_count]
    density_out, own_out, mail = refs[10 + block_count : 13 + block_count]
    (x, high_a, low_a, high_b, low_b, diag_row_a, diag_row_b, diag_col_a, diag_col_b) = refs[
        13 + block_count : 22 + block_count
    ]
    halo, deriv_held, row_part, deriv_sems, out_sem = refs[22 + block_count :]
    order = x.shape[0]
    rows = x_own.shape[0]
    atoms = rows // ORB
    slot_rows = (order - rows) // block_count
    left, right = slice(0, rows), slice(rows, order)

    deriv_copies = [
        pltpu.make_async_copy(deriv.at[c], deriv_held.at[c], deriv_sems.at[c]) for c in range(3)
    ]
    for copy in deriv_copies:
        copy.start()
    state_a = (high_a, low_a, diag_row_a, diag_col_a)
    state_b = (high_b, low_b, diag_row_b, diag_col_b)

    top = high_end[0]
    scale = 1.0 / (high_end[0] - low_end[0])
    for block in range(block_count):
        halo[block * slot_rows : (block + 1) * slot_rows, :] = pieces[block][...]
    asked_row, asked_col = asked_atoms(request, order - rows)
    live_row = (asked_row >= 0).astype(jnp.float32)
    live_col = (asked_col >= 0).astype(jnp.float32)
    for row in cut(order - rows):
        for col in cut(order - rows):
            if row.start <= col.start:
                value = start_block(halo, row, col, top, scale)
                value = value * live_col[row, :] * live_row[:, col]
                down, across = shifted(row, rows), shifted(col, rows)
                x[down, across] = value
                if row.start < col.start and down.start // PANEL == across.start // PANEL:
                    x[across, down] = value.T
                store_matrix(value, state_b, row, col)
    x[left, left] = x_own[...]
    high_a[left, left] = high_own[...]
    low_a[left, left] = low_own[...]
    diag_col_a[left, :] = own_col[...]
    diag_row_a[:, left] = own_row[...]
    keep, add = step_factors(branches, 0)
    for row in panels(0, rows):
        for col in panels(rows, order):
            at = shifted(col, -rows)
            off = three_passes(high_cross[row, :], low_cross[row, :], high_b[left, at], low_b[left, at])
            value = y_cross[row, at] + x_cross[row, at] * (add * diag_row_b[0:1, at]) + add * off
            x[row, col] = value
            if row.start // PANEL == col.start // PANEL:
                x[col, row] = value.T
            store_matrix(value, state_a, row, col)
    for row in panels(rows, order):
        for col in panels(rows, order):
            if row.start <= col.start:
                down, across = shifted(row, -rows), shifted(col, -rows)
                passes = square_passes if row.start == col.start else three_passes
                off = passes(high_b[down, left], low_b[down, left], high_b[left, across], low_b[left, across])
                on_diag = row.start == col.start
                value = combined(x[row, col], off, keep, add, state_b, down, across, on_diag)
                value = value + y_halo[down, across]
                x[row, col] = value
                store_matrix(value, state_a, row, col)

    def block_step(number, now, later, lines, cols):
        keep, add = step_factors(branches, number)
        high, low = now[:2]
        on_diag = lines.start == cols.start
        passes = square_passes if on_diag else three_passes
        off = passes(high[lines, :], low[lines, :], high[:, cols], low[:, cols])
        value = combined(x[lines, cols], off, keep, add, now, lines, cols, on_diag)
        x[lines, cols] = value
        store_matrix(value, later, lines, cols)

    def squaring(number, now, later, unless_last):
        away = []
        for cols in panels(0, order):
            for lines in panels(0, cols.stop):
                if lines.start >= rows:
                    away.append((lines, cols))
                else:
                    block_step(number, now, later, lines, cols)

        def others():
            for lines, cols in away:
                block_step(number, now, later, lines, cols)

        if unless_last:
            pl.when(number < ITERS - 1)(others)
        else:
            others()

    def two(pair, carry):
        squaring(2 * pair + 1, state_a, state_b, False)
        squaring(2 * pair + 2, state_b, state_a, True)
        return carry

    lax.fori_loop(0, (ITERS - 1) // 2, two, 0)
    for cols in panels(0, rows):
        for lines in panels(0, cols.start) if cols.start > 0 else []:
            x[cols, lines] = x[lines, cols].T

    out_copy = pltpu.make_async_copy(x.at[left, :], density_out, out_sem)
    out_copy.start()

    chunk = 64
    line = lax.broadcasted_iota(jnp.int32, (8, order), 0)
    columns = jnp.zeros((8, order), jnp.float32)
    own_rows = jnp.zeros((8, rows), jnp.float32)
    ones = jnp.ones((8, SUB), jnp.bfloat16)
    for c in range(3):
        deriv_copies[c].wait()

        def strip(number, total, c=c):
            at = pl.ds(pl.multiple_of(number * chunk, chunk), chunk)
            some = pl.ds(pl.multiple_of(number * (chunk // ORB), chunk // ORB), chunk // ORB)
            weighted = x[at, :] * deriv_held[c, some].reshape(chunk, order)
            row_part[at, :] = sum(weighted[:, lane : lane + SUB] for lane in range(0, order, SUB))
            return total + jnp.sum(weighted.reshape(chunk // 8, 8, order), axis=0)

        total = lax.fori_loop(0, rows // chunk, strip, jnp.zeros((8, order), jnp.float32))
        columns = jnp.where(line == c, jnp.sum(total, axis=0, keepdims=True), columns)
        row_sums = sum(
            lax.dot_general(ones, part, (((1,), (1,)), ((), ())), preferred_element_type=jnp.float32)
            for part in thirds(row_part[...])
        )
        own_rows = jnp.where(line[:, :rows] == c, row_sums, own_rows)
    atom_ids = lax.broadcasted_iota(jnp.int32, (rows, atoms), 1)
    own_hot = (lax.broadcasted_iota(jnp.int32, (rows, atoms), 0) // ORB == atom_ids).astype(jnp.float32)
    own_out[...] = dot_one_hot(2.0 * (own_rows - columns[:, :rows]), own_hot.astype(jnp.bfloat16))
    letter = jnp.where(line[:, rows:] == 3, asked_row, -2.0 * columns[:, rows:])
    empty = jnp.where(lax.broadcasted_iota(jnp.int32, (4, SUB - slot_rows), 0) == 3, -1.0, 0.0)
    mail[...] = jnp.zeros(mail.shape, jnp.float32)
    for block in range(block_count):
        content = letter[0:4, block * slot_rows : (block + 1) * slot_rows]
        to = lax.rem(place[0] + (block_offset(block) + mail.shape[0]), mail.shape[0])
        mail[to] = jnp.concatenate([content, empty], axis=1)
    out_copy.wait()


def collect(place, mail, own, forces):
    count = mail.shape[0]
    atoms = own.shape[1]
    letters = jnp.concatenate(
        [mail[lax.rem(place[0] + (count - block_offset(block)), count)] for block in range(2 * NB)],
        axis=1,
    )
    wanted = letters[3:4, :] == lax.broadcasted_iota(jnp.int32, (atoms, 1), 0).astype(jnp.float32)
    wanted = wanted.astype(jnp.float32).astype(jnp.bfloat16)
    sums = sum(
        lax.dot_general(part, wanted, (((1,), (1,)), ((), ())), preferred_element_type=jnp.float32)
        for part in thirds(jnp.concatenate([letters, letters], axis=0))
    )
    forces[...] = own[0:3, :] + sums[0:3, :]


def own_part(high_end, low_end, branches, core, request):
    rows, order = core.shape
    halo = order - rows
    vmem = pl.BlockSpec(memory_space=pltpu.VMEM)
    smem = pl.BlockSpec(memory_space=pltpu.SMEM)
    kinds = [
        ((rows, halo), jnp.bfloat16),
        ((rows, halo), jnp.bfloat16),
        ((rows, halo), jnp.float32),
        ((rows, halo), jnp.float32),
        ((halo, halo), jnp.float32),
        ((rows, rows), jnp.float32),
        ((rows, rows), jnp.bfloat16),
        ((rows, rows), jnp.bfloat16),
        ((rows, SUB), jnp.float32),
        ((8, rows), jnp.float32),
    ]
    return pl.pallas_call(
        own_kernel,
        out_shape=[jax.ShapeDtypeStruct(*kind) for kind in kinds],
        in_specs=[smem, smem, smem, vmem, vmem],
        out_specs=[vmem] * len(kinds),
        scratch_shapes=[
            pltpu.VMEM((order, order), jnp.bfloat16),
            pltpu.VMEM((order, order), jnp.bfloat16),
            pltpu.VMEM((8, order), jnp.float32),
            pltpu.VMEM((order, SUB), jnp.float32),
        ],
        compiler_params=pltpu.CompilerParams(vmem_limit_bytes=OWN_VMEM_BYTES),
        cost_estimate=pl.CostEstimate(
            flops=2 * 3 * order**3 // 3, bytes_accessed=13_000_000, transcendentals=0
        ),
    )(high_end, low_end, branches, core, request)


def density_and_terms(place, high_end, low_end, branches, request, deriv, ready, pieces):
    rows, order = deriv.shape[1] * ORB, deriv.shape[3]
    atoms = rows // ORB
    vmem = pl.BlockSpec(memory_space=pltpu.VMEM)
    smem = pl.BlockSpec(memory_space=pltpu.SMEM)
    anywhere = pl.BlockSpec(memory_space=pl.ANY)
    square = (order, order)
    return pl.pallas_call(
        kernel,
        out_shape=[
            jax.ShapeDtypeStruct((rows, order), jnp.float32),
            jax.ShapeDtypeStruct((8, atoms), jnp.float32),
            jax.ShapeDtypeStruct((lax.axis_size("dom"), 4, SUB), jnp.float32),
        ],
        in_specs=[smem, smem, smem, smem, vmem, anywhere] + [vmem] * (len(ready) + len(pieces)),
        out_specs=[anywhere, vmem, vmem],
        scratch_shapes=[
            pltpu.VMEM(square, jnp.float32),
            pltpu.VMEM(square, jnp.bfloat16),
            pltpu.VMEM(square, jnp.bfloat16),
            pltpu.VMEM(square, jnp.bfloat16),
            pltpu.VMEM(square, jnp.bfloat16),
            pltpu.VMEM((8, order), jnp.float32),
            pltpu.VMEM((8, order), jnp.float32),
            pltpu.VMEM((order, SUB), jnp.float32),
            pltpu.VMEM((order, SUB), jnp.float32),
            pltpu.VMEM((order - rows, order - rows), jnp.float32),
            pltpu.VMEM((3, atoms, ORB, order), jnp.float32),
            pltpu.VMEM((rows, SUB), jnp.float32),
            pltpu.SemaphoreType.DMA((3,)),
            pltpu.SemaphoreType.DMA,
        ],
        compiler_params=pltpu.CompilerParams(vmem_limit_bytes=VMEM_BYTES),
        cost_estimate=pl.CostEstimate(
            flops=2 * 3 * 3 * order**3, bytes_accessed=24_000_000, transcendentals=0
        ),
    )(place, high_end, low_end, branches, request, deriv, *ready, *pieces)


def per_device(ham_core, halo_rows, halo_request, deriv, e_low, e_high, branches):
    row_count, order_all = ham_core.shape
    block_count = 2 * NB
    halo = halo_rows[0, :, :, row_count:]
    early = (6, 3, 2, 1, 5)
    late = (0, 4, 7)
    pieces = {block: passed_along(halo[block], "dom", -block_offset(block)) for block in early}
    waiting, pieces[early[0]] = lax.optimization_barrier(
        ([halo[block] for block in late], pieces[early[0]])
    )
    for block, piece in zip(late, waiting):
        pieces[block] = passed_along(piece, "dom", -block_offset(block))
    request, pieces[early[2]] = lax.optimization_barrier((halo_request, pieces[early[2]]))
    ready = own_part(e_high, e_low, branches, ham_core, request)
    place = lax.axis_index("dom")[None].astype(jnp.int32)
    density, own, mail = density_and_terms(
        place,
        e_high,
        e_low,
        branches,
        halo_request,
        deriv,
        ready,
        [pieces[block] for block in range(block_count)],
    )
    arrived = lax.all_to_all(mail, "dom", 0, 0, tiled=True)
    forces = pl.pallas_call(
        collect,
        out_shape=jax.ShapeDtypeStruct((3, own.shape[1]), jnp.float32),
        in_specs=[
            pl.BlockSpec(memory_space=pltpu.SMEM),
            pl.BlockSpec(memory_space=pltpu.VMEM),
            pl.BlockSpec(memory_space=pltpu.VMEM),
        ],
        out_specs=pl.BlockSpec(memory_space=pltpu.VMEM),
    )(place, arrived, own)
    return (density, forces)


def solution(mesh):
    in_specs = (
        P("dom", None),
        P("dom", None, None, None),
        P("dom", None),
        P(None, "dom", None, None),
        P(),
        P(),
        P(),
    )
    out_specs = (P("dom", None), P(None, "dom"))
    return jax.shard_map(
        per_device, mesh=mesh, in_specs=in_specs, out_specs=out_specs, check_vma=False
    )
```
